256 devices in a mesh: mem: 16 (over x_hi, y, core), tile: 16 (over z, x_lo).
Axes of the slice: x: 4 (x_hi: 2, x_lo: 2; x = x_hi * 2 + x_lo), y: 4, z: 8, core: 2. Of those that a mesh axis runs over, the one named last changes fastest.
Arguments:
- perturb: bfloat16 [32, 6, 16, 256, 128], P('mem', None, None, 'tile'), may hold values from -2.5 to 2.5
- alpha: float32 [32, 16, 256, 128], P('mem', None, 'tile'), may hold values from -5 to 5
- alpha_mom: float32 [32, 16, 256, 128], P('mem', None, 'tile'), may hold values from -6 to 6
- static_ctl: float32 [6, 16, 256, 128], P(None, None, 'tile'), may hold values from -6 to 6
- static_mom: float32 [6, 16, 256, 128], P(None, 'mem', 'tile'), may hold values from -6 to 6
- loc_coef: float32 [2, 256, 128], P(None, 'tile'), may hold values from 0.04 to 0.36, as said below
- static_coef: float32 [2, 256, 128], P(None, 'tile'), may hold values from 0.04 to 0.36, as said below
- obs_cell: int32 [16, 1024], P('tile'), may hold values from 0 to 2047
- obs_mask: int32 [16, 1024], P('tile'), may hold values 0 or 1
- obs_value: float32 [6, 16, 16, 1024], P(None, None, 'tile'), may hold values from -6 to 6
- obs_weight: float32 [6, 16, 16, 1024], P(None, None, 'tile'), may hold values from 0.3 to 3
Outputs:
- new_alpha: float32 [32, 16, 256, 128], P('mem', None, 'tile')
- new_alpha_mom: float32 [32, 16, 256, 128], P('mem', None, 'tile')
- new_static: float32 [6, 16, 256, 128], P(None, 'mem', 'tile')
- new_static_mom: float32 [6, 16, 256, 128], P(None, 'mem', 'tile')
The draws below stay inside these ranges and needn't reach their ends.
Inputs may be any that keep to these rules, and one draw needn't show every extreme that they name: `obs_cell`: slots of a tile may name the same cell. `loc_coef`: index 0 lies in 0.18 to 0.36, index 1 in 0.04 to 0.08. `static_coef`: index 0 lies in 0.18 to 0.36, index 1 in 0.04 to 0.08.
All inputs are finite; a program needn't handle non-finite values. No bound on the sum of `obs_mask` on one device may be relied on, other than what follows from the above.
Results may differ from the reference program's by a relative error of at most 0.0003.
Values sent between devices are 32-bit elements; how exact they have to be, the bound alone decides.
No kernel may reach another device: no remote copies, remote signals or barrier semaphores. Data moves between devices by JAX's collectives and lax.ppermute only.
A program may use at most 64 MiB of HBM per device.

```python
import math
import jax
import jax.numpy as jnp
from jax import lax

VARIABLES = 6
LEVELS = 16
TILE_ROWS = 16
COLUMNS = 128
STATIONS = 1024
DIFF_STEPS = 12
MEMBERS = 32
TILE_COUNT = 16
GRID_ROWS = 256


log_two = 0.6931471805599453


def coefficient_field(key):
    uniform_part = jax.random.uniform(key, (2, GRID_ROWS, COLUMNS), jnp.float32)
    lowest = jnp.array([0.18, 0.04], jnp.float32)[:, None, None]
    return lowest * jnp.exp(uniform_part * log_two)


def draw_loc_coef(key, part):
    return coefficient_field(jax.random.fold_in(key, 11))


def draw_static_coef(key, part):
    return coefficient_field(jax.random.fold_in(key, 23))


def draw_alpha(key, part):
    layout = (MEMBERS, LEVELS, GRID_ROWS, COLUMNS)
    subkey = jax.random.fold_in(key, 37)
    return jnp.clip(0.8 + jax.random.normal(subkey, layout, jnp.float32), -5.0, 5.0)


def touch_ends(values, rng, low, high):
    place = [jax.random.randint(jax.random.fold_in(rng, axis), (), 0, length) for axis, length in enumerate(values.shape)]
    widest = values.shape.index(max(values.shape))
    beside = place[:widest] + [(place[widest] + 1) % values.shape[widest]] + place[widest + 1:]
    return values.at[tuple(place)].set(low).at[tuple(beside)].set(high)


def block_levels(own_key, dims, shards, least, top_value):
    def one(dim, parts):
        heights = jax.random.uniform(jax.random.fold_in(jax.random.fold_in(own_key, 6), dim), (parts,), jnp.float32, least / len(shards), top_value / len(shards))
        return jnp.repeat(jnp.exp(heights), dims[dim] // parts).reshape((-1,) + (1,) * (len(dims) - dim - 1))

    loudness = one(*shards[0])
    for cut in shards[1:]:
        loudness = loudness * one(*cut)
    return loudness


def normal_values(rng, extent, deviation, limit, split=(), kind=jnp.bfloat16):
    result = jax.random.normal(rng, extent, jnp.float32) * deviation
    if len(split) > 0:
        result = block_levels(rng, extent, split, -0.22, 0.18) * result
    return jnp.clip(result, min=-limit, max=limit).astype(kind)


def setup_inputs(seed: int = 0) -> dict:
    seeds = jax.random.split(jax.random.key(seed), 12)
    return {
        "perturb": normal_values(seeds[0], (MEMBERS, VARIABLES, LEVELS, GRID_ROWS, COLUMNS), 0.18, 2.5, ((0, 16), (3, 16))),
        "alpha": draw_alpha(jax.random.fold_in(seeds[11], 71), 0),
        "alpha_mom": normal_values(seeds[2], (MEMBERS, LEVELS, GRID_ROWS, COLUMNS), 0.5, 6.0, ((0, 16), (2, 16)), jnp.float32),
        "static_ctl": normal_values(seeds[3], (VARIABLES, LEVELS, GRID_ROWS, COLUMNS), 1.0, 6.0, ((2, 16),), jnp.float32),
        "static_mom": normal_values(seeds[4], (VARIABLES, LEVELS, GRID_ROWS, COLUMNS), 0.5, 6.0, ((1, 16), (2, 16)), jnp.float32),
        "loc_coef": draw_loc_coef(jax.random.fold_in(seeds[11], 71), 0),
        "static_coef": draw_static_coef(jax.random.fold_in(seeds[11], 71), 0),
        "obs_cell": touch_ends(jax.random.randint(seeds[7], (TILE_COUNT, STATIONS), 0, TILE_ROWS * COLUMNS), jax.random.fold_in(seeds[7], 1), 0, (TILE_ROWS * COLUMNS) - 1).astype(jnp.int32),
        "obs_mask": touch_ends((jax.random.randint(seeds[8], (TILE_COUNT, STATIONS), 0, 4) < 3).astype(jnp.int32), jax.random.fold_in(seeds[8], 1), 0, 1),
        "obs_value": normal_values(seeds[9], (VARIABLES, LEVELS, TILE_COUNT, STATIONS), 1.0, 6.0, ((2, 16),), jnp.float32),
        "obs_weight": jnp.clip(jnp.exp(math.log(3.0) - 2.3025851 * jax.random.uniform(seeds[10], (VARIABLES, LEVELS, TILE_COUNT, STATIONS), jnp.float32) ** block_levels(seeds[10], (VARIABLES, LEVELS, TILE_COUNT, STATIONS), ((2, 16),), -0.2, 0.2)), 0.3, 3.0),
    }


momentum_rate = 0.9
step_rate = 0.5

def smooth(padded, factors):
    faces_x = factors[0]
    faces_y = factors[1]
    flux_x = faces_x[:-1] * (padded[..., 1:, :] - padded[..., :-1, :])
    middle = padded[..., 1:-1, :]
    shifted = jnp.concatenate([middle[..., 1:], jnp.zeros_like(middle[..., :1])], axis=-1)
    flux_y = faces_y[1:-1] * (shifted - middle)
    flux_left = jnp.concatenate([jnp.zeros_like(flux_y[..., :1]), flux_y[..., :-1]], axis=-1)
    return middle + (flux_x[..., 1:, :] - flux_x[..., :-1, :]) + (flux_y - flux_left)

def diffuse(quantity, factors):
    padded_factors = jnp.pad(factors, ((0, 0), (1, 1), (0, 0)))
    widths = [(0, 0)] * (quantity.ndim - 2) + [(1, 1), (0, 0)]

    def advance(turn, current):
        return smooth(jnp.pad(current, widths), padded_factors)
    return lax.fori_loop(0, DIFF_STEPS, advance, quantity)

def reference(perturb, alpha, alpha_mom, static_ctl, static_mom, loc_coef, static_coef, obs_cell, obs_mask, obs_value, obs_weight):

    def add_member(running, pair):
        weights, member = pair
        localized = diffuse(weights, loc_coef)
        return (running + localized[None] * member.astype(jnp.float32), jnp.float32(0.0))
    ensemble, _ = lax.scan(add_member, jnp.zeros(static_ctl.shape, jnp.float32), (alpha, perturb))
    increment = ensemble + diffuse(static_ctl, static_coef)
    tile_total = obs_cell.shape[0]
    flat_index = (jnp.arange(tile_total, dtype=jnp.int32)[:, None] * (TILE_ROWS * COLUMNS) + obs_cell).reshape(-1).astype(jnp.int32)
    flattened = increment.reshape(VARIABLES, LEVELS, GRID_ROWS * COLUMNS)
    picked = jnp.take(flattened, flat_index, axis=2).reshape(VARIABLES, LEVELS, tile_total, STATIONS)
    misfit = obs_mask.astype(jnp.float32)[None, None] * obs_weight * (picked - obs_value)
    gradient = jnp.zeros_like(flattened).at[:, :, flat_index].add(misfit.reshape(VARIABLES, LEVELS, -1)).reshape(increment.shape)
    static_grad = static_ctl + diffuse(gradient, static_coef)

    def member_grad(carry, pair):
        weights, member = pair
        projected = lax.optimization_barrier(jnp.sum(member.astype(jnp.float32) * gradient, axis=0))
        return (carry, weights + diffuse(projected, loc_coef))
    _, alpha_grad = lax.scan(member_grad, jnp.float32(0.0), (alpha, perturb))
    new_alpha_mom = momentum_rate * alpha_mom + alpha_grad
    new_alpha = alpha - step_rate * new_alpha_mom
    new_static_mom = momentum_rate * static_mom + static_grad
    new_static = static_ctl - step_rate * new_static_mom
    return (new_alpha, new_alpha_mom, new_static, new_static_mom)
```

```python
import functools

import jax
import jax.numpy as jnp
from jax import lax
from jax.experimental import pallas as pl
from jax.experimental.pallas import tpu as pltpu
from jax.sharding import PartitionSpec as P

STEPS = 12
ROWS = 16
LANES = 128
SPAN = ROWS + 2 * STEPS
VARS = 6
HALF = 8

momentum_rate = 0.9
step_rate = 0.5

VM = pl.BlockSpec(memory_space=pltpu.VMEM)
ANY = pl.BlockSpec(memory_space=pl.ANY)


def shape(*dims):
    return jax.ShapeDtypeStruct(dims, jnp.float32)


def call(body, name, ins, outs, scratch=(), flops=1000000):
    return pl.pallas_call(
        body,
        name=name,
        in_specs=list(ins),
        out_specs=[VM] * len(outs),
        out_shape=list(outs),
        scratch_shapes=list(scratch),
        compiler_params=pltpu.CompilerParams(vmem_limit_bytes=32 * 1024 * 1024),
        cost_estimate=pl.CostEstimate(flops=flops, bytes_accessed=1000000, transcendentals=0),
    )


def f32(*dims):
    return pltpu.VMEM(dims, jnp.float32)


def place():
    mem = lax.axis_index("mem")
    return mem // 8, (mem // 2) % 4, mem % 2


def pack_rows(load, width, forward, backward):
    for row in range(ROWS):
        value = load(row)
        if row >= ROWS - STEPS:
            at = (row - (ROWS - STEPS)) * width
            forward[at : at + width, :] = value
        if row < STEPS:
            backward[row * width : (row + 1) * width, :] = value


def build_coefs(low_x, mid_x, high_x, low_y, mid_y, high_y, raw, coefs):
    raw[0:8, :] = jnp.zeros((8, LANES), jnp.float32)
    raw[8:20, :] = low_x
    raw[20:36, :] = mid_x
    raw[36:48, :] = high_x
    raw[48:60, :] = low_y
    raw[60:76, :] = mid_y
    raw[76:88, :] = high_y
    extent = ROWS * lax.axis_size("tile")
    first = lax.axis_index("tile") * ROWS - STEPS
    at = first + lax.broadcasted_iota(jnp.int32, (SPAN, LANES), 0)
    lane = lax.broadcasted_iota(jnp.int32, (SPAN, LANES), 1)
    valid = (at >= 0) & (at < extent)
    below = jnp.where(valid, raw[8:48, :], 0.0)
    raw[8:48, :] = below
    above = jnp.where(valid, raw[7:47, :], 0.0)
    right = jnp.where(valid, raw[48:88, :], 0.0)
    left = jnp.where(lane > 0, pltpu.roll(right, 1, 1), 0.0)
    centre = 1.0 - below - above - right - left
    coefs[0:40, :] = jnp.where(valid, centre, 0.0)
    coefs[40:80, :] = jnp.where(at + 1 < extent, below, 0.0)
    coefs[80:120, :] = above
    coefs[120:160, :] = jnp.where(lane < LANES - 1, right, 0.0)
    coefs[160:200, :] = left


def diffuse(load, width, pitch, coefs, bufs, emit):
    for turn in range(STEPS):
        source = bufs[turn % 2]
        target = bufs[(turn + 1) % 2]
        if turn == 0:
            take = load
        else:
            take = lambda row: source[row * pitch : row * pitch + width, :]
        before = take(turn)
        here = take(turn + 1)
        for row in range(turn + 1, SPAN - 1 - turn):
            after = take(row + 1)
            new = coefs[row : row + 1, :] * here
            new = new + coefs[40 + row : 41 + row, :] * after
            new = new + coefs[80 + row : 81 + row, :] * before
            new = new + coefs[120 + row : 121 + row, :] * pltpu.roll(here, LANES - 1, 1)
            new = new + coefs[160 + row : 161 + row, :] * pltpu.roll(here, 1, 1)
            if turn == STEPS - 1:
                emit(row - STEPS, new)
            else:
                target[row * pitch : row * pitch + width, :] = new
            before = here
            here = after


def alpha_row(alpha, parity, row):
    parts = [alpha[pl.ds(m * 256 + parity * ROWS + row, HALF, stride=2 * ROWS), :] for m in range(2)]
    return jnp.concatenate(parts, axis=0)


def pack_body(alpha, loc, static_ctl, static_coef, a_f, a_b, b_f, b_b, c_f, c_b, field, sem):
    mem = lax.axis_index("mem")
    own = mem % 2
    fetch = pltpu.make_async_copy(static_ctl.at[:, mem], field.reshape(8, ROWS, LANES).at[0:VARS], sem)
    fetch.start()
    pack_rows(lambda row: alpha_row(alpha, 1 - own, row), 16, a_f, a_b)
    for k in range(2):
        a_f[192 + k * 12 : 204 + k * 12, :] = loc[k * 16 + 4 : k * 16 + 16, :]
        a_b[192 + k * 12 : 204 + k * 12, :] = loc[k * 16 : k * 16 + 12, :]
    pack_rows(lambda row: alpha_row(alpha, own, row), 16, b_f, b_b)
    fetch.wait()
    field[VARS * ROWS :, :] = static_coef[...]
    pack_rows(lambda row: field[pl.ds(row, 8, stride=ROWS), :], 8, c_f, c_b)


def halo_loader(low, high, middle, width):
    def load(row):
        if row < STEPS:
            return low[row * width : (row + 1) * width, :]
        if row < STEPS + ROWS:
            return middle(row - STEPS)
        at = (row - STEPS - ROWS) * width
        return high[at : at + width, :]

    return load


def first_body(alpha, low, high, loc, perturb, sums, coefs, raw, buf0, buf1, local):
    parity = 1 - lax.axis_index("mem") % 2
    build_coefs(
        low[192:204, :], loc[0:16, :], high[192:204, :],
        low[204:216, :], loc[16:32, :], high[204:216, :], raw, coefs,
    )

    def emit(row, value):
        local[pl.ds(row, 16, stride=ROWS), :] = value

    load = halo_loader(low, high, lambda row: alpha_row(alpha, parity, row), 16)
    diffuse(load, 16, 16, coefs, (buf0, buf1), emit)
    for s in range(HALF):
        level = 2 * s + parity
        for v in range(VARS):
            total = local[s * 16 : s * 16 + 16, :] * perturb[0, v, level].astype(jnp.float32)
            total = total + local[128 + s * 16 : 144 + s * 16, :] * perturb[1, v, level].astype(jnp.float32)
            sums[s, v] = total


def second_body(alpha, low, high, coefs, perturb, received, o0, o1, o2, o3, buf0, buf1, local):
    _, y, parity = place()

    def emit(row, value):
        local[pl.ds(row, 16, stride=ROWS), :] = value

    load = halo_loader(low, high, lambda row: alpha_row(alpha, parity, row), 16)
    diffuse(load, 16, 16, coefs, (buf0, buf1), emit)
    for k, out in enumerate((o0, o1, o2, o3)):
        for j in range(2):
            s = (y ^ k) + 4 * j
            level = 2 * s + parity
            first = local[pl.ds(pl.multiple_of(s * 16, 16), 16), :]
            other = local[pl.ds(pl.multiple_of(128 + s * 16, 16), 16), :]
            for v in range(VARS):
                total = first * perturb[0, v, level].astype(jnp.float32)
                total = total + other * perturb[1, v, level].astype(jnp.float32)
                out[j, v] = total + received[s, v]


def static_first_body(low, high, field, o0, out, coefs, raw, buf0, buf1, result):
    x, _, _ = place()
    build_coefs(
        low[pl.ds(6, 12, stride=8), :], field[96:112, :], high[pl.ds(6, 12, stride=8), :],
        low[pl.ds(7, 12, stride=8), :], field[112:128, :], high[pl.ds(7, 12, stride=8), :], raw, coefs,
    )

    def emit(row, value):
        result[pl.ds(row, 8, stride=ROWS), :] = value

    load = halo_loader(low, high, lambda row: field[pl.ds(row, 8, stride=ROWS), :], 8)
    diffuse(load, 8, 8, coefs, (buf0, buf1), emit)
    for j in range(2):
        for v in range(VARS):
            part = result[v * 16 : v * 16 + 16, :]
            out[j, v] = o0[j, v] + jnp.where(x == j, part, 0.0)


def prepare_body(cell, mask, value, weight, sums, held, sem):
    _, y, c = place()
    copies = []
    for j in range(2):
        level = 2 * y + c + 8 * j
        for k, source in enumerate((weight, value)):
            spot = held.reshape(2, 2, VARS, 8, LANES).at[k, j]
            copies.append(pltpu.make_async_copy(source.at[:, level], spot, sem.at[2 * j + k]))
    for copy in copies:
        copy.start()
    for copy in copies:
        copy.wait()
    pieces = []
    for a in range(8):
        part = held[pl.ds(a, 24, stride=8), :]
        scaled = part[0:12, :] * mask[a : a + 1, :].astype(jnp.float32)
        pieces.append(jnp.concatenate([scaled, scaled * part[12:24, :]], axis=0))
    both = jnp.concatenate(pieces, axis=1)
    top = both.astype(jnp.bfloat16)
    rest = both - top.astype(jnp.float32)
    mid = rest.astype(jnp.bfloat16)
    low = (rest - mid.astype(jnp.float32)).astype(jnp.bfloat16)
    stacked = jnp.concatenate([top, mid, low], axis=0)
    cells = jnp.concatenate([cell[a : a + 1, :] for a in range(8)], axis=1)
    for block in range(8):
        ids = block * 256 + lax.broadcasted_iota(jnp.int32, (256, 1024), 0)
        hit = jnp.where(ids == cells, 1.0, 0.0).astype(jnp.bfloat16)
        got = lax.dot_general(stacked, hit, (((1,), (1,)), ((), ())), preferred_element_type=jnp.float32)
        total = got[0:24, :] + got[24:48, :] + got[48:72, :]
        for r in range(2):
            sums[pl.ds(block * 2 + r, 24, stride=ROWS), :] = total[:, r * LANES : (r + 1) * LANES]


def gradient_body(mine, other, sums, grad, forward, backward):
    x, _, _ = place()
    total = mine[...] + other[...]
    grad[...] = sums[0:192, :] * total - sums[192:384, :]
    pack_rows(lambda row: grad[pl.ds(x * 96 + row, VARS, stride=ROWS), :], VARS, forward, backward)


def project_body(own, g0, g1, g2, g3, perturb, forward, backward, middle):
    _, y, c = place()
    parity = c if own else 1 - c
    for k, g in enumerate((g0, g1, g2, g3)):
        for j in range(2):
            s = (y ^ k) + 4 * j
            level = 2 * s + parity
            for m in range(2):
                total = perturb[m, 0, level].astype(jnp.float32) * g[j, 0]
                for v in range(1, VARS):
                    total = total + perturb[m, v, level].astype(jnp.float32) * g[j, v]
                middle[pl.ds(pl.multiple_of((m * HALF + s) * 16, 16), 16), :] = total
    pack_rows(lambda row: middle[pl.ds(row, 16, stride=ROWS), :], 16, forward, backward)


def third_body(low, high, middle, coefs, out, buf0, buf1):
    def emit(row, value):
        out[pl.ds(row, 16, stride=ROWS), :] = value

    load = halo_loader(low, high, lambda row: middle[pl.ds(row, 16, stride=ROWS), :], 16)
    diffuse(load, 16, 16, coefs, (buf0, buf1), emit)


def fourth_body(low, high, middle, coefs, done, alpha, mom, new_alpha, new_mom, buf0, buf1, out):
    third_body(low, high, middle, coefs, out, buf0, buf1)
    c = lax.axis_index("mem") % 2
    for source, parity in ((done, c), (out, 1 - c)):
        for m in range(2):
            for s in range(HALF):
                at = pl.ds(pl.multiple_of(m * 256 + (2 * s + parity) * 16, 16), 16)
                old = alpha[at, :]
                grad = old + source[(m * HALF + s) * 16 : (m * HALF + s) * 16 + 16, :]
                moved = momentum_rate * mom[at, :] + grad
                new_mom[at, :] = moved
                new_alpha[at, :] = old - step_rate * moved


def static_last_body(low, high, grad, coefs, field, mom, new_static, new_mom, buf0, buf1, result):
    x, _, _ = place()

    def emit(row, value):
        result[pl.ds(row, VARS, stride=ROWS), :] = value

    load = halo_loader(low, high, lambda row: grad[pl.ds(x * 96 + row, VARS, stride=ROWS), :], VARS)
    diffuse(load, VARS, 8, coefs, (buf0, buf1), emit)
    old = field[0:96, :]
    moved = momentum_rate * mom[...] + (old + result[...])
    new_mom[...] = moved
    new_static[...] = old - step_rate * moved


def local(
    perturb,
    alpha,
    alpha_mom,
    static_ctl,
    static_mom,
    loc_coef,
    static_coef,
    obs_cell,
    obs_mask,
    obs_value,
    obs_weight,
):
    tiles = lax.axis_size("tile")
    up = [(i, (i + 1) % tiles) for i in range(tiles)]
    down = [(target, source) for source, target in up]
    members = lax.axis_size("mem")

    def swap(value, bits):
        return lax.ppermute(value, "mem", [(i, i ^ bits) for i in range(members)])

    def halo(forward, backward):
        return lax.ppermute(forward, "tile", up), lax.ppermute(backward, "tile", down)

    alpha2 = alpha.reshape(512, LANES)
    mom2 = alpha_mom.reshape(512, LANES)
    loc2 = loc_coef.reshape(32, LANES)
    bufs16 = [f32(SPAN * 16, LANES), f32(SPAN * 16, LANES)]
    bufs8 = [f32(SPAN * 8, LANES), f32(SPAN * 8, LANES)]
    raw = f32(88, LANES)

    a_f, a_b, b_f, b_b, c_f, c_b, field = call(
        pack_body,
        "pack",
        [VM, VM, ANY, VM],
        [shape(216, LANES)] * 2 + [shape(192, LANES)] * 2 + [shape(96, LANES)] * 2 + [shape(128, LANES)],
        [pltpu.SemaphoreType.DMA],
    )(alpha2, loc2, static_ctl, static_coef.reshape(32, LANES))
    a_low, a_high = halo(a_f, a_b)
    b_low, b_high = halo(b_f, b_b)

    (sums,) = call(
        prepare_body,
        "prepare",
        [VM, VM, ANY, ANY],
        [shape(384, LANES)],
        [f32(192, LANES), pltpu.SemaphoreType.DMA((4,))],
        flops=1000000000,
    )(
        obs_cell.reshape(8, LANES),
        obs_mask.reshape(8, LANES),
        obs_value.reshape(VARS, 16, 8, LANES),
        obs_weight.reshape(VARS, 16, 8, LANES),
    )

    quarter = shape(2, VARS, ROWS, LANES)
    part_a, loc_k = call(
        first_body,
        "first",
        [VM] * 5,
        [shape(HALF, VARS, ROWS, LANES), shape(200, LANES)],
        [raw] + bufs16 + [f32(256, LANES)],
    )(alpha2, a_low, a_high, loc2, perturb)
    got = swap(part_a, 1)
    o0, o1, o2, o3 = call(
        second_body,
        "second",
        [VM] * 6,
        [quarter] * 4,
        bufs16 + [f32(256, LANES)],
    )(alpha2, b_low, b_high, loc_k, perturb, got)
    r1, r2, r3 = swap(o1, 2), swap(o2, 4), swap(o3, 6)
    c_low, c_high = halo(*lax.optimization_barrier((c_f, c_b, o0))[:2])
    o0s, static_k = call(
        static_first_body,
        "static_first",
        [VM] * 4,
        [quarter, shape(200, LANES)],
        [raw] + bufs8 + [f32(128, LANES)],
    )(c_low, c_high, field, o0)
    mine = (o0s + r1 + r2 + r3).reshape(192, LANES)
    other = swap(mine, 8)
    grad, g_f, g_b = call(
        gradient_body,
        "gradient",
        [VM] * 3,
        [shape(192, LANES), shape(72, LANES), shape(72, LANES)],
    )(mine, other, sums)
    full = (2, VARS, ROWS, LANES)
    gs = [grad.reshape(full)]
    gs = gs + [swap(grad, 2 * k).reshape(full) for k in range(1, 4)]
    ps = [swap(g, 1) for g in gs]
    g_low, g_high = halo(g_f, g_b)
    packed = [shape(192, LANES), shape(192, LANES), shape(256, LANES)]
    p_f, p_b, p_m = call(functools.partial(project_body, True), "project_own", [VM] * 5, packed)(*gs, perturb)
    p_low, p_high = halo(p_f, p_b)
    q_f, q_b, q_m = call(functools.partial(project_body, False), "project_other", [VM] * 5, packed)(*ps, perturb)
    q_low, q_high = halo(q_f, q_b)
    new_static, new_static_mom = call(
        static_last_body,
        "static_last",
        [VM] * 6,
        [shape(96, LANES)] * 2,
        bufs8 + [f32(96, LANES)],
    )(g_low, g_high, grad, static_k, field, static_mom.reshape(96, LANES))
    (done,) = call(third_body, "third", [VM] * 4, [shape(256, LANES)], bufs16)(p_low, p_high, p_m, loc_k)
    new_alpha, new_alpha_mom = call(
        fourth_body,
        "fourth",
        [VM] * 7,
        [shape(512, LANES)] * 2,
        bufs16 + [f32(256, LANES)],
    )(q_low, q_high, q_m, loc_k, done, alpha2, mom2)
    return (
        new_alpha.reshape(alpha.shape),
        new_alpha_mom.reshape(alpha.shape),
        new_static.reshape(static_mom.shape),
        new_static_mom.reshape(static_mom.shape),
    )


def solution(mesh):
    return jax.shard_map(
        local,
        mesh=mesh,
        in_specs=(
            P("mem", None, None, "tile", None),
            P("mem", None, "tile", None),
            P("mem", None, "tile", None),
            P(None, None, "tile", None),
            P(None, "mem", "tile", None),
            P(None, "tile", None),
            P(None, "tile", None),
            P("tile", None),
            P("tile", None),
            P(None, None, "tile", None),
            P(None, None, "tile", None),
        ),
        out_specs=(
            P("mem", None, "tile", None),
            P("mem", None, "tile", None),
            P(None, "mem", "tile", None),
            P(None, "mem", "tile", None),
        ),
        check_vma=False,
    )
```

```python
import functools

import jax
import jax.numpy as jnp
from jax import lax
from jax.experimental import pallas as pl
from jax.experimental.pallas import tpu as pltpu
from jax.sharding import PartitionSpec as P

STEPS = 12
ROWS = 16
LANES = 128
SPAN = ROWS + 2 * STEPS
VARS = 6
HALF = 8

momentum_rate = 0.9
step_rate = 0.5

GRANT = 53.2
BUSY = 5000000000

VM = pl.BlockSpec(memory_space=pltpu.VMEM)
ANY = pl.BlockSpec(memory_space=pl.ANY)
HBM = pl.BlockSpec(memory_space=pltpu.HBM)


def shape(*dims):
    return jax.ShapeDtypeStruct(dims, jnp.float32)


def call(body, name, ins, outs, scratch=(), flops=1000000, out_specs=None, aliases=None, grant=32):
    return pl.pallas_call(
        body,
        name=name,
        in_specs=list(ins),
        out_specs=out_specs or [VM] * len(outs),
        out_shape=list(outs),
        scratch_shapes=list(scratch),
        input_output_aliases=aliases or {},
        compiler_params=pltpu.CompilerParams(vmem_limit_bytes=int(grant * 1024 * 1024)),
        cost_estimate=pl.CostEstimate(flops=flops, bytes_accessed=1000000, transcendentals=0),
    )


def f32(*dims):
    return pltpu.VMEM(dims, jnp.float32)


def place():
    mem = lax.axis_index("mem")
    return mem // 8, (mem // 2) % 4, mem % 2


def pack_rows(load, width, forward, backward, base=0):
    for row in range(ROWS):
        value = load(row)
        if row >= ROWS - STEPS:
            at = base + (row - (ROWS - STEPS)) * width
            forward[at : at + width, :] = value
        if row < STEPS:
            at = base + row * width
            backward[at : at + width, :] = value


def build_coefs(low_x, mid_x, high_x, low_y, mid_y, high_y, raw, coefs):
    raw[0:8, :] = jnp.zeros((8, LANES), jnp.float32)
    raw[8:20, :] = low_x
    raw[20:36, :] = mid_x
    raw[36:48, :] = high_x
    raw[48:60, :] = low_y
    raw[60:76, :] = mid_y
    raw[76:88, :] = high_y
    extent = ROWS * lax.axis_size("tile")
    first = lax.axis_index("tile") * ROWS - STEPS
    at = first + lax.broadcasted_iota(jnp.int32, (SPAN, LANES), 0)
    lane = lax.broadcasted_iota(jnp.int32, (SPAN, LANES), 1)
    valid = (at >= 0) & (at < extent)
    below = jnp.where(valid, raw[8:48, :], 0.0)
    raw[8:48, :] = below
    above = jnp.where(valid, raw[7:47, :], 0.0)
    right = jnp.where(valid, raw[48:88, :], 0.0)
    left = jnp.where(lane > 0, pltpu.roll(right, 1, 1), 0.0)
    centre = 1.0 - below - above - right - left
    coefs[0:40, :] = jnp.where(valid, centre, 0.0)
    coefs[40:80, :] = jnp.where(at + 1 < extent, below, 0.0)
    coefs[80:120, :] = above
    coefs[120:160, :] = jnp.where(lane < LANES - 1, right, 0.0)
    coefs[160:200, :] = left


def diffuse(load, width, pitch, coefs, bufs, emit):
    for turn in range(STEPS):
        source = bufs[turn % 2]
        target = bufs[(turn + 1) % 2]
        if turn == 0:
            take = load
        else:
            take = lambda row: source[row * pitch : row * pitch + width, :]
        before = take(turn)
        here = take(turn + 1)
        for row in range(turn + 1, SPAN - 1 - turn):
            after = take(row + 1)
            new = coefs[row : row + 1, :] * here
            new = new + coefs[40 + row : 41 + row, :] * after
            new = new + coefs[80 + row : 81 + row, :] * before
            new = new + coefs[120 + row : 121 + row, :] * pltpu.roll(here, LANES - 1, 1)
            new = new + coefs[160 + row : 161 + row, :] * pltpu.roll(here, 1, 1)
            if turn == STEPS - 1:
                emit(row - STEPS, new)
            else:
                target[row * pitch : row * pitch + width, :] = new
            before = here
            here = after


def alpha_row(alpha, parity, row):
    parts = [alpha[pl.ds(m * 256 + parity * ROWS + row, HALF, stride=2 * ROWS), :] for m in range(2)]
    return jnp.concatenate(parts, axis=0)


def pack_body(alpha_in, loc_in, static_ctl, static_coef, a_f, a_b, b_f, b_b, alpha, loc, field, sem):
    mem = lax.axis_index("mem")
    own = mem % 2
    copies = [
        pltpu.make_async_copy(alpha_in, alpha, sem.at[0]),
        pltpu.make_async_copy(loc_in, loc, sem.at[1]),
        pltpu.make_async_copy(static_ctl.at[:, mem], field.reshape(8, ROWS, LANES).at[0:VARS], sem.at[2]),
        pltpu.make_async_copy(static_coef, field.at[VARS * ROWS : 8 * ROWS], sem.at[3]),
    ]
    for copy in copies:
        copy.start()
    for copy in copies:
        copy.wait()
    pack_rows(lambda row: alpha_row(alpha, 1 - own, row), 16, a_f, a_b)
    for k in range(2):
        a_f[192 + k * 12 : 204 + k * 12, :] = loc[k * 16 + 4 : k * 16 + 16, :]
        a_b[192 + k * 12 : 204 + k * 12, :] = loc[k * 16 : k * 16 + 12, :]
    pack_rows(lambda row: field[pl.ds(row, 8, stride=ROWS), :], 8, a_f, a_b, 216)
    pack_rows(lambda row: alpha_row(alpha, own, row), 16, b_f, b_b)


def halo_loader(low, high, middle, width, base=0):
    def load(row):
        if row < STEPS:
            at = base + row * width
            return low[at : at + width, :]
        if row < STEPS + ROWS:
            return middle(row - STEPS)
        at = base + (row - STEPS - ROWS) * width
        return high[at : at + width, :]

    return load


def first_body(alpha, low, high, loc, perturb, sums, coefs, raw, buf0, buf1, local):
    parity = 1 - lax.axis_index("mem") % 2
    build_coefs(
        low[192:204, :], loc[0:16, :], high[192:204, :],
        low[204:216, :], loc[16:32, :], high[204:216, :], raw, coefs,
    )

    def emit(row, value):
        local[pl.ds(row, 16, stride=ROWS), :] = value

    load = halo_loader(low, high, lambda row: alpha_row(alpha, parity, row), 16)
    diffuse(load, 16, 16, coefs, (buf0, buf1), emit)
    for s in range(HALF):
        level = 2 * s + parity
        for v in range(VARS):
            total = local[s * 16 : s * 16 + 16, :] * perturb[0, v, level].astype(jnp.float32)
            total = total + local[128 + s * 16 : 144 + s * 16, :] * perturb[1, v, level].astype(jnp.float32)
            sums[s, v] = total


def static_first_body(low, high, field, out, coefs, raw, buf0, buf1, result):
    build_coefs(
        low[pl.ds(222, 12, stride=8), :], field[96:112, :], high[pl.ds(222, 12, stride=8), :],
        low[pl.ds(223, 12, stride=8), :], field[112:128, :], high[pl.ds(223, 12, stride=8), :], raw, coefs,
    )

    def emit(row, value):
        result[pl.ds(row, 8, stride=ROWS), :] = value

    load = halo_loader(low, high, lambda row: field[pl.ds(row, 8, stride=ROWS), :], 8, 216)
    diffuse(load, 8, 8, coefs, (buf0, buf1), emit)
    out[...] = result[0:96, :]


def second_body(alpha, low, high, coefs, out, buf0, buf1):
    def emit(row, value):
        out[pl.ds(row, 16, stride=ROWS), :] = value

    parity = lax.axis_index("mem") % 2
    load = halo_loader(low, high, lambda row: alpha_row(alpha, parity, row), 16)
    diffuse(load, 16, 16, coefs, (buf0, buf1), emit)


def sum_body(local, perturb, received, static, o0, o1, o2, o3):
    x, y, parity = place()
    for k, out in enumerate((o0, o1, o2, o3)):
        for j in range(2):
            s = (y ^ k) + 4 * j
            level = 2 * s + parity
            first = local[pl.ds(pl.multiple_of(s * 16, 16), 16), :]
            other = local[pl.ds(pl.multiple_of(128 + s * 16, 16), 16), :]
            for v in range(VARS):
                total = first * perturb[0, v, level].astype(jnp.float32)
                total = total + other * perturb[1, v, level].astype(jnp.float32)
                total = total + received[s, v]
                if k == 0:
                    total = total + jnp.where(x == j, static[v * 16 : v * 16 + 16, :], 0.0)
                out[j * 96 + v * 16 : j * 96 + v * 16 + 16, :] = total


def prepare_body(cell, mask, value, weight, sums, held, sem):
    _, y, c = place()
    copies = []
    for j in range(2):
        level = 2 * y + c + 8 * j
        for k, source in enumerate((weight, value)):
            spot = held.reshape(2, 2, VARS, 8, LANES).at[k, j]
            copies.append(pltpu.make_async_copy(source.at[:, level], spot, sem.at[2 * j + k]))
    for copy in copies:
        copy.start()
    for copy in copies:
        copy.wait()
    pieces = []
    for a in range(8):
        part = held[pl.ds(a, 24, stride=8), :]
        scaled = part[0:12, :] * mask[a : a + 1, :].astype(jnp.float32)
        pieces.append(jnp.concatenate([scaled, scaled * part[12:24, :]], axis=0))
    both = jnp.concatenate(pieces, axis=1)
    top = both.astype(jnp.bfloat16)
    rest = both - top.astype(jnp.float32)
    mid = rest.astype(jnp.bfloat16)
    low = (rest - mid.astype(jnp.float32)).astype(jnp.bfloat16)
    stacked = jnp.concatenate([top, mid, low], axis=0)
    cells = jnp.concatenate([cell[a : a + 1, :] for a in range(8)], axis=1)
    for block in range(8):
        ids = block * 256 + lax.broadcasted_iota(jnp.int32, (256, 1024), 0)
        hit = jnp.where(ids == cells, 1.0, 0.0).astype(jnp.bfloat16)
        got = lax.dot_general(stacked, hit, (((1,), (1,)), ((), ())), preferred_element_type=jnp.float32)
        total = got[0:24, :] + got[24:48, :] + got[48:72, :]
        for r in range(2):
            sums[pl.ds(block * 2 + r, 24, stride=ROWS), :] = total[:, r * LANES : (r + 1) * LANES]


def gradient_body(mine, other, sums, grad):
    total = mine[...] + other[...]
    grad[...] = sums[0:192, :] * total - sums[192:384, :]


def project(g, k, parity, perturb, middle):
    _, y, _ = place()
    for j in range(2):
        s = (y ^ k) + 4 * j
        level = 2 * s + parity
        fields = [g[j * 96 + v * 16 : j * 96 + v * 16 + 16, :] for v in range(VARS)]
        for m in range(2):
            total = perturb[m, 0, level].astype(jnp.float32) * fields[0]
            for v in range(1, VARS):
                total = total + perturb[m, v, level].astype(jnp.float32) * fields[v]
            middle[pl.ds(pl.multiple_of((m * HALF + s) * 16, 16), 16), :] = total


def project_own_body(g0, g1, g2, g3, perturb, forward, backward, middle, rest):
    x, _, c = place()
    for k, g in enumerate((g0, g1, g2, g3)):
        project(g, k, c, perturb, middle)
        if k > 0:
            rest[(k - 1) * 192 : k * 192, :] = g[...]
    pack_rows(lambda row: middle[pl.ds(row, 16, stride=ROWS), :], 16, forward, backward)
    pack_rows(lambda row: g0[pl.ds(x * 96 + row, VARS, stride=ROWS), :], VARS, forward, backward, 192)


def project_other_body(g0, rest, perturb, forward, backward, middle):
    _, _, c = place()
    project(g0, 0, 1 - c, perturb, middle)
    for k in range(1, 4):
        project(rest.at[(k - 1) * 192 : k * 192], k, 1 - c, perturb, middle)
    pack_rows(lambda row: middle[pl.ds(row, 16, stride=ROWS), :], 16, forward, backward)


def update_alpha(parity, out, alpha, mom, new_alpha, new_mom, stage0, stage1, sem):
    for m in range(2):
        for s in range(HALF):
            at = pl.ds(pl.multiple_of(m * 256 + (2 * s + parity) * 16, 16), 16)
            here = slice((m * HALF + s) * 16, (m * HALF + s) * 16 + 16)
            old = alpha[at, :]
            moved = momentum_rate * mom[at, :] + (old + out[here, :])
            stage1[here, :] = moved
            stage0[here, :] = old - step_rate * moved
    copies = [
        pltpu.make_async_copy(stage.reshape(2, HALF, ROWS, LANES), target.at[:, :, parity], sem.at[k])
        for k, (stage, target) in enumerate(((stage0, new_alpha), (stage1, new_mom)))
    ]
    for copy in copies:
        copy.start()
    return copies


def third_body(
    low, high, middle, coefs, alpha, mom, grad, static_coefs, field, static_mom,
    new_alpha, new_mom, new_static, new_static_mom,
    buf0, buf1, out, stage0, stage1, sem,
):
    x, _, c = place()

    def emit(row, value):
        out[pl.ds(row, 16, stride=ROWS), :] = value

    load = halo_loader(low, high, lambda row: middle[pl.ds(row, 16, stride=ROWS), :], 16)
    diffuse(load, 16, 16, coefs, (buf0, buf1), emit)
    copies = update_alpha(c, out, alpha, mom, new_alpha, new_mom, stage0, stage1, sem)

    load = halo_loader(low, high, lambda row: grad[pl.ds(x * 96 + row, VARS, stride=ROWS), :], VARS, 192)
    for row in range(SPAN):
        buf0[row * 8 : row * 8 + VARS, :] = load(row)

    def emit_static(row, value):
        out[pl.ds(row, 8, stride=ROWS), :] = value

    diffuse(lambda row: buf0[row * 8 : row * 8 + 8, :], 8, 8, static_coefs, (buf0, buf1), emit_static)
    old = field[0:96, :]
    moved = momentum_rate * static_mom[...] + (old + out[0:96, :])
    new_static_mom[...] = moved
    new_static[...] = old - step_rate * moved
    for copy in copies:
        copy.wait()


def fourth_body(
    low, high, middle, coefs, alpha, mom, half_alpha, half_mom, new_alpha, new_mom,
    buf0, buf1, out, stage0, stage1, sem,
):
    def emit(row, value):
        out[pl.ds(row, 16, stride=ROWS), :] = value

    load = halo_loader(low, high, lambda row: middle[pl.ds(row, 16, stride=ROWS), :], 16)
    diffuse(load, 16, 16, coefs, (buf0, buf1), emit)
    c = lax.axis_index("mem") % 2
    for copy in update_alpha(1 - c, out, alpha, mom, new_alpha, new_mom, stage0, stage1, sem):
        copy.wait()


def local(
    perturb,
    alpha,
    alpha_mom,
    static_ctl,
    static_mom,
    loc_coef,
    static_coef,
    obs_cell,
    obs_mask,
    obs_value,
    obs_weight,
):
    tiles = lax.axis_size("tile")
    up = [(i, (i + 1) % tiles) for i in range(tiles)]
    down = [(target, source) for source, target in up]
    members = lax.axis_size("mem")

    def swap(value, bits):
        return lax.ppermute(value, "mem", [(i, i ^ bits) for i in range(members)])

    def halo(forward, backward):
        return lax.ppermute(forward, "tile", up), lax.ppermute(backward, "tile", down)

    mom2 = alpha_mom.reshape(512, LANES)
    bufs16 = [f32(SPAN * 16, LANES), f32(SPAN * 16, LANES)]
    bufs8 = [f32(SPAN * 8, LANES), f32(SPAN * 8, LANES)]
    raw = f32(88, LANES)

    a_f, a_b, b_f, b_b, alpha2, loc2, field = call(
        pack_body,
        "pack",
        [HBM] * 4,
        [shape(312, LANES)] * 2 + [shape(192, LANES)] * 2 + [shape(512, LANES), shape(32, LANES), shape(128, LANES)],
        [pltpu.SemaphoreType.DMA((4,))],
        grant=GRANT,
    )(alpha.reshape(512, LANES), loc_coef.reshape(32, LANES), static_ctl, static_coef.reshape(32, LANES))
    a_low, a_high = halo(a_f, a_b)
    b_low, b_high = halo(b_f, b_b)

    (sums,) = call(
        prepare_body,
        "prepare",
        [VM, VM, ANY, ANY],
        [shape(384, LANES)],
        [f32(192, LANES), pltpu.SemaphoreType.DMA((4,))],
        flops=1000000000,
    )(
        obs_cell.reshape(8, LANES),
        obs_mask.reshape(8, LANES),
        obs_value.reshape(VARS, 16, 8, LANES),
        obs_weight.reshape(VARS, 16, 8, LANES),
    )

    part_a, loc_k = call(
        first_body,
        "first",
        [VM] * 5,
        [shape(HALF, VARS, ROWS, LANES), shape(200, LANES)],
        [raw] + bufs16 + [f32(256, LANES)],
        flops=BUSY,
    )(alpha2, a_low, a_high, loc2, perturb)
    got = swap(part_a, 1)
    static, static_k = call(
        static_first_body,
        "static_first",
        [VM] * 3,
        [shape(96, LANES), shape(200, LANES)],
        [raw] + bufs8 + [f32(128, LANES)],
        flops=BUSY,
    )(a_low, a_high, field)
    (second,) = call(second_body, "second", [VM] * 4, [shape(256, LANES)], bufs16, flops=BUSY)(
        alpha2, b_low, b_high, loc_k
    )
    quarter = shape(192, LANES)
    o0, o1, o2, o3 = call(sum_body, "sum", [VM] * 4, [quarter] * 4)(second, perturb, got, static)
    r1, r2, r3 = swap(o1, 2), swap(o2, 4), swap(o3, 6)
    mine = o0 + r1 + r2 + r3
    other = swap(mine, 8)
    (grad,) = call(gradient_body, "gradient", [VM] * 3, [quarter])(mine, other, sums)
    p0 = swap(grad, 1)
    gs = [grad] + [swap(grad, 2 * k) for k in range(1, 4)]
    p_f, p_b, p_m, rest = call(
        project_own_body,
        "project_own",
        [VM] * 5,
        [shape(264, LANES), shape(264, LANES), shape(256, LANES), shape(576, LANES)],
    )(*gs, perturb)
    p_low, p_high = halo(p_f, p_b)
    rest = swap(rest, 1)
    q_f, q_b, q_m = call(
        project_other_body, "project_other", [VM] * 3, [quarter, quarter, shape(256, LANES)]
    )(p0, rest, perturb)
    q_low, q_high = halo(q_f, q_b)
    whole = shape(2, HALF, 2, ROWS, LANES)
    stages = [f32(256, LANES)] * 3 + [pltpu.SemaphoreType.DMA((2,))]
    half_alpha, half_mom, new_static, new_static_mom = call(
        third_body,
        "third",
        [VM] * 10,
        [whole, whole, shape(96, LANES), shape(96, LANES)],
        bufs16 + stages,
        flops=BUSY,
        out_specs=[HBM, HBM, VM, VM],
    )(p_low, p_high, p_m, loc_k, alpha2, mom2, grad, static_k, field, static_mom.reshape(96, LANES))
    new_alpha, new_alpha_mom = call(
        fourth_body,
        "fourth",
        [VM] * 6 + [HBM] * 2,
        [whole, whole],
        bufs16 + stages,
        out_specs=[HBM, HBM],
        aliases={6: 0, 7: 1},
    )(q_low, q_high, q_m, loc_k, alpha2, mom2, half_alpha, half_mom)
    return (
        new_alpha.reshape(alpha.shape),
        new_alpha_mom.reshape(alpha.shape),
        new_static.reshape(static_mom.shape),
        new_static_mom.reshape(static_mom.shape),
    )


def solution(mesh):
    return jax.shard_map(
        local,
        mesh=mesh,
        in_specs=(
            P("mem", None, None, "tile", None),
            P("mem", None, "tile", None),
            P("mem", None, "tile", None),
            P(None, None, "tile", None),
            P(None, "mem", "tile", None),
            P(None, "tile", None),
            P(None, "tile", None),
            P("tile", None),
            P("tile", None),
            P(None, None, "tile", None),
            P(None, None, "tile", None),
        ),
        out_specs=(
            P("mem", None, "tile", None),
            P("mem", None, "tile", None),
            P(None, "mem", "tile", None),
            P(None, "mem", "tile", None),
        ),
        check_vma=False,
    )
```

```python
import functools

import jax
import jax.numpy as jnp
from jax import lax
from jax.experimental import pallas as pl
from jax.experimental.pallas import tpu as pltpu
from jax.sharding import PartitionSpec as P

STEPS = 12
ROWS = 16
LANES = 128
SPAN = ROWS + 2 * STEPS
VARS = 6
HALF = 8

momentum_rate = 0.9
step_rate = 0.5

GRANT = 54.6
GRANT2 = 53.2
BUSY = 5000000000

VM = pl.BlockSpec(memory_space=pltpu.VMEM)
ANY = pl.BlockSpec(memory_space=pl.ANY)
HBM = pl.BlockSpec(memory_space=pltpu.HBM)


def shape(*dims):
    return jax.ShapeDtypeStruct(dims, jnp.float32)


def call(body, name, ins, outs, scratch=(), flops=1000000, out_specs=None, grant=32):
    return pl.pallas_call(
        body,
        name=name,
        in_specs=list(ins),
        out_specs=out_specs or [VM] * len(outs),
        out_shape=list(outs),
        scratch_shapes=list(scratch),
        compiler_params=pltpu.CompilerParams(vmem_limit_bytes=int(grant * 1024 * 1024)),
        cost_estimate=pl.CostEstimate(flops=flops, bytes_accessed=1000000, transcendentals=0),
    )


def f32(*dims):
    return pltpu.VMEM(dims, jnp.float32)


def place():
    mem = lax.axis_index("mem")
    return mem // 8, (mem // 2) % 4, mem % 2


def pack_rows(load, width, forward, backward, base=0):
    for row in range(ROWS):
        value = load(row)
        if row >= ROWS - STEPS:
            at = base + (row - (ROWS - STEPS)) * width
            forward[at : at + width, :] = value
        if row < STEPS:
            at = base + row * width
            backward[at : at + width, :] = value


def build_coefs(low_x, mid_x, high_x, low_y, mid_y, high_y, raw, coefs):
    raw[0:8, :] = jnp.zeros((8, LANES), jnp.float32)
    raw[8:20, :] = low_x
    raw[20:36, :] = mid_x
    raw[36:48, :] = high_x
    raw[48:60, :] = low_y
    raw[60:76, :] = mid_y
    raw[76:88, :] = high_y
    extent = ROWS * lax.axis_size("tile")
    first = lax.axis_index("tile") * ROWS - STEPS
    at = first + lax.broadcasted_iota(jnp.int32, (SPAN, LANES), 0)
    lane = lax.broadcasted_iota(jnp.int32, (SPAN, LANES), 1)
    valid = (at >= 0) & (at < extent)
    below = jnp.where(valid, raw[8:48, :], 0.0)
    raw[8:48, :] = below
    above = jnp.where(valid, raw[7:47, :], 0.0)
    right = jnp.where(valid, raw[48:88, :], 0.0)
    left = jnp.where(lane > 0, pltpu.roll(right, 1, 1), 0.0)
    centre = 1.0 - below - above - right - left
    coefs[0:40, :] = jnp.where(valid, centre, 0.0)
    coefs[40:80, :] = jnp.where(at + 1 < extent, below, 0.0)
    coefs[80:120, :] = above
    coefs[120:160, :] = jnp.where(lane < LANES - 1, right, 0.0)
    coefs[160:200, :] = left


def diffuse(load, width, pitch, coefs, bufs, emit):
    for turn in range(STEPS):
        source = bufs[turn % 2]
        target = bufs[(turn + 1) % 2]
        if turn == 0:
            take = load
        else:
            take = lambda row: source[row * pitch : row * pitch + width, :]
        before = take(turn)
        here = take(turn + 1)
        for row in range(turn + 1, SPAN - 1 - turn):
            after = take(row + 1)
            new = coefs[row : row + 1, :] * here
            new = new + coefs[40 + row : 41 + row, :] * after
            new = new + coefs[80 + row : 81 + row, :] * before
            new = new + coefs[120 + row : 121 + row, :] * pltpu.roll(here, LANES - 1, 1)
            new = new + coefs[160 + row : 161 + row, :] * pltpu.roll(here, 1, 1)
            if turn == STEPS - 1:
                emit(row - STEPS, new)
            else:
                target[row * pitch : row * pitch + width, :] = new
            before = here
            here = after


def alpha_row(alpha, parity, row):
    parts = [alpha[pl.ds(m * 256 + parity * ROWS + row, HALF, stride=2 * ROWS), :] for m in range(2)]
    return jnp.concatenate(parts, axis=0)


def pack_body(alpha_in, loc_in, a_f, a_b, alpha, loc, sem):
    own = lax.axis_index("mem") % 2
    copies = [
        pltpu.make_async_copy(alpha_in, alpha, sem.at[0]),
        pltpu.make_async_copy(loc_in, loc, sem.at[1]),
    ]
    for copy in copies:
        copy.start()
    for copy in copies:
        copy.wait()
    pack_rows(lambda row: alpha_row(alpha, 1 - own, row), 16, a_f, a_b)
    for k in range(2):
        a_f[192 + k * 12 : 204 + k * 12, :] = loc[k * 16 + 4 : k * 16 + 16, :]
        a_b[192 + k * 12 : 204 + k * 12, :] = loc[k * 16 : k * 16 + 12, :]


def halo_loader(low, high, middle, width, base=0):
    def load(row):
        if row < STEPS:
            at = base + row * width
            return low[at : at + width, :]
        if row < STEPS + ROWS:
            return middle(row - STEPS)
        at = base + (row - STEPS - ROWS) * width
        return high[at : at + width, :]

    return load


def first_body(alpha, low, high, loc, perturb, sums, coefs, raw, buf0, buf1, local):
    parity = 1 - lax.axis_index("mem") % 2
    build_coefs(
        low[192:204, :], loc[0:16, :], high[192:204, :],
        low[204:216, :], loc[16:32, :], high[204:216, :], raw, coefs,
    )

    def emit(row, value):
        local[pl.ds(row, 16, stride=ROWS), :] = value

    load = halo_loader(low, high, lambda row: alpha_row(alpha, parity, row), 16)
    diffuse(load, 16, 16, coefs, (buf0, buf1), emit)
    for s in range(HALF):
        level = 2 * s + parity
        for v in range(VARS):
            total = local[s * 16 : s * 16 + 16, :] * perturb[0, v, level].astype(jnp.float32)
            total = total + local[128 + s * 16 : 144 + s * 16, :] * perturb[1, v, level].astype(jnp.float32)
            sums[s, v] = total


def static_first_body(low, high, field, out, coefs, raw, buf0, buf1, result):
    build_coefs(
        low[pl.ds(6, 12, stride=16), :], field[96:112, :], high[pl.ds(6, 12, stride=16), :],
        low[pl.ds(7, 12, stride=16), :], field[112:128, :], high[pl.ds(7, 12, stride=16), :], raw, coefs,
    )

    def emit(row, value):
        result[pl.ds(row, 16, stride=ROWS), :] = value

    load = halo_loader(low, high, lambda row: field[pl.ds(row, 16, stride=ROWS), :], 16)
    diffuse(load, 16, 16, coefs, (buf0, buf1), emit)
    for j in range(2):
        out[j * 96 : j * 96 + 96, :] = result[j * 128 : j * 128 + 96, :]


def second_body(alpha, low, high, coefs, out, buf0, buf1):
    def emit(row, value):
        out[pl.ds(row, 16, stride=ROWS), :] = value

    parity = lax.axis_index("mem") % 2
    load = halo_loader(low, high, lambda row: alpha_row(alpha, parity, row), 16)
    diffuse(load, 16, 16, coefs, (buf0, buf1), emit)


def sum_body(local, perturb, received, o0, o1, o2, o3):
    _, y, parity = place()
    for k, out in enumerate((o0, o1, o2, o3)):
        for j in range(2):
            s = (y ^ k) + 4 * j
            level = 2 * s + parity
            first = local[pl.ds(pl.multiple_of(s * 16, 16), 16), :]
            other = local[pl.ds(pl.multiple_of(128 + s * 16, 16), 16), :]
            for v in range(VARS):
                total = first * perturb[0, v, level].astype(jnp.float32)
                total = total + other * perturb[1, v, level].astype(jnp.float32)
                total = total + received[s, v]
                out[j * 96 + v * 16 : j * 96 + v * 16 + 16, :] = total


def prepare_body(
    alpha, cell, mask, value, weight, static_ctl, static_coef,
    sums, b_f, b_b, c_f, c_b, field, held, sem,
):
    _, y, c = place()
    copies = []
    for j in range(2):
        level = 2 * y + c + 8 * j
        for k, source in enumerate((weight, value)):
            spot = held.reshape(2, 2, VARS, 8, LANES).at[k, j]
            copies.append(pltpu.make_async_copy(source.at[:, level], spot, sem.at[3 * j + k]))
        spot = field.reshape(16, ROWS, LANES).at[8 * j : 8 * j + VARS]
        copies.append(pltpu.make_async_copy(static_ctl.at[:, level], spot, sem.at[3 * j + 2]))
    for copy in copies:
        copy.start()
    field[96:128, :] = static_coef[...]
    field[224:256, :] = jnp.zeros((32, LANES), jnp.float32)
    pack_rows(lambda row: alpha_row(alpha, c, row), 16, b_f, b_b)
    for copy in copies:
        copy.wait()
    pack_rows(lambda row: field[pl.ds(row, 16, stride=ROWS), :], 16, c_f, c_b)
    pieces = []
    for a in range(8):
        part = held[pl.ds(a, 24, stride=8), :]
        scaled = part[0:12, :] * mask[a : a + 1, :].astype(jnp.float32)
        pieces.append(jnp.concatenate([scaled, scaled * part[12:24, :]], axis=0))
    both = jnp.concatenate(pieces, axis=1)
    top = both.astype(jnp.bfloat16)
    rest = both - top.astype(jnp.float32)
    mid = rest.astype(jnp.bfloat16)
    low = (rest - mid.astype(jnp.float32)).astype(jnp.bfloat16)
    stacked = jnp.concatenate([top, mid, low], axis=0)
    cells = jnp.concatenate([cell[a : a + 1, :] for a in range(8)], axis=1)
    for block in range(8):
        ids = block * 256 + lax.broadcasted_iota(jnp.int32, (256, 1024), 0)
        hit = jnp.where(ids == cells, 1.0, 0.0).astype(jnp.bfloat16)
        got = lax.dot_general(stacked, hit, (((1,), (1,)), ((), ())), preferred_element_type=jnp.float32)
        total = got[0:24, :] + got[24:48, :] + got[48:72, :]
        for r in range(2):
            sums[pl.ds(block * 2 + r, 24, stride=ROWS), :] = total[:, r * LANES : (r + 1) * LANES]


def gradient_body(mine, other, static, sums, grad):
    total = mine[...] + other[...] + static[...]
    grad[...] = sums[0:192, :] * total - sums[192:384, :]


def project(g, k, parity, perturb, middle):
    _, y, _ = place()
    for j in range(2):
        s = (y ^ k) + 4 * j
        level = 2 * s + parity
        fields = [g[j * 96 + v * 16 : j * 96 + v * 16 + 16, :] for v in range(VARS)]
        for m in range(2):
            total = perturb[m, 0, level].astype(jnp.float32) * fields[0]
            for v in range(1, VARS):
                total = total + perturb[m, v, level].astype(jnp.float32) * fields[v]
            middle[pl.ds(pl.multiple_of((m * HALF + s) * 16, 16), 16), :] = total


def project_own_body(g0, g1, g2, g3, perturb, forward, backward, middle, rest):
    x, _, c = place()
    for k, g in enumerate((g0, g1, g2, g3)):
        project(g, k, c, perturb, middle)
        if k > 0:
            rest[(k - 1) * 192 : k * 192, :] = g[...]
    pack_rows(lambda row: middle[pl.ds(row, 16, stride=ROWS), :], 16, forward, backward)
    pack_rows(lambda row: g0[pl.ds(x * 96 + row, VARS, stride=ROWS), :], VARS, forward, backward, 192)


def project_other_body(g0, rest, perturb, forward, backward, middle):
    _, _, c = place()
    project(g0, 0, 1 - c, perturb, middle)
    for k in range(1, 4):
        project(rest.at[(k - 1) * 192 : k * 192], k, 1 - c, perturb, middle)
    pack_rows(lambda row: middle[pl.ds(row, 16, stride=ROWS), :], 16, forward, backward)


def update_alpha(parity, out, alpha, mom, stage0, stage1):
    for m in range(2):
        for s in range(HALF):
            at = pl.ds(pl.multiple_of(m * 256 + (2 * s + parity) * 16, 16), 16)
            here = slice((m * HALF + s) * 16, (m * HALF + s) * 16 + 16)
            old = alpha[at, :]
            moved = momentum_rate * mom[at, :] + (old + out[here, :])
            stage1[here, :] = moved
            stage0[here, :] = old - step_rate * moved


def third_body(
    low, high, middle, coefs, alpha, mom, grad, static_coefs, field, static_mom,
    stage0, stage1, new_static, new_static_mom, buf0, buf1, out,
):
    x, _, c = place()

    def emit(row, value):
        out[pl.ds(row, 16, stride=ROWS), :] = value

    load = halo_loader(low, high, lambda row: middle[pl.ds(row, 16, stride=ROWS), :], 16)
    diffuse(load, 16, 16, coefs, (buf0, buf1), emit)
    update_alpha(c, out, alpha, mom, stage0, stage1)

    load = halo_loader(low, high, lambda row: grad[pl.ds(x * 96 + row, VARS, stride=ROWS), :], VARS, 192)
    for row in range(SPAN):
        buf0[row * 8 : row * 8 + VARS, :] = load(row)

    def emit_static(row, value):
        out[pl.ds(row, 8, stride=ROWS), :] = value

    diffuse(lambda row: buf0[row * 8 : row * 8 + 8, :], 8, 8, static_coefs, (buf0, buf1), emit_static)
    old = field[pl.ds(pl.multiple_of(x * 128, 128), 96), :]
    moved = momentum_rate * static_mom[...] + (old + out[0:96, :])
    new_static_mom[...] = moved
    new_static[...] = old - step_rate * moved


def fourth_body(
    low, high, middle, coefs, alpha, mom, done0, done1, done2, done3,
    new_alpha, new_mom, new_static, new_static_mom,
    buf0, buf1, out, stage0, stage1, sem,
):
    c = lax.axis_index("mem") % 2

    def leave(source, target, parity, k):
        return pltpu.make_async_copy(source.reshape(2, HALF, ROWS, LANES), target.at[:, :, parity], sem.at[k])

    copies = [
        leave(done0, new_alpha, c, 0),
        leave(done1, new_mom, c, 1),
        pltpu.make_async_copy(done2, new_static, sem.at[2]),
        pltpu.make_async_copy(done3, new_static_mom, sem.at[3]),
    ]
    for copy in copies:
        copy.start()

    def emit(row, value):
        out[pl.ds(row, 16, stride=ROWS), :] = value

    load = halo_loader(low, high, lambda row: middle[pl.ds(row, 16, stride=ROWS), :], 16)
    diffuse(load, 16, 16, coefs, (buf0, buf1), emit)
    update_alpha(1 - c, out, alpha, mom, stage0, stage1)
    last = [leave(stage0, new_alpha, 1 - c, 4), leave(stage1, new_mom, 1 - c, 5)]
    for copy in last:
        copy.start()
    for copy in copies + last:
        copy.wait()


def local(
    perturb,
    alpha,
    alpha_mom,
    static_ctl,
    static_mom,
    loc_coef,
    static_coef,
    obs_cell,
    obs_mask,
    obs_value,
    obs_weight,
):
    tiles = lax.axis_size("tile")
    up = [(i, (i + 1) % tiles) for i in range(tiles)]
    down = [(target, source) for source, target in up]
    members = lax.axis_size("mem")

    def swap(value, bits):
        return lax.ppermute(value, "mem", [(i, i ^ bits) for i in range(members)])

    def halo(forward, backward):
        return lax.ppermute(forward, "tile", up), lax.ppermute(backward, "tile", down)

    mom2 = alpha_mom.reshape(512, LANES)
    bufs16 = [f32(SPAN * 16, LANES), f32(SPAN * 16, LANES)]
    raw = f32(88, LANES)

    alpha2 = alpha.reshape(512, LANES)
    loc2 = loc_coef.reshape(32, LANES)
    quarter = shape(192, LANES)
    half = shape(256, LANES)
    a_f, a_b = call(
        pack_body,
        "pack",
        [HBM] * 2,
        [shape(216, LANES)] * 2,
        [f32(512, LANES), f32(32, LANES), pltpu.SemaphoreType.DMA((2,))],
        grant=GRANT,
    )(alpha2, loc2)
    a_low, a_high = halo(a_f, a_b)
    sums, b_f, b_b, c_f, c_b, field = call(
        prepare_body,
        "prepare",
        [VM] * 3 + [HBM] * 3 + [VM],
        [shape(384, LANES)] + [quarter] * 4 + [half],
        [f32(192, LANES), pltpu.SemaphoreType.DMA((6,))],
        grant=GRANT2,
        flops=BUSY,
    )(
        alpha2,
        obs_cell.reshape(8, LANES),
        obs_mask.reshape(8, LANES),
        obs_value.reshape(VARS, 16, 8, LANES),
        obs_weight.reshape(VARS, 16, 8, LANES),
        static_ctl,
        static_coef.reshape(32, LANES),
    )
    b_low, b_high = halo(b_f, b_b)

    part_a, loc_k = call(
        first_body,
        "first",
        [VM] * 5,
        [shape(HALF, VARS, ROWS, LANES), shape(200, LANES)],
        [raw] + bufs16 + [f32(256, LANES)],
        flops=BUSY,
    )(alpha2, a_low, a_high, loc2, perturb)
    got = swap(part_a, 1)
    (second,) = call(second_body, "second", [VM] * 4, [half], bufs16, flops=BUSY)(alpha2, b_low, b_high, loc_k)
    o0, o1, o2, o3 = call(sum_body, "sum", [VM] * 3, [quarter] * 4)(second, perturb, got)
    r1, r2, r3 = swap(o1, 2), swap(o2, 4), swap(o3, 6)
    mine = o0 + r1 + r2 + r3
    other = swap(mine, 8)
    c_low, c_high = halo(*lax.optimization_barrier((c_f, c_b, o0))[:2])
    static, static_k = call(
        static_first_body,
        "static_first",
        [VM] * 3,
        [quarter, shape(200, LANES)],
        [raw] + bufs16 + [f32(256, LANES)],
        flops=BUSY,
    )(c_low, c_high, field)
    (grad,) = call(gradient_body, "gradient", [VM] * 4, [quarter])(mine, other, static, sums)
    p0 = swap(grad, 1)
    gs = [grad] + [swap(grad, 2 * k) for k in range(1, 4)]
    p_f, p_b, p_m, rest = call(
        project_own_body,
        "project_own",
        [VM] * 5,
        [shape(264, LANES), shape(264, LANES), shape(256, LANES), shape(576, LANES)],
    )(*gs, perturb)
    p_low, p_high = halo(p_f, p_b)
    rest = swap(rest, 1)
    q_f, q_b, q_m = call(
        project_other_body, "project_other", [VM] * 3, [quarter, quarter, shape(256, LANES)]
    )(p0, rest, perturb)
    q_low, q_high = halo(q_f, q_b)
    whole = shape(2, HALF, 2, ROWS, LANES)
    ready = call(
        third_body,
        "third",
        [VM] * 10,
        [half, half, shape(96, LANES), shape(96, LANES)],
        bufs16 + [f32(256, LANES)],
        flops=BUSY,
    )(p_low, p_high, p_m, loc_k, alpha2, mom2, grad, static_k, field, static_mom.reshape(96, LANES))
    new_alpha, new_alpha_mom, new_static, new_static_mom = call(
        fourth_body,
        "fourth",
        [VM] * 10,
        [whole, whole, shape(96, LANES), shape(96, LANES)],
        bufs16 + [f32(256, LANES)] * 3 + [pltpu.SemaphoreType.DMA((6,))],
        out_specs=[HBM] * 4,
    )(q_low, q_high, q_m, loc_k, alpha2, mom2, *ready)
    return (
        new_alpha.reshape(alpha.shape),
        new_alpha_mom.reshape(alpha.shape),
        new_static.reshape(static_mom.shape),
        new_static_mom.reshape(static_mom.shape),
    )


def solution(mesh):
    return jax.shard_map(
        local,
        mesh=mesh,
        in_specs=(
            P("mem", None, None, "tile", None),
            P("mem", None, "tile", None),
            P("mem", None, "tile", None),
            P(None, None, "tile", None),
            P(None, "mem", "tile", None),
            P(None, "tile", None),
            P(None, "tile", None),
            P("tile", None),
            P("tile", None),
            P(None, None, "tile", None),
            P(None, None, "tile", None),
        ),
        out_specs=(
            P("mem", None, "tile", None),
            P("mem", None, "tile", None),
            P(None, "mem", "tile", None),
            P(None, "mem", "tile", None),
        ),
        check_vma=False,
    )
```

```python
import functools

import jax
import jax.numpy as jnp
from jax import lax
from jax.experimental import pallas as pl
from jax.experimental.pallas import tpu as pltpu
from jax.sharding import PartitionSpec as P

STEPS = 12
ROWS = 16
LANES = 128
SPAN = ROWS + 2 * STEPS
VARS = 6
HALF = 8

momentum_rate = 0.9
step_rate = 0.5

GRANT = 54.6
GRANT2 = 53.2
BUSY = 5000000000

VM = pl.BlockSpec(memory_space=pltpu.VMEM)
ANY = pl.BlockSpec(memory_space=pl.ANY)
HBM = pl.BlockSpec(memory_space=pltpu.HBM)


def shape(*dims):
    return jax.ShapeDtypeStruct(dims, jnp.float32)


def call(body, name, ins, outs, scratch=(), flops=1000000, out_specs=None, grant=32):
    return pl.pallas_call(
        body,
        name=name,
        in_specs=list(ins),
        out_specs=out_specs or [VM] * len(outs),
        out_shape=list(outs),
        scratch_shapes=list(scratch),
        compiler_params=pltpu.CompilerParams(vmem_limit_bytes=int(grant * 1024 * 1024)),
        cost_estimate=pl.CostEstimate(flops=flops, bytes_accessed=1000000, transcendentals=0),
    )


def f32(*dims):
    return pltpu.VMEM(dims, jnp.float32)


def place():
    mem = lax.axis_index("mem")
    return mem // 8, (mem // 2) % 4, mem % 2


def pack_rows(load, width, forward, backward, base=0):
    for row in range(ROWS):
        value = load(row)
        if row >= ROWS - STEPS:
            at = base + (row - (ROWS - STEPS)) * width
            forward[at : at + width, :] = value
        if row < STEPS:
            at = base + row * width
            backward[at : at + width, :] = value


def build_coefs(low_x, mid_x, high_x, low_y, mid_y, high_y, raw, coefs):
    raw[0:8, :] = jnp.zeros((8, LANES), jnp.float32)
    raw[8:20, :] = low_x
    raw[20:36, :] = mid_x
    raw[36:48, :] = high_x
    raw[48:60, :] = low_y
    raw[60:76, :] = mid_y
    raw[76:88, :] = high_y
    extent = ROWS * lax.axis_size("tile")
    first = lax.axis_index("tile") * ROWS - STEPS
    at = first + lax.broadcasted_iota(jnp.int32, (SPAN, LANES), 0)
    lane = lax.broadcasted_iota(jnp.int32, (SPAN, LANES), 1)
    valid = (at >= 0) & (at < extent)
    below = jnp.where(valid, raw[8:48, :], 0.0)
    raw[8:48, :] = below
    above = jnp.where(valid, raw[7:47, :], 0.0)
    right = jnp.where(valid, raw[48:88, :], 0.0)
    left = jnp.where(lane > 0, pltpu.roll(right, 1, 1), 0.0)
    centre = 1.0 - below - above - right - left
    coefs[0:40, :] = jnp.where(valid, centre, 0.0)
    coefs[40:80, :] = jnp.where(at + 1 < extent, below, 0.0)
    coefs[80:120, :] = above
    coefs[120:160, :] = jnp.where(lane < LANES - 1, right, 0.0)
    coefs[160:200, :] = left


def diffuse(load, width, pitch, coefs, bufs, emit):
    for turn in range(STEPS):
        source = bufs[turn % 2]
        target = bufs[(turn + 1) % 2]
        if turn == 0:
            take = load
        else:
            take = lambda row: source[row * pitch : row * pitch + width, :]
        before = take(turn)
        here = take(turn + 1)
        for row in range(turn + 1, SPAN - 1 - turn):
            after = take(row + 1)
            new = coefs[row : row + 1, :] * here
            new = new + coefs[40 + row : 41 + row, :] * after
            new = new + coefs[80 + row : 81 + row, :] * before
            new = new + coefs[120 + row : 121 + row, :] * pltpu.roll(here, LANES - 1, 1)
            new = new + coefs[160 + row : 161 + row, :] * pltpu.roll(here, 1, 1)
            if turn == STEPS - 1:
                emit(row - STEPS, new)
            else:
                target[row * pitch : row * pitch + width, :] = new
            before = here
            here = after


def alpha_row(alpha, parity, row):
    parts = [alpha[pl.ds(m * 256 + parity * ROWS + row, HALF, stride=2 * ROWS), :] for m in range(2)]
    return jnp.concatenate(parts, axis=0)


def pack_body(alpha_in, loc_in, a_f, a_b, alpha, loc, sem):
    own = lax.axis_index("mem") % 2
    copies = [
        pltpu.make_async_copy(alpha_in, alpha, sem.at[0]),
        pltpu.make_async_copy(loc_in, loc, sem.at[1]),
    ]
    for copy in copies:
        copy.start()
    for copy in copies:
        copy.wait()
    pack_rows(lambda row: alpha_row(alpha, 1 - own, row), 16, a_f, a_b)
    for k in range(2):
        a_f[192 + k * 12 : 204 + k * 12, :] = loc[k * 16 + 4 : k * 16 + 16, :]
        a_b[192 + k * 12 : 204 + k * 12, :] = loc[k * 16 : k * 16 + 12, :]


def halo_loader(low, high, middle, width, base=0):
    def load(row):
        if row < STEPS:
            at = base + row * width
            return low[at : at + width, :]
        if row < STEPS + ROWS:
            return middle(row - STEPS)
        at = base + (row - STEPS - ROWS) * width
        return high[at : at + width, :]

    return load


def first_body(alpha, low, high, loc, perturb, ready, sums, coefs, raw, buf0, buf1, local):
    parity = 1 - lax.axis_index("mem") % 2
    build_coefs(
        low[192:204, :], loc[0:16, :], high[192:204, :],
        low[204:216, :], loc[16:32, :], high[204:216, :], raw, coefs,
    )

    def emit(row, value):
        local[pl.ds(row, 16, stride=ROWS), :] = value

    load = halo_loader(low, high, lambda row: alpha_row(alpha, parity, row), 16)
    diffuse(load, 16, 16, coefs, (buf0, buf1), emit)
    for s in range(HALF):
        level = 2 * s + parity
        for v in range(VARS):
            total = local[s * 16 : s * 16 + 16, :] * perturb[0, v, level].astype(jnp.float32)
            total = total + local[128 + s * 16 : 144 + s * 16, :] * perturb[1, v, level].astype(jnp.float32)
            sums[s, v] = total


def static_first_body(low, high, field, out, coefs, raw, buf0, buf1, result):
    build_coefs(
        low[pl.ds(6, 12, stride=16), :], field[96:112, :], high[pl.ds(6, 12, stride=16), :],
        low[pl.ds(7, 12, stride=16), :], field[112:128, :], high[pl.ds(7, 12, stride=16), :], raw, coefs,
    )

    def emit(row, value):
        result[pl.ds(row, 16, stride=ROWS), :] = value

    load = halo_loader(low, high, lambda row: field[pl.ds(row, 16, stride=ROWS), :], 16)
    diffuse(load, 16, 16, coefs, (buf0, buf1), emit)
    for j in range(2):
        out[j * 96 : j * 96 + 96, :] = result[j * 128 : j * 128 + 96, :]


def second_body(alpha, low, high, coefs, out, buf0, buf1):
    def emit(row, value):
        out[pl.ds(row, 16, stride=ROWS), :] = value

    parity = lax.axis_index("mem") % 2
    load = halo_loader(low, high, lambda row: alpha_row(alpha, parity, row), 16)
    diffuse(load, 16, 16, coefs, (buf0, buf1), emit)


def sum_body(local, perturb, received, o0, o1, o2, o3):
    _, y, parity = place()
    for k, out in enumerate((o0, o1, o2, o3)):
        for j in range(2):
            s = (y ^ k) + 4 * j
            level = 2 * s + parity
            first = local[pl.ds(pl.multiple_of(s * 16, 16), 16), :]
            other = local[pl.ds(pl.multiple_of(128 + s * 16, 16), 16), :]
            for v in range(VARS):
                total = first * perturb[0, v, level].astype(jnp.float32)
                total = total + other * perturb[1, v, level].astype(jnp.float32)
                total = total + received[s, v]
                out[j * 96 + v * 16 : j * 96 + v * 16 + 16, :] = total


def fetch_body(
    alpha_in, cell_in, mask_in, value, weight, static_ctl, static_coef,
    b_f, b_b, c_f, c_b, field, held, cell, mask, alpha, sem,
):
    _, y, c = place()
    first = pltpu.make_async_copy(alpha_in, alpha, sem.at[0])
    first.start()
    copies = [
        pltpu.make_async_copy(cell_in, cell, sem.at[1]),
        pltpu.make_async_copy(mask_in, mask, sem.at[2]),
        pltpu.make_async_copy(static_coef, field.at[96:128], sem.at[3]),
    ]
    for j in range(2):
        level = 2 * y + c + 8 * j
        for k, source in enumerate((weight, value)):
            spot = held.reshape(2, 2, VARS, 8, LANES).at[k, j]
            copies.append(pltpu.make_async_copy(source.at[:, level], spot, sem.at[4 + 3 * j + k]))
        spot = field.reshape(16, ROWS, LANES).at[8 * j : 8 * j + VARS]
        copies.append(pltpu.make_async_copy(static_ctl.at[:, level], spot, sem.at[6 + 3 * j]))
    for copy in copies:
        copy.start()
    field[224:256, :] = jnp.zeros((32, LANES), jnp.float32)
    first.wait()
    pack_rows(lambda row: alpha_row(alpha, c, row), 16, b_f, b_b)
    for copy in copies:
        copy.wait()
    pack_rows(lambda row: field[pl.ds(row, 16, stride=ROWS), :], 16, c_f, c_b)


def prepare_body(cell, mask, held, sums):
    pieces = []
    for a in range(8):
        part = held[pl.ds(a, 24, stride=8), :]
        scaled = part[0:12, :] * mask[a : a + 1, :].astype(jnp.float32)
        pieces.append(jnp.concatenate([scaled, scaled * part[12:24, :]], axis=0))
    both = jnp.concatenate(pieces, axis=1)
    top = both.astype(jnp.bfloat16)
    rest = both - top.astype(jnp.float32)
    mid = rest.astype(jnp.bfloat16)
    low = (rest - mid.astype(jnp.float32)).astype(jnp.bfloat16)
    stacked = jnp.concatenate([top, mid, low], axis=0)
    cells = jnp.concatenate([cell[a : a + 1, :] for a in range(8)], axis=1)
    for block in range(8):
        ids = block * 256 + lax.broadcasted_iota(jnp.int32, (256, 1024), 0)
        hit = jnp.where(ids == cells, 1.0, 0.0).astype(jnp.bfloat16)
        got = lax.dot_general(stacked, hit, (((1,), (1,)), ((), ())), preferred_element_type=jnp.float32)
        total = got[0:24, :] + got[24:48, :] + got[48:72, :]
        for r in range(2):
            sums[pl.ds(block * 2 + r, 24, stride=ROWS), :] = total[:, r * LANES : (r + 1) * LANES]


def gradient_body(mine, other, static, sums, grad, forward, backward):
    x, _, _ = place()
    total = mine[...] + other[...] + static[...]
    grad[...] = sums[0:192, :] * total - sums[192:384, :]
    pack_rows(lambda row: grad[pl.ds(x * 96 + row, VARS, stride=ROWS), :], VARS, forward, backward)


def project(g, k, parity, perturb, middle):
    _, y, _ = place()
    for j in range(2):
        s = (y ^ k) + 4 * j
        level = 2 * s + parity
        fields = [g[j * 96 + v * 16 : j * 96 + v * 16 + 16, :] for v in range(VARS)]
        for m in range(2):
            total = perturb[m, 0, level].astype(jnp.float32) * fields[0]
            for v in range(1, VARS):
                total = total + perturb[m, v, level].astype(jnp.float32) * fields[v]
            middle[pl.ds(pl.multiple_of((m * HALF + s) * 16, 16), 16), :] = total


def project_own_body(g0, g2, g1, g3, perturb, low, high, forward, backward, middle, rest, low_out, high_out):
    _, _, c = place()
    low_out[...] = low[...]
    high_out[...] = high[...]
    for k, g in enumerate((g0, g1, g2, g3)):
        project(g, k, c, perturb, middle)
        if k > 0:
            rest[(k - 1) * 192 : k * 192, :] = g[...]
    pack_rows(lambda row: middle[pl.ds(row, 16, stride=ROWS), :], 16, forward, backward)


def project_other_body(g0, rest, perturb, forward, backward, middle):
    _, _, c = place()
    project(g0, 0, 1 - c, perturb, middle)
    for k in range(1, 4):
        project(rest.at[(k - 1) * 192 : k * 192], k, 1 - c, perturb, middle)
    pack_rows(lambda row: middle[pl.ds(row, 16, stride=ROWS), :], 16, forward, backward)


def update_alpha(parity, out, alpha, mom, stage0, stage1):
    for m in range(2):
        for s in range(HALF):
            at = pl.ds(pl.multiple_of(m * 256 + (2 * s + parity) * 16, 16), 16)
            here = slice((m * HALF + s) * 16, (m * HALF + s) * 16 + 16)
            old = alpha[at, :]
            moved = momentum_rate * mom[at, :] + (old + out[here, :])
            stage1[here, :] = moved
            stage0[here, :] = old - step_rate * moved


def third_body(low, high, middle, coefs, alpha, mom, stage0, stage1, buf0, buf1, out):
    def emit(row, value):
        out[pl.ds(row, 16, stride=ROWS), :] = value

    load = halo_loader(low, high, lambda row: middle[pl.ds(row, 16, stride=ROWS), :], 16)
    diffuse(load, 16, 16, coefs, (buf0, buf1), emit)
    update_alpha(lax.axis_index("mem") % 2, out, alpha, mom, stage0, stage1)


def static_last_body(low, high, grad, coefs, field, static_mom, new_static, new_static_mom, buf0, buf1, out):
    x, _, _ = place()
    load = halo_loader(low, high, lambda row: grad[pl.ds(x * 96 + row, VARS, stride=ROWS), :], VARS)
    for row in range(SPAN):
        buf0[row * 8 : row * 8 + VARS, :] = load(row)

    def emit(row, value):
        out[pl.ds(row, 8, stride=ROWS), :] = value

    diffuse(lambda row: buf0[row * 8 : row * 8 + 8, :], 8, 8, coefs, (buf0, buf1), emit)
    old = field[pl.ds(pl.multiple_of(x * 128, 128), 96), :]
    moved = momentum_rate * static_mom[...] + (old + out[0:96, :])
    new_static_mom[...] = moved
    new_static[...] = old - step_rate * moved


def fourth_body(
    low, high, middle, coefs, alpha, mom, done0, done1, done2, done3,
    new_alpha, new_mom, new_static, new_static_mom,
    buf0, buf1, out, stage0, stage1, sem,
):
    c = lax.axis_index("mem") % 2

    def leave(source, target, parity, k):
        return pltpu.make_async_copy(source.reshape(2, HALF, ROWS, LANES), target.at[:, :, parity], sem.at[k])

    copies = [
        leave(done0, new_alpha, c, 0),
        leave(done1, new_mom, c, 1),
        pltpu.make_async_copy(done2, new_static, sem.at[2]),
        pltpu.make_async_copy(done3, new_static_mom, sem.at[3]),
    ]
    for copy in copies:
        copy.start()

    def emit(row, value):
        out[pl.ds(row, 16, stride=ROWS), :] = value

    load = halo_loader(low, high, lambda row: middle[pl.ds(row, 16, stride=ROWS), :], 16)
    diffuse(load, 16, 16, coefs, (buf0, buf1), emit)
    update_alpha(1 - c, out, alpha, mom, stage0, stage1)
    last = [leave(stage0, new_alpha, 1 - c, 4), leave(stage1, new_mom, 1 - c, 5)]
    for copy in last:
        copy.start()
    for copy in copies + last:
        copy.wait()


def local(
    perturb,
    alpha,
    alpha_mom,
    static_ctl,
    static_mom,
    loc_coef,
    static_coef,
    obs_cell,
    obs_mask,
    obs_value,
    obs_weight,
):
    tiles = lax.axis_size("tile")
    up = [(i, (i + 1) % tiles) for i in range(tiles)]
    down = [(target, source) for source, target in up]
    members = lax.axis_size("mem")

    def swap(value, bits):
        return lax.ppermute(value, "mem", [(i, i ^ bits) for i in range(members)])

    def halo(forward, backward):
        return lax.ppermute(forward, "tile", up), lax.ppermute(backward, "tile", down)

    mom2 = alpha_mom.reshape(512, LANES)
    bufs16 = [f32(SPAN * 16, LANES), f32(SPAN * 16, LANES)]
    raw = f32(88, LANES)

    alpha2 = alpha.reshape(512, LANES)
    loc2 = loc_coef.reshape(32, LANES)
    quarter = shape(192, LANES)
    half = shape(256, LANES)
    a_f, a_b = call(
        pack_body,
        "pack",
        [HBM] * 2,
        [shape(216, LANES)] * 2,
        [f32(512, LANES), f32(32, LANES), pltpu.SemaphoreType.DMA((2,))],
        grant=GRANT,
    )(alpha2, loc2)
    a_low, a_high = halo(a_f, a_b)
    ints = jax.ShapeDtypeStruct((8, LANES), jnp.int32)
    b_f, b_b, c_f, c_b, field, held, cell, mask = call(
        fetch_body,
        "fetch",
        [HBM] * 7,
        [quarter] * 4 + [half, quarter, ints, ints],
        [f32(512, LANES), pltpu.SemaphoreType.DMA((10,))],
        flops=BUSY,
        grant=GRANT2,
    )(
        alpha2,
        obs_cell.reshape(8, LANES),
        obs_mask.reshape(8, LANES),
        obs_value.reshape(VARS, 16, 8, LANES),
        obs_weight.reshape(VARS, 16, 8, LANES),
        static_ctl,
        static_coef.reshape(32, LANES),
    )
    b_low, b_high = halo(b_f, b_b)
    (sums,) = call(prepare_body, "prepare", [VM] * 3, [shape(384, LANES)], flops=BUSY)(cell, mask, held)

    part_a, loc_k = call(
        first_body,
        "first",
        [VM] * 6,
        [shape(HALF, VARS, ROWS, LANES), shape(200, LANES)],
        [raw] + bufs16 + [f32(256, LANES)],
        flops=BUSY,
    )(alpha2, a_low, a_high, loc2, perturb, sums)
    got = swap(part_a, 1)
    (second,) = call(second_body, "second", [VM] * 4, [half], bufs16, flops=BUSY)(alpha2, b_low, b_high, loc_k)
    o0, o1, o2, o3 = call(sum_body, "sum", [VM] * 3, [quarter] * 4)(second, perturb, got)
    r2, r1, r3 = swap(o2, 4), swap(o1, 2), swap(o3, 6)
    mine = o0 + r2 + r1 + r3
    other = swap(mine, 8)
    c_low, c_high = halo(*lax.optimization_barrier((c_f, c_b, o0))[:2])
    static, static_k = call(
        static_first_body,
        "static_first",
        [VM] * 3,
        [quarter, shape(200, LANES)],
        [raw] + bufs16 + [f32(256, LANES)],
        flops=BUSY,
    )(c_low, c_high, field)
    narrow = shape(72, LANES)
    grad, g_f, g_b = call(gradient_body, "gradient", [VM] * 4, [quarter, narrow, narrow])(mine, other, static, sums)
    g2, g1, g3 = swap(grad, 4), swap(grad, 2), swap(grad, 6)
    g_low, g_high = halo(g_f, g_b)
    p0 = swap(grad, 1)
    gs = [grad, g2, g1, g3]
    p_f, p_b, p_m, rest, g_low, g_high = call(
        project_own_body,
        "project_own",
        [VM] * 7,
        [quarter, quarter, half, shape(576, LANES), narrow, narrow],
    )(*gs, perturb, g_low, g_high)
    p_low, p_high = halo(p_f, p_b)
    rest = swap(rest, 1)
    q_f, q_b, q_m = call(project_other_body, "project_other", [VM] * 3, [quarter, quarter, half])(p0, rest, perturb)
    q_low, q_high = halo(q_f, q_b)
    whole = shape(2, HALF, 2, ROWS, LANES)
    work = bufs16 + [f32(256, LANES)]
    static_ready = call(static_last_body, "static_last", [VM] * 6, [shape(96, LANES)] * 2, work, flops=BUSY)(
        g_low, g_high, grad, static_k, field, static_mom.reshape(96, LANES)
    )
    ready = call(third_body, "third", [VM] * 6, [half, half], work, flops=BUSY)(
        p_low, p_high, p_m, loc_k, alpha2, mom2
    )
    new_alpha, new_alpha_mom, new_static, new_static_mom = call(
        fourth_body,
        "fourth",
        [VM] * 10,
        [whole, whole, shape(96, LANES), shape(96, LANES)],
        bufs16 + [f32(256, LANES)] * 3 + [pltpu.SemaphoreType.DMA((6,))],
        out_specs=[HBM] * 4,
    )(q_low, q_high, q_m, loc_k, alpha2, mom2, *ready, *static_ready)
    return (
        new_alpha.reshape(alpha.shape),
        new_alpha_mom.reshape(alpha.shape),
        new_static.reshape(static_mom.shape),
        new_static_mom.reshape(static_mom.shape),
    )


def solution(mesh):
    return jax.shard_map(
        local,
        mesh=mesh,
        in_specs=(
            P("mem", None, None, "tile", None),
            P("mem", None, "tile", None),
            P("mem", None, "tile", None),
            P(None, None, "tile", None),
            P(None, "mem", "tile", None),
            P(None, "tile", None),
            P(None, "tile", None),
            P("tile", None),
            P("tile", None),
            P(None, None, "tile", None),
            P(None, None, "tile", None),
        ),
        out_specs=(
            P("mem", None, "tile", None),
            P("mem", None, "tile", None),
            P(None, "mem", "tile", None),
            P(None, "mem", "tile", None),
        ),
        check_vma=False,
    )
```

```python
import functools

import jax
import jax.numpy as jnp
from jax import lax
from jax.experimental import pallas as pl
from jax.experimental.pallas import tpu as pltpu
from jax.sharding import PartitionSpec as P

STEPS = 12
ROWS = 16
LANES = 128
SPAN = ROWS + 2 * STEPS
VARS = 6
HALF = 8

momentum_rate = 0.9
step_rate = 0.5

GRANT = 54.6
GRANT2 = 53.2
BUSY = 5000000000

VM = pl.BlockSpec(memory_space=pltpu.VMEM)
ANY = pl.BlockSpec(memory_space=pl.ANY)
HBM = pl.BlockSpec(memory_space=pltpu.HBM)


def shape(*dims):
    return jax.ShapeDtypeStruct(dims, jnp.float32)


def call(body, name, ins, outs, scratch=(), flops=1000000, out_specs=None, grant=32):
    return pl.pallas_call(
        body,
        name=name,
        in_specs=list(ins),
        out_specs=out_specs or [VM] * len(outs),
        out_shape=list(outs),
        scratch_shapes=list(scratch),
        compiler_params=pltpu.CompilerParams(vmem_limit_bytes=int(grant * 1024 * 1024)),
        cost_estimate=pl.CostEstimate(flops=flops, bytes_accessed=1000000, transcendentals=0),
    )


def f32(*dims):
    return pltpu.VMEM(dims, jnp.float32)


def place():
    mem = lax.axis_index("mem")
    return mem // 8, (mem // 2) % 4, mem % 2


def pack_rows(load, width, forward, backward, base=0):
    for row in range(ROWS):
        value = load(row)
        if row >= ROWS - STEPS:
            at = base + (row - (ROWS - STEPS)) * width
            forward[at : at + width, :] = value
        if row < STEPS:
            at = base + row * width
            backward[at : at + width, :] = value


def build_coefs(low_x, mid_x, high_x, low_y, mid_y, high_y, raw, coefs):
    raw[0:8, :] = jnp.zeros((8, LANES), jnp.float32)
    raw[8:20, :] = low_x
    raw[20:36, :] = mid_x
    raw[36:48, :] = high_x
    raw[48:60, :] = low_y
    raw[60:76, :] = mid_y
    raw[76:88, :] = high_y
    extent = ROWS * lax.axis_size("tile")
    first = lax.axis_index("tile") * ROWS - STEPS
    at = first + lax.broadcasted_iota(jnp.int32, (SPAN, LANES), 0)
    lane = lax.broadcasted_iota(jnp.int32, (SPAN, LANES), 1)
    valid = (at >= 0) & (at < extent)
    below = jnp.where(valid, raw[8:48, :], 0.0)
    raw[8:48, :] = below
    above = jnp.where(valid, raw[7:47, :], 0.0)
    right = jnp.where(valid, raw[48:88, :], 0.0)
    left = jnp.where(lane > 0, pltpu.roll(right, 1, 1), 0.0)
    centre = 1.0 - below - above - right - left
    coefs[0:40, :] = jnp.where(valid, centre, 0.0)
    coefs[40:80, :] = jnp.where(at + 1 < extent, below, 0.0)
    coefs[80:120, :] = above
    coefs[120:160, :] = jnp.where(lane < LANES - 1, right, 0.0)
    coefs[160:200, :] = left


def diffuse(load, width, pitch, coefs, bufs, emit):
    for turn in range(STEPS):
        source = bufs[turn % 2]
        target = bufs[(turn + 1) % 2]
        if turn == 0:
            take = load
        else:
            take = lambda row: source[row * pitch : row * pitch + width, :]
        before = take(turn)
        here = take(turn + 1)
        for row in range(turn + 1, SPAN - 1 - turn):
            after = take(row + 1)
            new = coefs[row : row + 1, :] * here
            new = new + coefs[40 + row : 41 + row, :] * after
            new = new + coefs[80 + row : 81 + row, :] * before
            new = new + coefs[120 + row : 121 + row, :] * pltpu.roll(here, LANES - 1, 1)
            new = new + coefs[160 + row : 161 + row, :] * pltpu.roll(here, 1, 1)
            if turn == STEPS - 1:
                emit(row - STEPS, new)
            else:
                target[row * pitch : row * pitch + width, :] = new
            before = here
            here = after


def alpha_row(alpha, parity, row):
    parts = [alpha[pl.ds(m * 256 + parity * ROWS + row, HALF, stride=2 * ROWS), :] for m in range(2)]
    return jnp.concatenate(parts, axis=0)


def pack_body(alpha_in, loc_in, a_f, a_b, alpha, loc, sem):
    own = lax.axis_index("mem") % 2
    copies = [
        pltpu.make_async_copy(alpha_in, alpha, sem.at[0]),
        pltpu.make_async_copy(loc_in, loc, sem.at[1]),
    ]
    for copy in copies:
        copy.start()
    for copy in copies:
        copy.wait()
    pack_rows(lambda row: alpha_row(alpha, 1 - own, row), 16, a_f, a_b)
    for k in range(2):
        a_f[192 + k * 12 : 204 + k * 12, :] = loc[k * 16 + 4 : k * 16 + 16, :]
        a_b[192 + k * 12 : 204 + k * 12, :] = loc[k * 16 : k * 16 + 12, :]


def halo_loader(low, high, middle, width, base=0):
    def load(row):
        if row < STEPS:
            at = base + row * width
            return low[at : at + width, :]
        if row < STEPS + ROWS:
            return middle(row - STEPS)
        at = base + (row - STEPS - ROWS) * width
        return high[at : at + width, :]

    return load


def first_body(alpha, low, high, loc, perturb, ready, sums, coefs, raw, buf0, buf1, local):
    parity = 1 - lax.axis_index("mem") % 2
    build_coefs(
        low[192:204, :], loc[0:16, :], high[192:204, :],
        low[204:216, :], loc[16:32, :], high[204:216, :], raw, coefs,
    )

    def emit(row, value):
        local[pl.ds(row, 16, stride=ROWS), :] = value

    load = halo_loader(low, high, lambda row: alpha_row(alpha, parity, row), 16)
    diffuse(load, 16, 16, coefs, (buf0, buf1), emit)
    for s in range(HALF):
        level = 2 * s + parity
        for v in range(VARS):
            total = local[s * 16 : s * 16 + 16, :] * perturb[0, v, level].astype(jnp.float32)
            total = total + local[128 + s * 16 : 144 + s * 16, :] * perturb[1, v, level].astype(jnp.float32)
            sums[s, v] = total


def static_first_body(low, high, field, out, coefs, raw, buf0, buf1, result):
    build_coefs(
        low[pl.ds(6, 12, stride=16), :], field[96:112, :], high[pl.ds(6, 12, stride=16), :],
        low[pl.ds(7, 12, stride=16), :], field[112:128, :], high[pl.ds(7, 12, stride=16), :], raw, coefs,
    )

    def emit(row, value):
        result[pl.ds(row, 16, stride=ROWS), :] = value

    load = halo_loader(low, high, lambda row: field[pl.ds(row, 16, stride=ROWS), :], 16)
    diffuse(load, 16, 16, coefs, (buf0, buf1), emit)
    for j in range(2):
        out[j * 96 : j * 96 + 96, :] = result[j * 128 : j * 128 + 96, :]


def second_body(alpha, low, high, coefs, out, buf0, buf1):
    def emit(row, value):
        out[pl.ds(row, 16, stride=ROWS), :] = value

    parity = lax.axis_index("mem") % 2
    load = halo_loader(low, high, lambda row: alpha_row(alpha, parity, row), 16)
    diffuse(load, 16, 16, coefs, (buf0, buf1), emit)


def sum_body(local, perturb, received, o0, o1, o2, o3):
    _, y, parity = place()
    for k, out in enumerate((o0, o1, o2, o3)):
        for j in range(2):
            s = (y ^ k) + 4 * j
            level = 2 * s + parity
            first = local[pl.ds(pl.multiple_of(s * 16, 16), 16), :]
            other = local[pl.ds(pl.multiple_of(128 + s * 16, 16), 16), :]
            for v in range(VARS):
                total = first * perturb[0, v, level].astype(jnp.float32)
                total = total + other * perturb[1, v, level].astype(jnp.float32)
                total = total + received[s, v]
                out[j * 96 + v * 16 : j * 96 + v * 16 + 16, :] = total


def fetch_body(
    alpha_in, cell_in, mask_in, value, weight, static_ctl, static_coef,
    b_f, b_b, c_f, c_b, field, held, cell, mask, alpha, sem,
):
    _, y, c = place()
    first = pltpu.make_async_copy(alpha_in, alpha, sem.at[0])
    first.start()
    copies = [
        pltpu.make_async_copy(cell_in, cell, sem.at[1]),
        pltpu.make_async_copy(mask_in, mask, sem.at[2]),
        pltpu.make_async_copy(static_coef, field.at[96:128], sem.at[3]),
    ]
    for j in range(2):
        level = 2 * y + c + 8 * j
        for k, source in enumerate((weight, value)):
            spot = held.reshape(2, 2, VARS, 8, LANES).at[k, j]
            copies.append(pltpu.make_async_copy(source.at[:, level], spot, sem.at[4 + 3 * j + k]))
        spot = field.reshape(16, ROWS, LANES).at[8 * j : 8 * j + VARS]
        copies.append(pltpu.make_async_copy(static_ctl.at[:, level], spot, sem.at[6 + 3 * j]))
    for copy in copies:
        copy.start()
    field[224:256, :] = jnp.zeros((32, LANES), jnp.float32)
    first.wait()
    pack_rows(lambda row: alpha_row(alpha, c, row), 16, b_f, b_b)
    for copy in copies:
        copy.wait()
    pack_rows(lambda row: field[pl.ds(row, 16, stride=ROWS), :], 16, c_f, c_b)


def prepare_body(cell, mask, held, sums):
    pieces = []
    for a in range(8):
        part = held[pl.ds(a, 24, stride=8), :]
        scaled = part[0:12, :] * mask[a : a + 1, :].astype(jnp.float32)
        pieces.append(jnp.concatenate([scaled, scaled * part[12:24, :]], axis=0))
    both = jnp.concatenate(pieces, axis=1)
    top = both.astype(jnp.bfloat16)
    rest = both - top.astype(jnp.float32)
    mid = rest.astype(jnp.bfloat16)
    low = (rest - mid.astype(jnp.float32)).astype(jnp.bfloat16)
    stacked = jnp.concatenate([top, mid, low], axis=0)
    cells = jnp.concatenate([cell[a : a + 1, :] for a in range(8)], axis=1)
    for block in range(8):
        ids = block * 256 + lax.broadcasted_iota(jnp.int32, (256, 1024), 0)
        hit = jnp.where(ids == cells, 1.0, 0.0).astype(jnp.bfloat16)
        got = lax.dot_general(stacked, hit, (((1,), (1,)), ((), ())), preferred_element_type=jnp.float32)
        total = got[0:24, :] + got[24:48, :] + got[48:72, :]
        for r in range(2):
            sums[pl.ds(block * 2 + r, 24, stride=ROWS), :] = total[:, r * LANES : (r + 1) * LANES]


def gradient_body(mine, other, static, sums, grad):
    total = mine[...] + other[...] + static[...]
    grad[...] = sums[0:192, :] * total - sums[192:384, :]


def project(g, k, parity, perturb, middle):
    _, y, _ = place()
    for j in range(2):
        s = (y ^ k) + 4 * j
        level = 2 * s + parity
        fields = [g[j * 96 + v * 16 : j * 96 + v * 16 + 16, :] for v in range(VARS)]
        for m in range(2):
            total = perturb[m, 0, level].astype(jnp.float32) * fields[0]
            for v in range(1, VARS):
                total = total + perturb[m, v, level].astype(jnp.float32) * fields[v]
            middle[pl.ds(pl.multiple_of((m * HALF + s) * 16, 16), 16), :] = total


def project_own_body(g0, mate, g3, g1, g2, perturb, forward, backward, middle, rest, kept):
    x, _, c = place()
    kept[...] = mate[...]
    for k, g in enumerate((g0, g1, g2, g3)):
        project(g, k, c, perturb, middle)
        if k > 0:
            rest[(k - 1) * 192 : k * 192, :] = g[...]
    pack_rows(lambda row: middle[pl.ds(row, 16, stride=ROWS), :], 16, forward, backward)
    pack_rows(lambda row: g0[pl.ds(x * 96 + row, VARS, stride=ROWS), :], VARS, forward, backward, 192)


def project_other_body(g0, rest, perturb, forward, backward, middle):
    _, _, c = place()
    project(g0, 0, 1 - c, perturb, middle)
    for k in range(1, 4):
        project(rest.at[(k - 1) * 192 : k * 192], k, 1 - c, perturb, middle)
    pack_rows(lambda row: middle[pl.ds(row, 16, stride=ROWS), :], 16, forward, backward)


def update_alpha(parity, out, alpha, mom, stage0, stage1):
    for m in range(2):
        for s in range(HALF):
            at = pl.ds(pl.multiple_of(m * 256 + (2 * s + parity) * 16, 16), 16)
            here = slice((m * HALF + s) * 16, (m * HALF + s) * 16 + 16)
            old = alpha[at, :]
            moved = momentum_rate * mom[at, :] + (old + out[here, :])
            stage1[here, :] = moved
            stage0[here, :] = old - step_rate * moved


def third_body(low, high, middle, coefs, alpha, mom, after, stage0, stage1, buf0, buf1, out):
    def emit(row, value):
        out[pl.ds(row, 16, stride=ROWS), :] = value

    load = halo_loader(low, high, lambda row: middle[pl.ds(row, 16, stride=ROWS), :], 16)
    diffuse(load, 16, 16, coefs, (buf0, buf1), emit)
    update_alpha(lax.axis_index("mem") % 2, out, alpha, mom, stage0, stage1)


def static_last_body(low, high, grad, coefs, field, static_mom, after, new_static, new_static_mom, buf0, buf1, out):
    x, _, _ = place()
    load = halo_loader(low, high, lambda row: grad[pl.ds(x * 96 + row, VARS, stride=ROWS), :], VARS, 192)
    for row in range(SPAN):
        buf0[row * 8 : row * 8 + VARS, :] = load(row)

    def emit(row, value):
        out[pl.ds(row, 8, stride=ROWS), :] = value

    diffuse(lambda row: buf0[row * 8 : row * 8 + 8, :], 8, 8, coefs, (buf0, buf1), emit)
    old = field[pl.ds(pl.multiple_of(x * 128, 128), 96), :]
    moved = momentum_rate * static_mom[...] + (old + out[0:96, :])
    new_static_mom[...] = moved
    new_static[...] = old - step_rate * moved


def fourth_body(
    low, high, middle, coefs, alpha, mom, done0, done1, done2, done3,
    new_alpha, new_mom, new_static, new_static_mom,
    buf0, buf1, out, stage0, stage1, sem,
):
    c = lax.axis_index("mem") % 2

    def leave(source, target, parity, k):
        return pltpu.make_async_copy(source.reshape(2, HALF, ROWS, LANES), target.at[:, :, parity], sem.at[k])

    copies = [
        leave(done0, new_alpha, c, 0),
        leave(done1, new_mom, c, 1),
        pltpu.make_async_copy(done2, new_static, sem.at[2]),
        pltpu.make_async_copy(done3, new_static_mom, sem.at[3]),
    ]
    for copy in copies:
        copy.start()

    def emit(row, value):
        out[pl.ds(row, 16, stride=ROWS), :] = value

    load = halo_loader(low, high, lambda row: middle[pl.ds(row, 16, stride=ROWS), :], 16)
    diffuse(load, 16, 16, coefs, (buf0, buf1), emit)
    update_alpha(1 - c, out, alpha, mom, stage0, stage1)
    last = [leave(stage0, new_alpha, 1 - c, 4), leave(stage1, new_mom, 1 - c, 5)]
    for copy in last:
        copy.start()
    for copy in copies + last:
        copy.wait()


def local(
    perturb,
    alpha,
    alpha_mom,
    static_ctl,
    static_mom,
    loc_coef,
    static_coef,
    obs_cell,
    obs_mask,
    obs_value,
    obs_weight,
):
    tiles = lax.axis_size("tile")
    up = [(i, (i + 1) % tiles) for i in range(tiles)]
    down = [(target, source) for source, target in up]
    members = lax.axis_size("mem")

    def swap(value, bits):
        return lax.ppermute(value, "mem", [(i, i ^ bits) for i in range(members)])

    def halo(forward, backward):
        return lax.ppermute(forward, "tile", up), lax.ppermute(backward, "tile", down)

    mom2 = alpha_mom.reshape(512, LANES)
    bufs16 = [f32(SPAN * 16, LANES), f32(SPAN * 16, LANES)]
    raw = f32(88, LANES)

    alpha2 = alpha.reshape(512, LANES)
    loc2 = loc_coef.reshape(32, LANES)
    quarter = shape(192, LANES)
    half = shape(256, LANES)
    a_f, a_b = call(
        pack_body,
        "pack",
        [HBM] * 2,
        [shape(216, LANES)] * 2,
        [f32(512, LANES), f32(32, LANES), pltpu.SemaphoreType.DMA((2,))],
        grant=GRANT,
    )(alpha2, loc2)
    a_low, a_high = halo(a_f, a_b)
    ints = jax.ShapeDtypeStruct((8, LANES), jnp.int32)
    b_f, b_b, c_f, c_b, field, held, cell, mask = call(
        fetch_body,
        "fetch",
        [HBM] * 7,
        [quarter] * 4 + [half, quarter, ints, ints],
        [f32(512, LANES), pltpu.SemaphoreType.DMA((10,))],
        flops=BUSY,
        grant=GRANT2,
    )(
        alpha2,
        obs_cell.reshape(8, LANES),
        obs_mask.reshape(8, LANES),
        obs_value.reshape(VARS, 16, 8, LANES),
        obs_weight.reshape(VARS, 16, 8, LANES),
        static_ctl,
        static_coef.reshape(32, LANES),
    )
    b_low, b_high = halo(b_f, b_b)
    (sums,) = call(prepare_body, "prepare", [VM] * 3, [shape(384, LANES)], flops=BUSY)(cell, mask, held)

    part_a, loc_k = call(
        first_body,
        "first",
        [VM] * 6,
        [shape(HALF, VARS, ROWS, LANES), shape(200, LANES)],
        [raw] + bufs16 + [f32(256, LANES)],
        flops=BUSY,
    )(alpha2, a_low, a_high, loc2, perturb, sums)
    got = swap(part_a, 1)
    (second,) = call(second_body, "second", [VM] * 4, [half], bufs16, flops=BUSY)(alpha2, b_low, b_high, loc_k)
    o0, o1, o2, o3 = call(sum_body, "sum", [VM] * 3, [quarter] * 4)(second, perturb, got)
    r2, r1, r3 = swap(o2, 4), swap(o1, 2), swap(o3, 6)
    mine = o0 + r2 + r1 + r3
    other = swap(mine, 8)
    c_low, c_high = halo(*lax.optimization_barrier((c_f, c_b, o0))[:2])
    static, static_k = call(
        static_first_body,
        "static_first",
        [VM] * 3,
        [quarter, shape(200, LANES)],
        [raw] + bufs16 + [f32(256, LANES)],
        flops=BUSY,
    )(c_low, c_high, field)
    (grad,) = call(gradient_body, "gradient", [VM] * 4, [quarter])(mine, other, static, sums)
    g2, g1, g3 = swap(grad, 4), swap(grad, 2), swap(grad, 6)
    p0 = swap(grad, 1)
    p_f, p_b, p_m, rest, p0 = call(
        project_own_body,
        "project_own",
        [VM] * 6,
        [shape(264, LANES), shape(264, LANES), half, shape(576, LANES), quarter],
    )(grad, p0, g3, g1, g2, perturb)
    p_low, p_high = halo(p_f, p_b)
    rest = swap(rest, 1)
    q_f, q_b, q_m = call(project_other_body, "project_other", [VM] * 3, [quarter, quarter, half])(p0, rest, perturb)
    q_low, q_high = halo(q_f, q_b)
    whole = shape(2, HALF, 2, ROWS, LANES)
    work = bufs16 + [f32(256, LANES)]
    static_ready = call(static_last_body, "static_last", [VM] * 7, [shape(96, LANES)] * 2, work, flops=BUSY)(
        p_low, p_high, grad, static_k, field, static_mom.reshape(96, LANES), q_m
    )
    ready = call(third_body, "third", [VM] * 7, [half, half], work, flops=BUSY)(
        p_low, p_high, p_m, loc_k, alpha2, mom2, q_m
    )
    new_alpha, new_alpha_mom, new_static, new_static_mom = call(
        fourth_body,
        "fourth",
        [VM] * 10,
        [whole, whole, shape(96, LANES), shape(96, LANES)],
        bufs16 + [f32(256, LANES)] * 3 + [pltpu.SemaphoreType.DMA((6,))],
        out_specs=[HBM] * 4,
    )(q_low, q_high, q_m, loc_k, alpha2, mom2, *ready, *static_ready)
    return (
        new_alpha.reshape(alpha.shape),
        new_alpha_mom.reshape(alpha.shape),
        new_static.reshape(static_mom.shape),
        new_static_mom.reshape(static_mom.shape),
    )


def solution(mesh):
    return jax.shard_map(
        local,
        mesh=mesh,
        in_specs=(
            P("mem", None, None, "tile", None),
            P("mem", None, "tile", None),
            P("mem", None, "tile", None),
            P(None, None, "tile", None),
            P(None, "mem", "tile", None),
            P(None, "tile", None),
            P(None, "tile", None),
            P("tile", None),
            P("tile", None),
            P(None, None, "tile", None),
            P(None, None, "tile", None),
        ),
        out_specs=(
            P("mem", None, "tile", None),
            P("mem", None, "tile", None),
            P(None, "mem", "tile", None),
            P(None, "mem", "tile", None),
        ),
        check_vma=False,
    )
```

```python
import functools

import jax
import jax.numpy as jnp
from jax import lax
from jax.experimental import pallas as pl
from jax.experimental.pallas import tpu as pltpu
from jax.sharding import PartitionSpec as P

STEPS = 12
ROWS = 16
LANES = 128
SPAN = ROWS + 2 * STEPS
VARS = 6
HALF = 8

momentum_rate = 0.9
step_rate = 0.5

GRANT = 54.6
GRANT2 = 53.2
BUSY = 5000000000

VM = pl.BlockSpec(memory_space=pltpu.VMEM)
ANY = pl.BlockSpec(memory_space=pl.ANY)
HBM = pl.BlockSpec(memory_space=pltpu.HBM)


def shape(*dims):
    return jax.ShapeDtypeStruct(dims, jnp.float32)


def call(body, name, ins, outs, scratch=(), flops=1000000, out_specs=None, grant=32):
    return pl.pallas_call(
        body,
        name=name,
        in_specs=list(ins),
        out_specs=out_specs or [VM] * len(outs),
        out_shape=list(outs),
        scratch_shapes=list(scratch),
        compiler_params=pltpu.CompilerParams(vmem_limit_bytes=int(grant * 1024 * 1024)),
        cost_estimate=pl.CostEstimate(flops=flops, bytes_accessed=1000000, transcendentals=0),
    )


def f32(*dims):
    return pltpu.VMEM(dims, jnp.float32)


def place():
    mem = lax.axis_index("mem")
    return mem // 8, (mem // 2) % 4, mem % 2


def pack_rows(load, width, forward, backward, base=0):
    for row in range(ROWS):
        value = load(row)
        if row >= ROWS - STEPS:
            at = base + (row - (ROWS - STEPS)) * width
            forward[at : at + width, :] = value
        if row < STEPS:
            at = base + row * width
            backward[at : at + width, :] = value


def build_coefs(low_x, mid_x, high_x, low_y, mid_y, high_y, raw, coefs):
    raw[0:8, :] = jnp.zeros((8, LANES), jnp.float32)
    raw[8:20, :] = low_x
    raw[20:36, :] = mid_x
    raw[36:48, :] = high_x
    raw[48:60, :] = low_y
    raw[60:76, :] = mid_y
    raw[76:88, :] = high_y
    extent = ROWS * lax.axis_size("tile")
    first = lax.axis_index("tile") * ROWS - STEPS
    at = first + lax.broadcasted_iota(jnp.int32, (SPAN, LANES), 0)
    lane = lax.broadcasted_iota(jnp.int32, (SPAN, LANES), 1)
    valid = (at >= 0) & (at < extent)
    below = jnp.where(valid, raw[8:48, :], 0.0)
    raw[8:48, :] = below
    above = jnp.where(valid, raw[7:47, :], 0.0)
    right = jnp.where(valid, raw[48:88, :], 0.0)
    left = jnp.where(lane > 0, pltpu.roll(right, 1, 1), 0.0)
    centre = 1.0 - below - above - right - left
    coefs[0:40, :] = jnp.where(valid, centre, 0.0)
    coefs[40:80, :] = jnp.where(at + 1 < extent, below, 0.0)
    coefs[80:120, :] = above
    coefs[120:160, :] = jnp.where(lane < LANES - 1, right, 0.0)
    coefs[160:200, :] = left


def diffuse(load, width, pitch, coefs, bufs, emit):
    for turn in range(STEPS):
        source = bufs[turn % 2]
        target = bufs[(turn + 1) % 2]
        if turn == 0:
            take = load
        else:
            take = lambda row: source[row * pitch : row * pitch + width, :]
        before = take(turn)
        here = take(turn + 1)
        for row in range(turn + 1, SPAN - 1 - turn):
            after = take(row + 1)
            new = coefs[row : row + 1, :] * here
            new = new + coefs[40 + row : 41 + row, :] * after
            new = new + coefs[80 + row : 81 + row, :] * before
            new = new + coefs[120 + row : 121 + row, :] * pltpu.roll(here, LANES - 1, 1)
            new = new + coefs[160 + row : 161 + row, :] * pltpu.roll(here, 1, 1)
            if turn == STEPS - 1:
                emit(row - STEPS, new)
            else:
                target[row * pitch : row * pitch + width, :] = new
            before = here
            here = after


def alpha_row(alpha, parity, row):
    parts = [alpha[pl.ds(m * 256 + parity * ROWS + row, HALF, stride=2 * ROWS), :] for m in range(2)]
    return jnp.concatenate(parts, axis=0)


def pack_body(alpha_in, loc_in, a_f, a_b, alpha, loc, sem):
    own = lax.axis_index("mem") % 2
    copies = [
        pltpu.make_async_copy(alpha_in, alpha, sem.at[0]),
        pltpu.make_async_copy(loc_in, loc, sem.at[1]),
    ]
    for copy in copies:
        copy.start()
    for copy in copies:
        copy.wait()
    pack_rows(lambda row: alpha_row(alpha, 1 - own, row), 16, a_f, a_b)
    for k in range(2):
        a_f[192 + k * 12 : 204 + k * 12, :] = loc[k * 16 + 4 : k * 16 + 16, :]
        a_b[192 + k * 12 : 204 + k * 12, :] = loc[k * 16 : k * 16 + 12, :]


def halo_loader(low, high, middle, width, base=0):
    def load(row):
        if row < STEPS:
            at = base + row * width
            return low[at : at + width, :]
        if row < STEPS + ROWS:
            return middle(row - STEPS)
        at = base + (row - STEPS - ROWS) * width
        return high[at : at + width, :]

    return load


def first_body(alpha, low, high, loc, perturb, ready, sums, coefs, raw, buf0, buf1, local):
    parity = 1 - lax.axis_index("mem") % 2
    build_coefs(
        low[192:204, :], loc[0:16, :], high[192:204, :],
        low[204:216, :], loc[16:32, :], high[204:216, :], raw, coefs,
    )

    def emit(row, value):
        local[pl.ds(row, 16, stride=ROWS), :] = value

    load = halo_loader(low, high, lambda row: alpha_row(alpha, parity, row), 16)
    diffuse(load, 16, 16, coefs, (buf0, buf1), emit)
    for s in range(HALF):
        level = 2 * s + parity
        for v in range(VARS):
            total = local[s * 16 : s * 16 + 16, :] * perturb[0, v, level].astype(jnp.float32)
            total = total + local[128 + s * 16 : 144 + s * 16, :] * perturb[1, v, level].astype(jnp.float32)
            sums[s, v] = total


def static_first_body(low, high, field, out, coefs, raw, buf0, buf1, result):
    build_coefs(
        low[pl.ds(6, 12, stride=16), :], field[96:112, :], high[pl.ds(6, 12, stride=16), :],
        low[pl.ds(7, 12, stride=16), :], field[112:128, :], high[pl.ds(7, 12, stride=16), :], raw, coefs,
    )

    def emit(row, value):
        result[pl.ds(row, 16, stride=ROWS), :] = value

    load = halo_loader(low, high, lambda row: field[pl.ds(row, 16, stride=ROWS), :], 16)
    diffuse(load, 16, 16, coefs, (buf0, buf1), emit)
    for j in range(2):
        out[j * 96 : j * 96 + 96, :] = result[j * 128 : j * 128 + 96, :]


def second_body(alpha, low, high, coefs, out, buf0, buf1):
    def emit(row, value):
        out[pl.ds(row, 16, stride=ROWS), :] = value

    parity = lax.axis_index("mem") % 2
    load = halo_loader(low, high, lambda row: alpha_row(alpha, parity, row), 16)
    diffuse(load, 16, 16, coefs, (buf0, buf1), emit)


def sum_body(local, perturb, received, o0, o1, o2, o3):
    _, y, parity = place()
    for k, out in enumerate((o0, o1, o2, o3)):
        for j in range(2):
            s = (y ^ k) + 4 * j
            level = 2 * s + parity
            first = local[pl.ds(pl.multiple_of(s * 16, 16), 16), :]
            other = local[pl.ds(pl.multiple_of(128 + s * 16, 16), 16), :]
            for v in range(VARS):
                total = first * perturb[0, v, level].astype(jnp.float32)
                total = total + other * perturb[1, v, level].astype(jnp.float32)
                total = total + received[s, v]
                out[j * 96 + v * 16 : j * 96 + v * 16 + 16, :] = total


def fetch_body(
    alpha_in, cell_in, mask_in, value, weight, static_ctl, static_coef,
    b_f, b_b, c_f, c_b, field, held, cell, mask, alpha, sem,
):
    _, y, c = place()
    first = pltpu.make_async_copy(alpha_in, alpha, sem.at[0])
    first.start()
    copies = [
        pltpu.make_async_copy(cell_in, cell, sem.at[1]),
        pltpu.make_async_copy(mask_in, mask, sem.at[2]),
        pltpu.make_async_copy(static_coef, field.at[96:128], sem.at[3]),
    ]
    for j in range(2):
        level = 2 * y + c + 8 * j
        for k, source in enumerate((weight, value)):
            spot = held.reshape(2, 2, VARS, 8, LANES).at[k, j]
            copies.append(pltpu.make_async_copy(source.at[:, level], spot, sem.at[4 + 3 * j + k]))
        spot = field.reshape(16, ROWS, LANES).at[8 * j : 8 * j + VARS]
        copies.append(pltpu.make_async_copy(static_ctl.at[:, level], spot, sem.at[6 + 3 * j]))
    for copy in copies:
        copy.start()
    field[224:256, :] = jnp.zeros((32, LANES), jnp.float32)
    first.wait()
    pack_rows(lambda row: alpha_row(alpha, c, row), 16, b_f, b_b)
    for copy in copies:
        copy.wait()
    pack_rows(lambda row: field[pl.ds(row, 16, stride=ROWS), :], 16, c_f, c_b)


def prepare_body(cell, mask, held, sums):
    pieces = []
    for a in range(8):
        part = held[pl.ds(a, 24, stride=8), :]
        scaled = part[0:12, :] * mask[a : a + 1, :].astype(jnp.float32)
        pieces.append(jnp.concatenate([scaled, scaled * part[12:24, :]], axis=0))
    both = jnp.concatenate(pieces, axis=1)
    top = both.astype(jnp.bfloat16)
    rest = both - top.astype(jnp.float32)
    mid = rest.astype(jnp.bfloat16)
    low = (rest - mid.astype(jnp.float32)).astype(jnp.bfloat16)
    stacked = jnp.concatenate([top, mid, low], axis=0)
    cells = jnp.concatenate([cell[a : a + 1, :] for a in range(8)], axis=1)
    for block in range(8):
        ids = block * 256 + lax.broadcasted_iota(jnp.int32, (256, 1024), 0)
        hit = jnp.where(ids == cells, 1.0, 0.0).astype(jnp.bfloat16)
        got = lax.dot_general(stacked, hit, (((1,), (1,)), ((), ())), preferred_element_type=jnp.float32)
        total = got[0:24, :] + got[24:48, :] + got[48:72, :]
        for r in range(2):
            sums[pl.ds(block * 2 + r, 24, stride=ROWS), :] = total[:, r * LANES : (r + 1) * LANES]


def project(g, k, parity, perturb, middle):
    _, y, _ = place()
    for j in range(2):
        level = 2 * ((y ^ k) + 4 * j) + parity
        fields = [g[j * 96 + v * 16 : j * 96 + v * 16 + 16, :] for v in range(VARS)]
        for m in range(2):
            total = perturb[m, 0, level].astype(jnp.float32) * fields[0]
            for v in range(1, VARS):
                total = total + perturb[m, v, level].astype(jnp.float32) * fields[v]
            at = (k * 4 + m * 2 + j) * 16
            middle[at : at + 16, :] = total


def gradient_body(mine, other, static, sums, perturb, grad, forward, backward, middle):
    x, _, c = place()
    total = mine[...] + other[...] + static[...]
    grad[...] = sums[0:192, :] * total - sums[192:384, :]
    project(grad, 0, c, perturb, middle)
    pack_rows(lambda row: grad[pl.ds(x * 96 + row, VARS, stride=ROWS), :], VARS, forward, backward)
    pack_rows(lambda row: middle[pl.ds(row, 4, stride=ROWS), :], 4, forward, backward, 72)


def project_own_body(g0, g3, g1, g2, perturb, start, low, high, forward, backward, middle, rest, low_out, high_out):
    c = lax.axis_index("mem") % 2
    low_out[...] = low[...]
    high_out[...] = high[...]
    middle[0:64, :] = start[...]
    rest[0:192, :] = g0[...]
    for k, g in ((1, g1), (2, g2), (3, g3)):
        project(g, k, c, perturb, middle)
        rest[k * 192 : k * 192 + 192, :] = g[...]
    pack_rows(lambda row: middle[pl.ds(64 + row, 12, stride=ROWS), :], 12, forward, backward)


def project_other_body(rest, perturb, forward, backward, middle):
    c = lax.axis_index("mem") % 2
    for k in range(4):
        project(rest.at[k * 192 : k * 192 + 192], k, 1 - c, perturb, middle)
    pack_rows(lambda row: middle[pl.ds(row, 16, stride=ROWS), :], 16, forward, backward)


def update_alpha(parity, out, alpha, mom, stage0, stage1):
    _, y, _ = place()
    for k in range(4):
        for m in range(2):
            for j in range(2):
                t = (k * 4 + m * 2 + j) * 16
                s = (y ^ k) + 4 * j
                at = pl.ds(pl.multiple_of(m * 256 + (2 * s + parity) * 16, 16), 16)
                here = pl.ds(pl.multiple_of((m * HALF + s) * 16, 16), 16)
                old = alpha[at, :]
                moved = momentum_rate * mom[at, :] + (old + out[t : t + 16, :])
                stage1[here, :] = moved
                stage0[here, :] = old - step_rate * moved


def third_body(
    early_low, early_high, low, high, middle, coefs, alpha, mom, after, stage0, stage1, buf0, buf1, out,
):
    for row in range(SPAN):
        at = row * 16
        if STEPS <= row < STEPS + ROWS:
            buf0[at : at + 16, :] = middle[pl.ds(row - STEPS, 16, stride=ROWS), :]
        else:
            near, far, k = (early_low, low, row) if row < STEPS else (early_high, high, row - STEPS - ROWS)
            buf0[at : at + 4, :] = near[72 + k * 4 : 76 + k * 4, :]
            buf0[at + 4 : at + 16, :] = far[k * 12 : k * 12 + 12, :]

    def emit(row, value):
        out[pl.ds(row, 16, stride=ROWS), :] = value

    diffuse(lambda row: buf0[row * 16 : row * 16 + 16, :], 16, 16, coefs, (buf0, buf1), emit)
    update_alpha(lax.axis_index("mem") % 2, out, alpha, mom, stage0, stage1)


def static_last_body(low, high, grad, coefs, field, static_mom, after, new_static, new_static_mom, buf0, buf1, out):
    x, _, _ = place()
    load = halo_loader(low, high, lambda row: grad[pl.ds(x * 96 + row, VARS, stride=ROWS), :], VARS)
    for row in range(SPAN):
        buf0[row * 8 : row * 8 + VARS, :] = load(row)

    def emit(row, value):
        out[pl.ds(row, 8, stride=ROWS), :] = value

    diffuse(lambda row: buf0[row * 8 : row * 8 + 8, :], 8, 8, coefs, (buf0, buf1), emit)
    old = field[pl.ds(pl.multiple_of(x * 128, 128), 96), :]
    moved = momentum_rate * static_mom[...] + (old + out[0:96, :])
    new_static_mom[...] = moved
    new_static[...] = old - step_rate * moved


def fourth_body(
    low, high, middle, coefs, alpha, mom, done0, done1, done2, done3,
    new_alpha, new_mom, new_static, new_static_mom,
    buf0, buf1, out, stage0, stage1, sem,
):
    c = lax.axis_index("mem") % 2

    def leave(source, target, parity, k):
        return pltpu.make_async_copy(source.reshape(2, HALF, ROWS, LANES), target.at[:, :, parity], sem.at[k])

    copies = [
        leave(done0, new_alpha, c, 0),
        leave(done1, new_mom, c, 1),
        pltpu.make_async_copy(done2, new_static, sem.at[2]),
        pltpu.make_async_copy(done3, new_static_mom, sem.at[3]),
    ]
    for copy in copies:
        copy.start()

    def emit(row, value):
        out[pl.ds(row, 16, stride=ROWS), :] = value

    load = halo_loader(low, high, lambda row: middle[pl.ds(row, 16, stride=ROWS), :], 16)
    diffuse(load, 16, 16, coefs, (buf0, buf1), emit)
    update_alpha(1 - c, out, alpha, mom, stage0, stage1)
    last = [leave(stage0, new_alpha, 1 - c, 4), leave(stage1, new_mom, 1 - c, 5)]
    for copy in last:
        copy.start()
    for copy in copies + last:
        copy.wait()


def local(
    perturb,
    alpha,
    alpha_mom,
    static_ctl,
    static_mom,
    loc_coef,
    static_coef,
    obs_cell,
    obs_mask,
    obs_value,
    obs_weight,
):
    tiles = lax.axis_size("tile")
    up = [(i, (i + 1) % tiles) for i in range(tiles)]
    down = [(target, source) for source, target in up]
    members = lax.axis_size("mem")

    def swap(value, bits):
        return lax.ppermute(value, "mem", [(i, i ^ bits) for i in range(members)])

    def halo(forward, backward):
        return lax.ppermute(forward, "tile", up), lax.ppermute(backward, "tile", down)

    mom2 = alpha_mom.reshape(512, LANES)
    bufs16 = [f32(SPAN * 16, LANES), f32(SPAN * 16, LANES)]
    raw = f32(88, LANES)

    alpha2 = alpha.reshape(512, LANES)
    loc2 = loc_coef.reshape(32, LANES)
    quarter = shape(192, LANES)
    half = shape(256, LANES)
    a_f, a_b = call(
        pack_body,
        "pack",
        [HBM] * 2,
        [shape(216, LANES)] * 2,
        [f32(512, LANES), f32(32, LANES), pltpu.SemaphoreType.DMA((2,))],
        grant=GRANT,
    )(alpha2, loc2)
    a_low, a_high = halo(a_f, a_b)
    ints = jax.ShapeDtypeStruct((8, LANES), jnp.int32)
    b_f, b_b, c_f, c_b, field, held, cell, mask = call(
        fetch_body,
        "fetch",
        [HBM] * 7,
        [quarter] * 4 + [half, quarter, ints, ints],
        [f32(512, LANES), pltpu.SemaphoreType.DMA((10,))],
        flops=BUSY,
        grant=GRANT2,
    )(
        alpha2,
        obs_cell.reshape(8, LANES),
        obs_mask.reshape(8, LANES),
        obs_value.reshape(VARS, 16, 8, LANES),
        obs_weight.reshape(VARS, 16, 8, LANES),
        static_ctl,
        static_coef.reshape(32, LANES),
    )
    b_low, b_high = halo(b_f, b_b)
    (sums,) = call(prepare_body, "prepare", [VM] * 3, [shape(384, LANES)], flops=BUSY)(cell, mask, held)

    part_a, loc_k = call(
        first_body,
        "first",
        [VM] * 6,
        [shape(HALF, VARS, ROWS, LANES), shape(200, LANES)],
        [raw] + bufs16 + [f32(256, LANES)],
        flops=BUSY,
    )(alpha2, a_low, a_high, loc2, perturb, sums)
    got = swap(part_a, 1)
    (second,) = call(second_body, "second", [VM] * 4, [half], bufs16, flops=BUSY)(alpha2, b_low, b_high, loc_k)
    o0, o1, o2, o3 = call(sum_body, "sum", [VM] * 3, [quarter] * 4)(second, perturb, got)
    r2, r1, r3 = swap(o2, 4), swap(o1, 2), swap(o3, 6)
    mine = o0 + r2 + r1 + r3
    other = swap(mine, 8)
    c_low, c_high = halo(*lax.optimization_barrier((c_f, c_b, o0))[:2])
    static, static_k = call(
        static_first_body,
        "static_first",
        [VM] * 3,
        [quarter, shape(200, LANES)],
        [raw] + bufs16 + [f32(256, LANES)],
        flops=BUSY,
    )(c_low, c_high, field)
    early = shape(120, LANES)
    grad, g_f, g_b, start = call(
        gradient_body, "gradient", [VM] * 5, [quarter, early, early, shape(64, LANES)]
    )(mine, other, static, sums, perturb)
    g2, g1, g3 = swap(grad, 4), swap(grad, 2), swap(grad, 6)
    g_low, g_high = halo(g_f, g_b)
    far = shape(144, LANES)
    p_f, p_b, p_m, rest, g_low, g_high = call(
        project_own_body,
        "project_own",
        [VM] * 8,
        [far, far, half, shape(768, LANES), early, early],
    )(grad, g3, g1, g2, perturb, start, g_low, g_high)
    p_low, p_high = halo(p_f, p_b)
    rest = swap(rest, 1)
    q_f, q_b, q_m = call(project_other_body, "project_other", [VM] * 2, [quarter, quarter, half])(rest, perturb)
    q_low, q_high = halo(q_f, q_b)
    whole = shape(2, HALF, 2, ROWS, LANES)
    work = bufs16 + [f32(256, LANES)]
    static_ready = call(static_last_body, "static_last", [VM] * 7, [shape(96, LANES)] * 2, work, flops=BUSY)(
        g_low, g_high, grad, static_k, field, static_mom.reshape(96, LANES), q_m
    )
    ready = call(third_body, "third", [VM] * 9, [half, half], work, flops=BUSY)(
        g_low, g_high, p_low, p_high, p_m, loc_k, alpha2, mom2, q_m
    )
    new_alpha, new_alpha_mom, new_static, new_static_mom = call(
        fourth_body,
        "fourth",
        [VM] * 10,
        [whole, whole, shape(96, LANES), shape(96, LANES)],
        bufs16 + [f32(256, LANES)] * 3 + [pltpu.SemaphoreType.DMA((6,))],
        out_specs=[HBM] * 4,
    )(q_low, q_high, q_m, loc_k, alpha2, mom2, *ready, *static_ready)
    return (
        new_alpha.reshape(alpha.shape),
        new_alpha_mom.reshape(alpha.shape),
        new_static.reshape(static_mom.shape),
        new_static_mom.reshape(static_mom.shape),
    )


def solution(mesh):
    return jax.shard_map(
        local,
        mesh=mesh,
        in_specs=(
            P("mem", None, None, "tile", None),
            P("mem", None, "tile", None),
            P("mem", None, "tile", None),
            P(None, None, "tile", None),
            P(None, "mem", "tile", None),
            P(None, "tile", None),
            P(None, "tile", None),
            P("tile", None),
            P("tile", None),
            P(None, None, "tile", None),
            P(None, None, "tile", None),
        ),
        out_specs=(
            P("mem", None, "tile", None),
            P("mem", None, "tile", None),
            P(None, "mem", "tile", None),
            P(None, "mem", "tile", None),
        ),
        check_vma=False,
    )
```

```python
import functools

import jax
import jax.numpy as jnp
from jax import lax
from jax.experimental import pallas as pl
from jax.experimental.pallas import tpu as pltpu
from jax.sharding import PartitionSpec as P

STEPS = 12
ROWS = 16
LANES = 128
SPAN = ROWS + 2 * STEPS
VARS = 6
HALF = 8

momentum_rate = 0.9
step_rate = 0.5

GRANT = 54.6
GRANT2 = 53.2
BUSY = 5000000000

VM = pl.BlockSpec(memory_space=pltpu.VMEM)
ANY = pl.BlockSpec(memory_space=pl.ANY)
HBM = pl.BlockSpec(memory_space=pltpu.HBM)


def shape(*dims):
    return jax.ShapeDtypeStruct(dims, jnp.float32)


def call(body, name, ins, outs, scratch=(), flops=1000000, out_specs=None, grant=32):
    return pl.pallas_call(
        body,
        name=name,
        in_specs=list(ins),
        out_specs=out_specs or [VM] * len(outs),
        out_shape=list(outs),
        scratch_shapes=list(scratch),
        compiler_params=pltpu.CompilerParams(vmem_limit_bytes=int(grant * 1024 * 1024)),
        cost_estimate=pl.CostEstimate(flops=flops, bytes_accessed=1000000, transcendentals=0),
    )


def f32(*dims):
    return pltpu.VMEM(dims, jnp.float32)


def place():
    mem = lax.axis_index("mem")
    return mem // 8, (mem // 2) % 4, mem % 2


def pack_rows(load, width, forward, backward, base=0):
    for row in range(ROWS):
        value = load(row)
        if row >= ROWS - STEPS:
            at = base + (row - (ROWS - STEPS)) * width
            forward[at : at + width, :] = value
        if row < STEPS:
            at = base + row * width
            backward[at : at + width, :] = value


def build_coefs(low_x, mid_x, high_x, low_y, mid_y, high_y, raw, coefs):
    raw[0:8, :] = jnp.zeros((8, LANES), jnp.float32)
    raw[8:20, :] = low_x
    raw[20:36, :] = mid_x
    raw[36:48, :] = high_x
    raw[48:60, :] = low_y
    raw[60:76, :] = mid_y
    raw[76:88, :] = high_y
    extent = ROWS * lax.axis_size("tile")
    first = lax.axis_index("tile") * ROWS - STEPS
    at = first + lax.broadcasted_iota(jnp.int32, (SPAN, LANES), 0)
    lane = lax.broadcasted_iota(jnp.int32, (SPAN, LANES), 1)
    valid = (at >= 0) & (at < extent)
    below = jnp.where(valid, raw[8:48, :], 0.0)
    raw[8:48, :] = below
    above = jnp.where(valid, raw[7:47, :], 0.0)
    right = jnp.where(valid, raw[48:88, :], 0.0)
    left = jnp.where(lane > 0, pltpu.roll(right, 1, 1), 0.0)
    centre = 1.0 - below - above - right - left
    coefs[0:40, :] = jnp.where(valid, centre, 0.0)
    coefs[40:80, :] = jnp.where(at + 1 < extent, below, 0.0)
    coefs[80:120, :] = above
    coefs[120:160, :] = jnp.where(lane < LANES - 1, right, 0.0)
    coefs[160:200, :] = left


def diffuse(load, width, pitch, coefs, bufs, emit):
    for turn in range(STEPS):
        source = bufs[turn % 2]
        target = bufs[(turn + 1) % 2]
        if turn == 0:
            take = load
        else:
            take = lambda row: source[row * pitch : row * pitch + width, :]
        before = take(turn)
        here = take(turn + 1)
        for row in range(turn + 1, SPAN - 1 - turn):
            after = take(row + 1)
            new = coefs[row : row + 1, :] * here
            new = new + coefs[40 + row : 41 + row, :] * after
            new = new + coefs[80 + row : 81 + row, :] * before
            new = new + coefs[120 + row : 121 + row, :] * pltpu.roll(here, LANES - 1, 1)
            new = new + coefs[160 + row : 161 + row, :] * pltpu.roll(here, 1, 1)
            if turn == STEPS - 1:
                emit(row - STEPS, new)
            else:
                target[row * pitch : row * pitch + width, :] = new
            before = here
            here = after


def alpha_row(alpha, parity, row):
    parts = [alpha[pl.ds(m * 256 + parity * ROWS + row, HALF, stride=2 * ROWS), :] for m in range(2)]
    return jnp.concatenate(parts, axis=0)


def pack_body(alpha_in, loc_in, a_f, a_b, alpha, loc, sem):
    own = lax.axis_index("mem") % 2
    copies = [
        pltpu.make_async_copy(alpha_in, alpha, sem.at[0]),
        pltpu.make_async_copy(loc_in, loc, sem.at[1]),
    ]
    for copy in copies:
        copy.start()
    for copy in copies:
        copy.wait()
    pack_rows(lambda row: alpha_row(alpha, 1 - own, row), 16, a_f, a_b)
    for k in range(2):
        a_f[192 + k * 12 : 204 + k * 12, :] = loc[k * 16 + 4 : k * 16 + 16, :]
        a_b[192 + k * 12 : 204 + k * 12, :] = loc[k * 16 : k * 16 + 12, :]


def halo_loader(low, high, middle, width, base=0):
    def load(row):
        if row < STEPS:
            at = base + row * width
            return low[at : at + width, :]
        if row < STEPS + ROWS:
            return middle(row - STEPS)
        at = base + (row - STEPS - ROWS) * width
        return high[at : at + width, :]

    return load


def first_body(alpha, low, high, loc, perturb, ready, sums, coefs, raw, buf0, buf1, local):
    parity = 1 - lax.axis_index("mem") % 2
    build_coefs(
        low[192:204, :], loc[0:16, :], high[192:204, :],
        low[204:216, :], loc[16:32, :], high[204:216, :], raw, coefs,
    )

    def emit(row, value):
        local[pl.ds(row, 16, stride=ROWS), :] = value

    load = halo_loader(low, high, lambda row: alpha_row(alpha, parity, row), 16)
    diffuse(load, 16, 16, coefs, (buf0, buf1), emit)
    for s in range(HALF):
        level = 2 * s + parity
        for v in range(VARS):
            total = local[s * 16 : s * 16 + 16, :] * perturb[0, v, level].astype(jnp.float32)
            total = total + local[128 + s * 16 : 144 + s * 16, :] * perturb[1, v, level].astype(jnp.float32)
            sums[s, v] = total


def static_first_body(low, high, field, out, coefs, raw, buf0, buf1, result):
    build_coefs(
        low[pl.ds(6, 12, stride=16), :], field[96:112, :], high[pl.ds(6, 12, stride=16), :],
        low[pl.ds(7, 12, stride=16), :], field[112:128, :], high[pl.ds(7, 12, stride=16), :], raw, coefs,
    )

    def emit(row, value):
        result[pl.ds(row, 16, stride=ROWS), :] = value

    load = halo_loader(low, high, lambda row: field[pl.ds(row, 16, stride=ROWS), :], 16)
    diffuse(load, 16, 16, coefs, (buf0, buf1), emit)
    for j in range(2):
        out[j * 96 : j * 96 + 96, :] = result[j * 128 : j * 128 + 96, :]


def second_body(alpha, low, high, coefs, out, buf0, buf1):
    def emit(row, value):
        out[pl.ds(row, 16, stride=ROWS), :] = value

    parity = lax.axis_index("mem") % 2
    load = halo_loader(low, high, lambda row: alpha_row(alpha, parity, row), 16)
    diffuse(load, 16, 16, coefs, (buf0, buf1), emit)


def sum_body(local, perturb, received, o0, o1, o2, o3):
    _, y, parity = place()
    for k, out in enumerate((o0, o1, o2, o3)):
        for j in range(2):
            s = (y ^ k) + 4 * j
            level = 2 * s + parity
            first = local[pl.ds(pl.multiple_of(s * 16, 16), 16), :]
            other = local[pl.ds(pl.multiple_of(128 + s * 16, 16), 16), :]
            for v in range(VARS):
                total = first * perturb[0, v, level].astype(jnp.float32)
                total = total + other * perturb[1, v, level].astype(jnp.float32)
                total = total + received[s, v]
                out[j * 96 + v * 16 : j * 96 + v * 16 + 16, :] = total


def fetch_body(
    alpha_in, value, weight, static_ctl, static_coef, b_f, b_b, c_f, c_b, field, held, alpha, sem,
):
    _, y, c = place()
    first = pltpu.make_async_copy(alpha_in, alpha, sem.at[0])
    first.start()
    copies = [
        pltpu.make_async_copy(static_coef, field.at[96:128], sem.at[1]),
    ]
    for j in range(2):
        level = 2 * y + c + 8 * j
        for k, source in enumerate((weight, value)):
            spot = held.reshape(2, 2, VARS, 8, LANES).at[k, j]
            copies.append(pltpu.make_async_copy(source.at[:, level], spot, sem.at[2 + 3 * j + k]))
        spot = field.reshape(16, ROWS, LANES).at[8 * j : 8 * j + VARS]
        copies.append(pltpu.make_async_copy(static_ctl.at[:, level], spot, sem.at[4 + 3 * j]))
    for copy in copies:
        copy.start()
    field[224:256, :] = jnp.zeros((32, LANES), jnp.float32)
    first.wait()
    pack_rows(lambda row: alpha_row(alpha, c, row), 16, b_f, b_b)
    for copy in copies:
        copy.wait()
    pack_rows(lambda row: field[pl.ds(row, 16, stride=ROWS), :], 16, c_f, c_b)


def prepare_body(cell, mask, held, sums):
    pieces = []
    for a in range(8):
        part = held[pl.ds(a, 24, stride=8), :]
        scaled = part[0:12, :] * mask[a : a + 1, :].astype(jnp.float32)
        pieces.append(jnp.concatenate([scaled, scaled * part[12:24, :]], axis=0))
    both = jnp.concatenate(pieces, axis=1)
    top = both.astype(jnp.bfloat16)
    rest = both - top.astype(jnp.float32)
    mid = rest.astype(jnp.bfloat16)
    low = (rest - mid.astype(jnp.float32)).astype(jnp.bfloat16)
    stacked = jnp.concatenate([top, mid, low], axis=0)
    cells = jnp.concatenate([cell[a : a + 1, :] for a in range(8)], axis=1)
    for block in range(8):
        ids = block * 256 + lax.broadcasted_iota(jnp.int32, (256, 1024), 0)
        hit = jnp.where(ids == cells, 1.0, 0.0).astype(jnp.bfloat16)
        got = lax.dot_general(stacked, hit, (((1,), (1,)), ((), ())), preferred_element_type=jnp.float32)
        total = got[0:24, :] + got[24:48, :] + got[48:72, :]
        for r in range(2):
            sums[pl.ds(block * 2 + r, 24, stride=ROWS), :] = total[:, r * LANES : (r + 1) * LANES]


def project(g, k, parity, perturb, middle):
    _, y, _ = place()
    for j in range(2):
        level = 2 * ((y ^ k) + 4 * j) + parity
        fields = [g[j * 96 + v * 16 : j * 96 + v * 16 + 16, :] for v in range(VARS)]
        for m in range(2):
            total = perturb[m, 0, level].astype(jnp.float32) * fields[0]
            for v in range(1, VARS):
                total = total + perturb[m, v, level].astype(jnp.float32) * fields[v]
            at = (k * 4 + m * 2 + j) * 16
            middle[at : at + 16, :] = total


def gradient_body(mine, other, static, sums, perturb, grad, forward, backward, middle):
    x, _, c = place()
    total = mine[...] + other[...] + static[...]
    grad[...] = sums[0:192, :] * total - sums[192:384, :]
    project(grad, 0, c, perturb, middle)
    pack_rows(lambda row: grad[pl.ds(x * 96 + row, VARS, stride=ROWS), :], VARS, forward, backward)
    pack_rows(lambda row: middle[pl.ds(row, 4, stride=ROWS), :], 4, forward, backward, 72)


def join_body(g3, g1, g2, g0, out):
    for k, g in enumerate((g0, g1, g2, g3)):
        out[k * 192 : k * 192 + 192, :] = g[...]


def project_own_body(g3, g1, g2, perturb, start, low, high, forward, backward, middle, low_out, high_out):
    c = lax.axis_index("mem") % 2
    low_out[...] = low[...]
    high_out[...] = high[...]
    middle[0:64, :] = start[...]
    for k, g in ((1, g1), (2, g2), (3, g3)):
        project(g, k, c, perturb, middle)
    pack_rows(lambda row: middle[pl.ds(64 + row, 12, stride=ROWS), :], 12, forward, backward)


def project_other_body(rest, perturb, forward, backward, middle):
    c = lax.axis_index("mem") % 2
    for k in range(4):
        project(rest.at[k * 192 : k * 192 + 192], k, 1 - c, perturb, middle)
    pack_rows(lambda row: middle[pl.ds(row, 16, stride=ROWS), :], 16, forward, backward)


def update_alpha(parity, out, alpha, mom, stage0, stage1):
    _, y, _ = place()
    for k in range(4):
        for m in range(2):
            for j in range(2):
                t = (k * 4 + m * 2 + j) * 16
                s = (y ^ k) + 4 * j
                at = pl.ds(pl.multiple_of(m * 256 + (2 * s + parity) * 16, 16), 16)
                here = pl.ds(pl.multiple_of((m * HALF + s) * 16, 16), 16)
                old = alpha[at, :]
                moved = momentum_rate * mom[at, :] + (old + out[t : t + 16, :])
                stage1[here, :] = moved
                stage0[here, :] = old - step_rate * moved


def third_body(
    early_low, early_high, low, high, middle, coefs, alpha, mom, after, stage0, stage1, buf0, buf1, out,
):
    for row in range(SPAN):
        at = row * 16
        if STEPS <= row < STEPS + ROWS:
            buf0[at : at + 16, :] = middle[pl.ds(row - STEPS, 16, stride=ROWS), :]
        else:
            near, far, k = (early_low, low, row) if row < STEPS else (early_high, high, row - STEPS - ROWS)
            buf0[at : at + 4, :] = near[72 + k * 4 : 76 + k * 4, :]
            buf0[at + 4 : at + 16, :] = far[k * 12 : k * 12 + 12, :]

    def emit(row, value):
        out[pl.ds(row, 16, stride=ROWS), :] = value

    diffuse(lambda row: buf0[row * 16 : row * 16 + 16, :], 16, 16, coefs, (buf0, buf1), emit)
    update_alpha(lax.axis_index("mem") % 2, out, alpha, mom, stage0, stage1)


def static_last_body(low, high, grad, coefs, field, static_mom, after, new_static, new_static_mom, buf0, buf1, out):
    x, _, _ = place()
    load = halo_loader(low, high, lambda row: grad[pl.ds(x * 96 + row, VARS, stride=ROWS), :], VARS)
    for row in range(SPAN):
        buf0[row * 8 : row * 8 + VARS, :] = load(row)

    def emit(row, value):
        out[pl.ds(row, 8, stride=ROWS), :] = value

    diffuse(lambda row: buf0[row * 8 : row * 8 + 8, :], 8, 8, coefs, (buf0, buf1), emit)
    old = field[pl.ds(pl.multiple_of(x * 128, 128), 96), :]
    moved = momentum_rate * static_mom[...] + (old + out[0:96, :])
    new_static_mom[...] = moved
    new_static[...] = old - step_rate * moved


def fourth_body(
    low, high, middle, coefs, alpha, mom, done0, done1, done2, done3,
    new_alpha, new_mom, new_static, new_static_mom,
    buf0, buf1, out, stage0, stage1, sem,
):
    c = lax.axis_index("mem") % 2

    def leave(source, target, parity, k):
        return pltpu.make_async_copy(source.reshape(2, HALF, ROWS, LANES), target.at[:, :, parity], sem.at[k])

    copies = [
        leave(done0, new_alpha, c, 0),
        leave(done1, new_mom, c, 1),
        pltpu.make_async_copy(done2, new_static, sem.at[2]),
        pltpu.make_async_copy(done3, new_static_mom, sem.at[3]),
    ]
    for copy in copies:
        copy.start()

    def emit(row, value):
        out[pl.ds(row, 16, stride=ROWS), :] = value

    load = halo_loader(low, high, lambda row: middle[pl.ds(row, 16, stride=ROWS), :], 16)
    diffuse(load, 16, 16, coefs, (buf0, buf1), emit)
    update_alpha(1 - c, out, alpha, mom, stage0, stage1)
    last = [leave(stage0, new_alpha, 1 - c, 4), leave(stage1, new_mom, 1 - c, 5)]
    for copy in last:
        copy.start()
    for copy in copies + last:
        copy.wait()


def local(
    perturb,
    alpha,
    alpha_mom,
    static_ctl,
    static_mom,
    loc_coef,
    static_coef,
    obs_cell,
    obs_mask,
    obs_value,
    obs_weight,
):
    tiles = lax.axis_size("tile")
    up = [(i, (i + 1) % tiles) for i in range(tiles)]
    down = [(target, source) for source, target in up]
    members = lax.axis_size("mem")

    def swap(value, bits):
        return lax.ppermute(value, "mem", [(i, i ^ bits) for i in range(members)])

    def halo(forward, backward):
        return lax.ppermute(forward, "tile", up), lax.ppermute(backward, "tile", down)

    mom2 = alpha_mom.reshape(512, LANES)
    bufs16 = [f32(SPAN * 16, LANES), f32(SPAN * 16, LANES)]
    raw = f32(88, LANES)

    alpha2 = alpha.reshape(512, LANES)
    loc2 = loc_coef.reshape(32, LANES)
    quarter = shape(192, LANES)
    half = shape(256, LANES)
    a_f, a_b = call(
        pack_body,
        "pack",
        [HBM] * 2,
        [shape(216, LANES)] * 2,
        [f32(512, LANES), f32(32, LANES), pltpu.SemaphoreType.DMA((2,))],
        grant=GRANT,
    )(alpha2, loc2)
    a_low, a_high = halo(a_f, a_b)
    b_f, b_b, c_f, c_b, field, held = call(
        fetch_body,
        "fetch",
        [HBM] * 5,
        [quarter] * 4 + [half, quarter],
        [f32(512, LANES), pltpu.SemaphoreType.DMA((8,))],
        flops=BUSY,
        grant=GRANT2,
    )(
        alpha2,
        obs_value.reshape(VARS, 16, 8, LANES),
        obs_weight.reshape(VARS, 16, 8, LANES),
        static_ctl,
        static_coef.reshape(32, LANES),
    )
    b_low, b_high = halo(b_f, b_b)
    (sums,) = call(prepare_body, "prepare", [VM] * 3, [shape(384, LANES)], flops=BUSY)(
        obs_cell.reshape(8, LANES), obs_mask.reshape(8, LANES), held
    )

    part_a, loc_k = call(
        first_body,
        "first",
        [VM] * 6,
        [shape(HALF, VARS, ROWS, LANES), shape(200, LANES)],
        [raw] + bufs16 + [f32(256, LANES)],
        flops=BUSY,
    )(alpha2, a_low, a_high, loc2, perturb, sums)
    got = swap(part_a, 1)
    (second,) = call(second_body, "second", [VM] * 4, [half], bufs16, flops=BUSY)(alpha2, b_low, b_high, loc_k)
    o0, o1, o2, o3 = call(sum_body, "sum", [VM] * 3, [quarter] * 4)(second, perturb, got)
    r2, r1, r3 = swap(o2, 4), swap(o1, 2), swap(o3, 6)
    mine = o0 + r2 + r1 + r3
    other = swap(mine, 8)
    c_low, c_high = halo(*lax.optimization_barrier((c_f, c_b, o0))[:2])
    static, static_k = call(
        static_first_body,
        "static_first",
        [VM] * 3,
        [quarter, shape(200, LANES)],
        [raw] + bufs16 + [f32(256, LANES)],
        flops=BUSY,
    )(c_low, c_high, field)
    early = shape(120, LANES)
    grad, g_f, g_b, start = call(
        gradient_body, "gradient", [VM] * 5, [quarter, early, early, shape(64, LANES)]
    )(mine, other, static, sums, perturb)
    g2, g1, g3 = swap(grad, 4), swap(grad, 2), swap(grad, 6)
    g_low, g_high = halo(g_f, g_b)
    far = shape(144, LANES)
    (rest,) = call(join_body, "join", [VM] * 4, [shape(768, LANES)], flops=0)(g3, g1, g2, grad)
    rest = swap(rest, 1)
    p_f, p_b, p_m, g_low, g_high = call(
        project_own_body,
        "project_own",
        [VM] * 7,
        [far, far, half, early, early],
        flops=BUSY,
    )(g3, g1, g2, perturb, start, g_low, g_high)
    p_low, p_high = halo(p_f, p_b)
    q_f, q_b, q_m = call(project_other_body, "project_other", [VM] * 2, [quarter, quarter, half])(rest, perturb)
    q_low, q_high = halo(q_f, q_b)
    whole = shape(2, HALF, 2, ROWS, LANES)
    work = bufs16 + [f32(256, LANES)]
    static_ready = call(static_last_body, "static_last", [VM] * 7, [shape(96, LANES)] * 2, work, flops=BUSY)(
        g_low, g_high, grad, static_k, field, static_mom.reshape(96, LANES), q_m
    )
    ready = call(third_body, "third", [VM] * 9, [half, half], work, flops=BUSY)(
        g_low, g_high, p_low, p_high, p_m, loc_k, alpha2, mom2, q_m
    )
    new_alpha, new_alpha_mom, new_static, new_static_mom = call(
        fourth_body,
        "fourth",
        [VM] * 10,
        [whole, whole, shape(96, LANES), shape(96, LANES)],
        bufs16 + [f32(256, LANES)] * 3 + [pltpu.SemaphoreType.DMA((6,))],
        out_specs=[HBM] * 4,
    )(q_low, q_high, q_m, loc_k, alpha2, mom2, *ready, *static_ready)
    return (
        new_alpha.reshape(alpha.shape),
        new_alpha_mom.reshape(alpha.shape),
        new_static.reshape(static_mom.shape),
        new_static_mom.reshape(static_mom.shape),
    )


def solution(mesh):
    return jax.shard_map(
        local,
        mesh=mesh,
        in_specs=(
            P("mem", None, None, "tile", None),
            P("mem", None, "tile", None),
            P("mem", None, "tile", None),
            P(None, None, "tile", None),
            P(None, "mem", "tile", None),
            P(None, "tile", None),
            P(None, "tile", None),
            P("tile", None),
            P("tile", None),
            P(None, None, "tile", None),
            P(None, None, "tile", None),
        ),
        out_specs=(
            P("mem", None, "tile", None),
            P("mem", None, "tile", None),
            P(None, "mem", "tile", None),
            P(None, "mem", "tile", None),
        ),
        check_vma=False,
    )
```

```python
import functools

import jax
import jax.numpy as jnp
from jax import lax
from jax.experimental import pallas as pl
from jax.experimental.pallas import tpu as pltpu
from jax.sharding import PartitionSpec as P

STEPS = 12
ROWS = 16
LANES = 128
SPAN = ROWS + 2 * STEPS
VARS = 6
HALF = 8

momentum_rate = 0.9
step_rate = 0.5

GRANT = 54.6
GRANT2 = 53.2
BUSY = 5000000000

VM = pl.BlockSpec(memory_space=pltpu.VMEM)
ANY = pl.BlockSpec(memory_space=pl.ANY)
HBM = pl.BlockSpec(memory_space=pltpu.HBM)


def shape(*dims):
    return jax.ShapeDtypeStruct(dims, jnp.float32)


def call(body, name, ins, outs, scratch=(), flops=1000000, out_specs=None, grant=32):
    return pl.pallas_call(
        body,
        name=name,
        in_specs=list(ins),
        out_specs=out_specs or [VM] * len(outs),
        out_shape=list(outs),
        scratch_shapes=list(scratch),
        compiler_params=pltpu.CompilerParams(vmem_limit_bytes=int(grant * 1024 * 1024)),
        cost_estimate=pl.CostEstimate(flops=flops, bytes_accessed=1000000, transcendentals=0),
    )


def f32(*dims):
    return pltpu.VMEM(dims, jnp.float32)


def place():
    mem = lax.axis_index("mem")
    return mem // 8, (mem // 2) % 4, mem % 2


def pack_rows(load, width, forward, backward, base=0):
    for row in range(ROWS):
        value = load(row)
        if row >= ROWS - STEPS:
            at = base + (row - (ROWS - STEPS)) * width
            forward[at : at + width, :] = value
        if row < STEPS:
            at = base + row * width
            backward[at : at + width, :] = value


def build_coefs(low_x, mid_x, high_x, low_y, mid_y, high_y, raw, coefs):
    raw[0:8, :] = jnp.zeros((8, LANES), jnp.float32)
    raw[8:20, :] = low_x
    raw[20:36, :] = mid_x
    raw[36:48, :] = high_x
    raw[48:60, :] = low_y
    raw[60:76, :] = mid_y
    raw[76:88, :] = high_y
    extent = ROWS * lax.axis_size("tile")
    first = lax.axis_index("tile") * ROWS - STEPS
    at = first + lax.broadcasted_iota(jnp.int32, (SPAN, LANES), 0)
    lane = lax.broadcasted_iota(jnp.int32, (SPAN, LANES), 1)
    valid = (at >= 0) & (at < extent)
    below = jnp.where(valid, raw[8:48, :], 0.0)
    raw[8:48, :] = below
    above = jnp.where(valid, raw[7:47, :], 0.0)
    right = jnp.where(valid, raw[48:88, :], 0.0)
    left = jnp.where(lane > 0, pltpu.roll(right, 1, 1), 0.0)
    centre = 1.0 - below - above - right - left
    coefs[0:40, :] = jnp.where(valid, centre, 0.0)
    coefs[40:80, :] = jnp.where(at + 1 < extent, below, 0.0)
    coefs[80:120, :] = above
    coefs[120:160, :] = jnp.where(lane < LANES - 1, right, 0.0)
    coefs[160:200, :] = left


def diffuse(load, width, pitch, coefs, bufs, emit):
    for turn in range(STEPS):
        source = bufs[turn % 2]
        target = bufs[(turn + 1) % 2]
        if turn == 0:
            take = load
        else:
            take = lambda row: source[row * pitch : row * pitch + width, :]
        before = take(turn)
        here = take(turn + 1)
        for row in range(turn + 1, SPAN - 1 - turn):
            after = take(row + 1)
            new = coefs[row : row + 1, :] * here
            new = new + coefs[40 + row : 41 + row, :] * after
            new = new + coefs[80 + row : 81 + row, :] * before
            new = new + coefs[120 + row : 121 + row, :] * pltpu.roll(here, LANES - 1, 1)
            new = new + coefs[160 + row : 161 + row, :] * pltpu.roll(here, 1, 1)
            if turn == STEPS - 1:
                emit(row - STEPS, new)
            else:
                target[row * pitch : row * pitch + width, :] = new
            before = here
            here = after


def alpha_row(alpha, parity, row):
    parts = [alpha[pl.ds(m * 256 + parity * ROWS + row, HALF, stride=2 * ROWS), :] for m in range(2)]
    return jnp.concatenate(parts, axis=0)


def pack_body(alpha_in, loc_in, a_f, a_b, alpha, loc, sem):
    own = lax.axis_index("mem") % 2
    copies = [
        pltpu.make_async_copy(alpha_in, alpha, sem.at[0]),
        pltpu.make_async_copy(loc_in, loc, sem.at[1]),
    ]
    for copy in copies:
        copy.start()
    for copy in copies:
        copy.wait()
    pack_rows(lambda row: alpha_row(alpha, 1 - own, row), 16, a_f, a_b)
    for k in range(2):
        a_f[192 + k * 12 : 204 + k * 12, :] = loc[k * 16 + 4 : k * 16 + 16, :]
        a_b[192 + k * 12 : 204 + k * 12, :] = loc[k * 16 : k * 16 + 12, :]


def halo_loader(low, high, middle, width, base=0):
    def load(row):
        if row < STEPS:
            at = base + row * width
            return low[at : at + width, :]
        if row < STEPS + ROWS:
            return middle(row - STEPS)
        at = base + (row - STEPS - ROWS) * width
        return high[at : at + width, :]

    return load


def first_body(alpha, low, high, loc, perturb, ready, sums, coefs, raw, buf0, buf1, local):
    parity = 1 - lax.axis_index("mem") % 2
    build_coefs(
        low[192:204, :], loc[0:16, :], high[192:204, :],
        low[204:216, :], loc[16:32, :], high[204:216, :], raw, coefs,
    )

    def emit(row, value):
        local[pl.ds(row, 16, stride=ROWS), :] = value

    load = halo_loader(low, high, lambda row: alpha_row(alpha, parity, row), 16)
    diffuse(load, 16, 16, coefs, (buf0, buf1), emit)
    for s in range(HALF):
        level = 2 * s + parity
        for v in range(VARS):
            total = local[s * 16 : s * 16 + 16, :] * perturb[0, v, level].astype(jnp.float32)
            total = total + local[128 + s * 16 : 144 + s * 16, :] * perturb[1, v, level].astype(jnp.float32)
            sums[s, v] = total


def static_first_body(low, high, field, out, coefs, raw, buf0, buf1, result):
    build_coefs(
        low[pl.ds(6, 12, stride=16), :], field[96:112, :], high[pl.ds(6, 12, stride=16), :],
        low[pl.ds(7, 12, stride=16), :], field[112:128, :], high[pl.ds(7, 12, stride=16), :], raw, coefs,
    )

    def emit(row, value):
        result[pl.ds(row, 16, stride=ROWS), :] = value

    load = halo_loader(low, high, lambda row: field[pl.ds(row, 16, stride=ROWS), :], 16)
    diffuse(load, 16, 16, coefs, (buf0, buf1), emit)
    for j in range(2):
        out[j * 96 : j * 96 + 96, :] = result[j * 128 : j * 128 + 96, :]


def second_body(alpha, low, high, coefs, out, buf0, buf1):
    def emit(row, value):
        out[pl.ds(row, 16, stride=ROWS), :] = value

    parity = lax.axis_index("mem") % 2
    load = halo_loader(low, high, lambda row: alpha_row(alpha, parity, row), 16)
    diffuse(load, 16, 16, coefs, (buf0, buf1), emit)


def sum_body(local, perturb, received, o0, o1, o2, o3):
    _, y, parity = place()
    for k, out in enumerate((o0, o1, o2, o3)):
        for j in range(2):
            s = (y ^ k) + 4 * j
            level = 2 * s + parity
            first = local[pl.ds(pl.multiple_of(s * 16, 16), 16), :]
            other = local[pl.ds(pl.multiple_of(128 + s * 16, 16), 16), :]
            for v in range(VARS):
                total = first * perturb[0, v, level].astype(jnp.float32)
                total = total + other * perturb[1, v, level].astype(jnp.float32)
                total = total + received[s, v]
                out[j * 96 + v * 16 : j * 96 + v * 16 + 16, :] = total


def fetch_body(
    alpha_in, value, weight, static_ctl, static_coef, b_f, b_b, c_f, c_b, field, held, alpha, sem,
):
    _, y, c = place()
    first = pltpu.make_async_copy(alpha_in, alpha, sem.at[0])
    first.start()
    copies = [
        pltpu.make_async_copy(static_coef, field.at[96:128], sem.at[1]),
    ]
    for j in range(2):
        level = 2 * y + c + 8 * j
        for k, source in enumerate((weight, value)):
            spot = held.reshape(2, 2, VARS, 8, LANES).at[k, j]
            copies.append(pltpu.make_async_copy(source.at[:, level], spot, sem.at[2 + 3 * j + k]))
        spot = field.reshape(16, ROWS, LANES).at[8 * j : 8 * j + VARS]
        copies.append(pltpu.make_async_copy(static_ctl.at[:, level], spot, sem.at[4 + 3 * j]))
    for copy in copies:
        copy.start()
    field[224:256, :] = jnp.zeros((32, LANES), jnp.float32)
    first.wait()
    pack_rows(lambda row: alpha_row(alpha, c, row), 16, b_f, b_b)
    for copy in copies:
        copy.wait()
    pack_rows(lambda row: field[pl.ds(row, 16, stride=ROWS), :], 16, c_f, c_b)


def prepare_body(cell, mask, held, sums):
    pieces = []
    for a in range(8):
        part = held[pl.ds(a, 24, stride=8), :]
        scaled = part[0:12, :] * mask[a : a + 1, :].astype(jnp.float32)
        pieces.append(jnp.concatenate([scaled, scaled * part[12:24, :]], axis=0))
    both = jnp.concatenate(pieces, axis=1)
    top = both.astype(jnp.bfloat16)
    rest = both - top.astype(jnp.float32)
    mid = rest.astype(jnp.bfloat16)
    low = (rest - mid.astype(jnp.float32)).astype(jnp.bfloat16)
    stacked = jnp.concatenate([top, mid, low], axis=0)
    cells = jnp.concatenate([cell[a : a + 1, :] for a in range(8)], axis=1)
    for block in range(8):
        ids = block * 256 + lax.broadcasted_iota(jnp.int32, (256, 1024), 0)
        hit = jnp.where(ids == cells, 1.0, 0.0).astype(jnp.bfloat16)
        got = lax.dot_general(stacked, hit, (((1,), (1,)), ((), ())), preferred_element_type=jnp.float32)
        total = got[0:24, :] + got[24:48, :] + got[48:72, :]
        for r in range(2):
            sums[pl.ds(block * 2 + r, 24, stride=ROWS), :] = total[:, r * LANES : (r + 1) * LANES]


def project(g, k, parity, perturb, middle):
    _, y, _ = place()
    for j in range(2):
        level = 2 * ((y ^ k) + 4 * j) + parity
        fields = [g[j * 96 + v * 16 : j * 96 + v * 16 + 16, :] for v in range(VARS)]
        for m in range(2):
            total = perturb[m, 0, level].astype(jnp.float32) * fields[0]
            for v in range(1, VARS):
                total = total + perturb[m, v, level].astype(jnp.float32) * fields[v]
            at = (k * 4 + m * 2 + j) * 16
            middle[at : at + 16, :] = total


def gradient_body(mine, other, static, sums, perturb, grad, forward, backward, middle):
    x, _, c = place()
    total = mine[...] + other[...] + static[...]
    grad[...] = sums[0:192, :] * total - sums[192:384, :]
    project(grad, 0, c, perturb, middle)
    pack_rows(lambda row: grad[pl.ds(x * 96 + row, VARS, stride=ROWS), :], VARS, forward, backward)
    pack_rows(lambda row: middle[pl.ds(row, 4, stride=ROWS), :], 4, forward, backward, 72)


def join_body(g3, g1, g2, g0, out):
    for k, g in enumerate((g0, g1, g2, g3)):
        out[k * 192 : k * 192 + 192, :] = g[...]


def project_own_body(g3, g1, g2, perturb, start, low, high, forward, backward, middle, low_out, high_out):
    c = lax.axis_index("mem") % 2
    low_out[...] = low[...]
    high_out[...] = high[...]
    middle[0:64, :] = start[...]
    for k, g in ((1, g1), (2, g2), (3, g3)):
        project(g, k, c, perturb, middle)
    pack_rows(lambda row: middle[pl.ds(64 + row, 12, stride=ROWS), :], 12, forward, backward)


def project_other_body(rest, perturb, forward, backward, middle):
    c = lax.axis_index("mem") % 2
    for k in range(4):
        project(rest.at[k * 192 : k * 192 + 192], k, 1 - c, perturb, middle)
    pack_rows(lambda row: middle[pl.ds(row, 16, stride=ROWS), :], 16, forward, backward)


def update_alpha(parity, out, alpha, mom, stage0, stage1, finish=None):
    _, y, _ = place()
    for m in range(2):
        for k in range(4):
            for j in range(2):
                t = (k * 4 + m * 2 + j) * 16
                s = (y ^ k) + 4 * j
                at = pl.ds(pl.multiple_of(m * 256 + (2 * s + parity) * 16, 16), 16)
                here = pl.ds(pl.multiple_of((m * HALF + s) * 16, 16), 16)
                old = alpha[at, :]
                moved = momentum_rate * mom[at, :] + (old + out[t : t + 16, :])
                stage1[here, :] = moved
                stage0[here, :] = old - step_rate * moved
        if finish is not None:
            finish(m)


def third_body(
    early_low, early_high, low, high, middle, coefs, alpha, mom, after, stage0, stage1, buf0, buf1, out,
):
    for row in range(SPAN):
        at = row * 16
        if STEPS <= row < STEPS + ROWS:
            buf0[at : at + 16, :] = middle[pl.ds(row - STEPS, 16, stride=ROWS), :]
        else:
            near, far, k = (early_low, low, row) if row < STEPS else (early_high, high, row - STEPS - ROWS)
            buf0[at : at + 4, :] = near[72 + k * 4 : 76 + k * 4, :]
            buf0[at + 4 : at + 16, :] = far[k * 12 : k * 12 + 12, :]

    def emit(row, value):
        out[pl.ds(row, 16, stride=ROWS), :] = value

    diffuse(lambda row: buf0[row * 16 : row * 16 + 16, :], 16, 16, coefs, (buf0, buf1), emit)
    update_alpha(lax.axis_index("mem") % 2, out, alpha, mom, stage0, stage1)


def static_last_body(low, high, grad, coefs, field, static_mom, after, new_static, new_static_mom, buf0, buf1, out):
    x, _, _ = place()
    load = halo_loader(low, high, lambda row: grad[pl.ds(x * 96 + row, VARS, stride=ROWS), :], VARS)
    for row in range(SPAN):
        buf0[row * 8 : row * 8 + VARS, :] = load(row)

    def emit(row, value):
        out[pl.ds(row, 8, stride=ROWS), :] = value

    diffuse(lambda row: buf0[row * 8 : row * 8 + 8, :], 8, 8, coefs, (buf0, buf1), emit)
    old = field[pl.ds(pl.multiple_of(x * 128, 128), 96), :]
    moved = momentum_rate * static_mom[...] + (old + out[0:96, :])
    new_static_mom[...] = moved
    new_static[...] = old - step_rate * moved


def fourth_body(
    low, high, middle, coefs, alpha, mom, done0, done1, done2, done3,
    new_alpha, new_mom, new_static, new_static_mom,
    buf0, buf1, out, stage0, stage1, sem,
):
    c = lax.axis_index("mem") % 2

    def leave(source, target, parity, k):
        return pltpu.make_async_copy(source.reshape(2, HALF, ROWS, LANES), target.at[:, :, parity], sem.at[k])

    copies = [
        leave(done0, new_alpha, c, 0),
        leave(done1, new_mom, c, 1),
        pltpu.make_async_copy(done2, new_static, sem.at[2]),
        pltpu.make_async_copy(done3, new_static_mom, sem.at[3]),
    ]
    for copy in copies:
        copy.start()

    def emit(row, value):
        out[pl.ds(row, 16, stride=ROWS), :] = value

    load = halo_loader(low, high, lambda row: middle[pl.ds(row, 16, stride=ROWS), :], 16)
    diffuse(load, 16, 16, coefs, (buf0, buf1), emit)
    def finish(m):
        for k, (stage, target) in enumerate(((stage0, new_alpha), (stage1, new_mom))):
            part = stage.at[m * 128 : m * 128 + 128].reshape(HALF, ROWS, LANES)
            copy = pltpu.make_async_copy(part, target.at[m, :, 1 - c], sem.at[4 + 2 * m + k])
            copy.start()
            copies.append(copy)

    update_alpha(1 - c, out, alpha, mom, stage0, stage1, finish)
    for copy in copies:
        copy.wait()


def local(
    perturb,
    alpha,
    alpha_mom,
    static_ctl,
    static_mom,
    loc_coef,
    static_coef,
    obs_cell,
    obs_mask,
    obs_value,
    obs_weight,
):
    tiles = lax.axis_size("tile")
    up = [(i, (i + 1) % tiles) for i in range(tiles)]
    down = [(target, source) for source, target in up]
    members = lax.axis_size("mem")

    def swap(value, bits):
        return lax.ppermute(value, "mem", [(i, i ^ bits) for i in range(members)])

    def halo(forward, backward):
        return lax.ppermute(forward, "tile", up), lax.ppermute(backward, "tile", down)

    mom2 = alpha_mom.reshape(512, LANES)
    bufs16 = [f32(SPAN * 16, LANES), f32(SPAN * 16, LANES)]
    raw = f32(88, LANES)

    alpha2 = alpha.reshape(512, LANES)
    loc2 = loc_coef.reshape(32, LANES)
    quarter = shape(192, LANES)
    half = shape(256, LANES)
    a_f, a_b = call(
        pack_body,
        "pack",
        [HBM] * 2,
        [shape(216, LANES)] * 2,
        [f32(512, LANES), f32(32, LANES), pltpu.SemaphoreType.DMA((2,))],
        grant=GRANT,
    )(alpha2, loc2)
    a_low, a_high = halo(a_f, a_b)
    b_f, b_b, c_f, c_b, field, held = call(
        fetch_body,
        "fetch",
        [HBM] * 5,
        [quarter] * 4 + [half, quarter],
        [f32(512, LANES), pltpu.SemaphoreType.DMA((8,))],
        flops=BUSY,
        grant=GRANT2,
    )(
        alpha2,
        obs_value.reshape(VARS, 16, 8, LANES),
        obs_weight.reshape(VARS, 16, 8, LANES),
        static_ctl,
        static_coef.reshape(32, LANES),
    )
    b_low, b_high = halo(b_f, b_b)
    (sums,) = call(prepare_body, "prepare", [VM] * 3, [shape(384, LANES)], flops=BUSY)(
        obs_cell.reshape(8, LANES), obs_mask.reshape(8, LANES), held
    )

    part_a, loc_k = call(
        first_body,
        "first",
        [VM] * 6,
        [shape(HALF, VARS, ROWS, LANES), shape(200, LANES)],
        [raw] + bufs16 + [f32(256, LANES)],
        flops=BUSY,
    )(alpha2, a_low, a_high, loc2, perturb, sums)
    got = swap(part_a, 1)
    (second,) = call(second_body, "second", [VM] * 4, [half], bufs16, flops=BUSY)(alpha2, b_low, b_high, loc_k)
    o0, o1, o2, o3 = call(sum_body, "sum", [VM] * 3, [quarter] * 4)(second, perturb, got)
    r2, r1, r3 = swap(o2, 4), swap(o1, 2), swap(o3, 6)
    mine = o0 + r2 + r1 + r3
    other = swap(mine, 8)
    c_low, c_high = halo(*lax.optimization_barrier((c_f, c_b, o0))[:2])
    static, static_k = call(
        static_first_body,
        "static_first",
        [VM] * 3,
        [quarter, shape(200, LANES)],
        [raw] + bufs16 + [f32(256, LANES)],
        flops=BUSY,
    )(c_low, c_high, field)
    early = shape(120, LANES)
    grad, g_f, g_b, start = call(
        gradient_body, "gradient", [VM] * 5, [quarter, early, early, shape(64, LANES)]
    )(mine, other, static, sums, perturb)
    g2, g1, g3 = swap(grad, 4), swap(grad, 2), swap(grad, 6)
    g_low, g_high = halo(g_f, g_b)
    far = shape(144, LANES)
    (rest,) = call(join_body, "join", [VM] * 4, [shape(768, LANES)], flops=0)(g3, g1, g2, grad)
    rest = swap(rest, 1)
    p_f, p_b, p_m, g_low, g_high = call(
        project_own_body,
        "project_own",
        [VM] * 7,
        [far, far, half, early, early],
        flops=BUSY,
    )(g3, g1, g2, perturb, start, g_low, g_high)
    p_low, p_high = halo(p_f, p_b)
    q_f, q_b, q_m = call(project_other_body, "project_other", [VM] * 2, [quarter, quarter, half])(rest, perturb)
    q_low, q_high = halo(q_f, q_b)
    whole = shape(2, HALF, 2, ROWS, LANES)
    work = bufs16 + [f32(256, LANES)]
    static_ready = call(static_last_body, "static_last", [VM] * 7, [shape(96, LANES)] * 2, work, flops=BUSY)(
        g_low, g_high, grad, static_k, field, static_mom.reshape(96, LANES), q_m
    )
    ready = call(third_body, "third", [VM] * 9, [half, half], work, flops=BUSY)(
        g_low, g_high, p_low, p_high, p_m, loc_k, alpha2, mom2, q_m
    )
    new_alpha, new_alpha_mom, new_static, new_static_mom = call(
        fourth_body,
        "fourth",
        [VM] * 10,
        [whole, whole, shape(96, LANES), shape(96, LANES)],
        bufs16 + [f32(256, LANES)] * 3 + [pltpu.SemaphoreType.DMA((8,))],
        out_specs=[HBM] * 4,
    )(q_low, q_high, q_m, loc_k, alpha2, mom2, *ready, *static_ready)
    return (
        new_alpha.reshape(alpha.shape),
        new_alpha_mom.reshape(alpha.shape),
        new_static.reshape(static_mom.shape),
        new_static_mom.reshape(static_mom.shape),
    )


def solution(mesh):
    return jax.shard_map(
        local,
        mesh=mesh,
        in_specs=(
            P("mem", None, None, "tile", None),
            P("mem", None, "tile", None),
            P("mem", None, "tile", None),
            P(None, None, "tile", None),
            P(None, "mem", "tile", None),
            P(None, "tile", None),
            P(None, "tile", None),
            P("tile", None),
            P("tile", None),
            P(None, None, "tile", None),
            P(None, None, "tile", None),
        ),
        out_specs=(
            P("mem", None, "tile", None),
            P("mem", None, "tile", None),
            P(None, "mem", "tile", None),
            P(None, "mem", "tile", None),
        ),
        check_vma=False,
    )
```

```python
import functools

import jax
import jax.numpy as jnp
from jax import lax
from jax.experimental import pallas as pl
from jax.experimental.pallas import tpu as pltpu
from jax.sharding import PartitionSpec as P

STEPS = 12
ROWS = 16
LANES = 128
SPAN = ROWS + 2 * STEPS
VARS = 6
HALF = 8

momentum_rate = 0.9
step_rate = 0.5

GRANT = 54.6
GRANT2 = 53.2
BUSY = 5000000000

VM = pl.BlockSpec(memory_space=pltpu.VMEM)
ANY = pl.BlockSpec(memory_space=pl.ANY)
HBM = pl.BlockSpec(memory_space=pltpu.HBM)


def shape(*dims):
    return jax.ShapeDtypeStruct(dims, jnp.float32)


def call(body, name, ins, outs, scratch=(), flops=1000000, out_specs=None, grant=32):
    return pl.pallas_call(
        body,
        name=name,
        in_specs=list(ins),
        out_specs=out_specs or [VM] * len(outs),
        out_shape=list(outs),
        scratch_shapes=list(scratch),
        compiler_params=pltpu.CompilerParams(vmem_limit_bytes=int(grant * 1024 * 1024)),
        cost_estimate=pl.CostEstimate(flops=flops, bytes_accessed=1000000, transcendentals=0),
    )


def f32(*dims):
    return pltpu.VMEM(dims, jnp.float32)


def place():
    mem = lax.axis_index("mem")
    return mem // 8, (mem // 2) % 4, mem % 2


def pack_rows(load, width, forward, backward, base=0):
    for row in range(ROWS):
        value = load(row)
        if row >= ROWS - STEPS:
            at = base + (row - (ROWS - STEPS)) * width
            forward[at : at + width, :] = value
        if row < STEPS:
            at = base + row * width
            backward[at : at + width, :] = value


def build_coefs(low_x, mid_x, high_x, low_y, mid_y, high_y, raw, coefs):
    raw[0:8, :] = jnp.zeros((8, LANES), jnp.float32)
    raw[8:20, :] = low_x
    raw[20:36, :] = mid_x
    raw[36:48, :] = high_x
    raw[48:60, :] = low_y
    raw[60:76, :] = mid_y
    raw[76:88, :] = high_y
    extent = ROWS * lax.axis_size("tile")
    first = lax.axis_index("tile") * ROWS - STEPS
    at = first + lax.broadcasted_iota(jnp.int32, (SPAN, LANES), 0)
    lane = lax.broadcasted_iota(jnp.int32, (SPAN, LANES), 1)
    valid = (at >= 0) & (at < extent)
    below = jnp.where(valid, raw[8:48, :], 0.0)
    raw[8:48, :] = below
    above = jnp.where(valid, raw[7:47, :], 0.0)
    right = jnp.where(valid, raw[48:88, :], 0.0)
    left = jnp.where(lane > 0, pltpu.roll(right, 1, 1), 0.0)
    centre = 1.0 - below - above - right - left
    coefs[0:40, :] = jnp.where(valid, centre, 0.0)
    coefs[40:80, :] = jnp.where(at + 1 < extent, below, 0.0)
    coefs[80:120, :] = above
    coefs[120:160, :] = jnp.where(lane < LANES - 1, right, 0.0)
    coefs[160:200, :] = left


def diffuse(load, width, pitch, coefs, bufs, emit):
    for turn in range(STEPS):
        source = bufs[turn % 2]
        target = bufs[(turn + 1) % 2]
        if turn == 0:
            take = load
        else:
            take = lambda row: source[row * pitch : row * pitch + width, :]
        before = take(turn)
        here = take(turn + 1)
        for row in range(turn + 1, SPAN - 1 - turn):
            after = take(row + 1)
            new = coefs[row : row + 1, :] * here
            new = new + coefs[40 + row : 41 + row, :] * after
            new = new + coefs[80 + row : 81 + row, :] * before
            new = new + coefs[120 + row : 121 + row, :] * pltpu.roll(here, LANES - 1, 1)
            new = new + coefs[160 + row : 161 + row, :] * pltpu.roll(here, 1, 1)
            if turn == STEPS - 1:
                emit(row - STEPS, new)
            else:
                target[row * pitch : row * pitch + width, :] = new
            before = here
            here = after


def alpha_row(alpha, parity, row):
    parts = [alpha[pl.ds(m * 256 + parity * ROWS + row, HALF, stride=2 * ROWS), :] for m in range(2)]
    return jnp.concatenate(parts, axis=0)


def pack_body(alpha_in, loc_in, a_f, a_b, alpha, loc, sem):
    own = lax.axis_index("mem") % 2
    copies = [
        pltpu.make_async_copy(alpha_in, alpha, sem.at[0]),
        pltpu.make_async_copy(loc_in, loc, sem.at[1]),
    ]
    for copy in copies:
        copy.start()
    for copy in copies:
        copy.wait()
    pack_rows(lambda row: alpha_row(alpha, 1 - own, row), 16, a_f, a_b)
    for k in range(2):
        a_f[192 + k * 12 : 204 + k * 12, :] = loc[k * 16 + 4 : k * 16 + 16, :]
        a_b[192 + k * 12 : 204 + k * 12, :] = loc[k * 16 : k * 16 + 12, :]


def halo_loader(low, high, middle, width, base=0):
    def load(row):
        if row < STEPS:
            at = base + row * width
            return low[at : at + width, :]
        if row < STEPS + ROWS:
            return middle(row - STEPS)
        at = base + (row - STEPS - ROWS) * width
        return high[at : at + width, :]

    return load


def first_body(alpha, low, high, loc, perturb, ready, sums, coefs, raw, buf0, buf1, local):
    parity = 1 - lax.axis_index("mem") % 2
    build_coefs(
        low[192:204, :], loc[0:16, :], high[192:204, :],
        low[204:216, :], loc[16:32, :], high[204:216, :], raw, coefs,
    )

    def emit(row, value):
        local[pl.ds(row, 16, stride=ROWS), :] = value

    load = halo_loader(low, high, lambda row: alpha_row(alpha, parity, row), 16)
    diffuse(load, 16, 16, coefs, (buf0, buf1), emit)
    for s in range(HALF):
        level = 2 * s + parity
        for v in range(VARS):
            total = local[s * 16 : s * 16 + 16, :] * perturb[0, v, level].astype(jnp.float32)
            total = total + local[128 + s * 16 : 144 + s * 16, :] * perturb[1, v, level].astype(jnp.float32)
            sums[s, v] = total


def static_first_body(low, high, field, out, coefs, raw, buf0, buf1, result):
    build_coefs(
        low[pl.ds(6, 12, stride=16), :], field[96:112, :], high[pl.ds(6, 12, stride=16), :],
        low[pl.ds(7, 12, stride=16), :], field[112:128, :], high[pl.ds(7, 12, stride=16), :], raw, coefs,
    )

    def emit(row, value):
        result[pl.ds(row, 16, stride=ROWS), :] = value

    load = halo_loader(low, high, lambda row: field[pl.ds(row, 16, stride=ROWS), :], 16)
    diffuse(load, 16, 16, coefs, (buf0, buf1), emit)
    for j in range(2):
        out[j * 96 : j * 96 + 96, :] = result[j * 128 : j * 128 + 96, :]


def second_body(alpha, low, high, coefs, out, buf0, buf1):
    def emit(row, value):
        out[pl.ds(row, 16, stride=ROWS), :] = value

    parity = lax.axis_index("mem") % 2
    load = halo_loader(low, high, lambda row: alpha_row(alpha, parity, row), 16)
    diffuse(load, 16, 16, coefs, (buf0, buf1), emit)


def sum_body(local, perturb, received, o0, o1, o2, o3):
    _, y, parity = place()
    for k, out in enumerate((o0, o1, o2, o3)):
        for j in range(2):
            s = (y ^ k) + 4 * j
            level = 2 * s + parity
            first = local[pl.ds(pl.multiple_of(s * 16, 16), 16), :]
            other = local[pl.ds(pl.multiple_of(128 + s * 16, 16), 16), :]
            for v in range(VARS):
                total = first * perturb[0, v, level].astype(jnp.float32)
                total = total + other * perturb[1, v, level].astype(jnp.float32)
                total = total + received[s, v]
                out[j * 96 + v * 16 : j * 96 + v * 16 + 16, :] = total


def fetch_body(
    alpha_in, value, weight, static_ctl, static_coef, b_f, b_b, c_f, c_b, field, held, alpha, sem,
):
    _, y, c = place()
    first = pltpu.make_async_copy(alpha_in, alpha, sem.at[0])
    first.start()
    copies = [
        pltpu.make_async_copy(static_coef, field.at[96:128], sem.at[1]),
    ]
    for j in range(2):
        level = 2 * y + c + 8 * j
        for k, source in enumerate((weight, value)):
            spot = held.reshape(2, 2, VARS, 8, LANES).at[k, j]
            copies.append(pltpu.make_async_copy(source.at[:, level], spot, sem.at[2 + 3 * j + k]))
        spot = field.reshape(16, ROWS, LANES).at[8 * j : 8 * j + VARS]
        copies.append(pltpu.make_async_copy(static_ctl.at[:, level], spot, sem.at[4 + 3 * j]))
    for copy in copies:
        copy.start()
    field[224:256, :] = jnp.zeros((32, LANES), jnp.float32)
    first.wait()
    pack_rows(lambda row: alpha_row(alpha, c, row), 16, b_f, b_b)
    for copy in copies:
        copy.wait()
    pack_rows(lambda row: field[pl.ds(row, 16, stride=ROWS), :], 16, c_f, c_b)


def prepare_body(cell, mask, held, sums):
    pieces = []
    for a in range(8):
        part = held[pl.ds(a, 24, stride=8), :]
        scaled = part[0:12, :] * mask[a : a + 1, :].astype(jnp.float32)
        pieces.append(jnp.concatenate([scaled, scaled * part[12:24, :]], axis=0))
    both = jnp.concatenate(pieces, axis=1)
    top = both.astype(jnp.bfloat16)
    rest = both - top.astype(jnp.float32)
    mid = rest.astype(jnp.bfloat16)
    low = (rest - mid.astype(jnp.float32)).astype(jnp.bfloat16)
    stacked = jnp.concatenate([top, mid, low], axis=0)
    cells = jnp.concatenate([cell[a : a + 1, :] for a in range(8)], axis=1)
    for block in range(8):
        ids = block * 256 + lax.broadcasted_iota(jnp.int32, (256, 1024), 0)
        hit = jnp.where(ids == cells, 1.0, 0.0).astype(jnp.bfloat16)
        got = lax.dot_general(stacked, hit, (((1,), (1,)), ((), ())), preferred_element_type=jnp.float32)
        total = got[0:24, :] + got[24:48, :] + got[48:72, :]
        for r in range(2):
            sums[pl.ds(block * 2 + r, 24, stride=ROWS), :] = total[:, r * LANES : (r + 1) * LANES]


def project(g, k, parity, perturb, middle):
    _, y, _ = place()
    for j in range(2):
        level = 2 * ((y ^ k) + 4 * j) + parity
        fields = [g[j * 96 + v * 16 : j * 96 + v * 16 + 16, :] for v in range(VARS)]
        for m in range(2):
            total = perturb[m, 0, level].astype(jnp.float32) * fields[0]
            for v in range(1, VARS):
                total = total + perturb[m, v, level].astype(jnp.float32) * fields[v]
            at = (k * 4 + m * 2 + j) * 16
            middle[at : at + 16, :] = total


def gradient_body(mine, other, static, sums, perturb, grad, forward, backward, middle):
    c = lax.axis_index("mem") % 2
    total = mine[...] + other[...] + static[...]
    grad[...] = sums[0:192, :] * total - sums[192:384, :]
    project(grad, 0, c, perturb, middle)
    pack_rows(lambda row: middle[pl.ds(row, 4, stride=ROWS), :], 4, forward, backward)


def join_body(g2, g1, g3, g0, out):
    for k, g in enumerate((g0, g1, g2, g3)):
        out[k * 192 : k * 192 + 192, :] = g[...]


def project_own_body(g2, g1, g3, g0, perturb, start, low, high, forward, backward, middle, low_out, high_out):
    x, _, c = place()
    low_out[...] = low[...]
    high_out[...] = high[...]
    middle[0:64, :] = start[...]
    for k, g in ((1, g1), (2, g2), (3, g3)):
        project(g, k, c, perturb, middle)
    pack_rows(lambda row: middle[pl.ds(64 + row, 12, stride=ROWS), :], 12, forward, backward)
    pack_rows(lambda row: g0[pl.ds(x * 96 + row, VARS, stride=ROWS), :], VARS, forward, backward, 144)


def project_other_body(rest, perturb, forward, backward, middle):
    c = lax.axis_index("mem") % 2
    for k in range(4):
        project(rest.at[k * 192 : k * 192 + 192], k, 1 - c, perturb, middle)
    pack_rows(lambda row: middle[pl.ds(row, 16, stride=ROWS), :], 16, forward, backward)


def update_alpha(parity, out, alpha, mom, stage0, stage1, finish=None):
    _, y, _ = place()
    for m in range(2):
        for k in range(4):
            for j in range(2):
                t = (k * 4 + m * 2 + j) * 16
                s = (y ^ k) + 4 * j
                at = pl.ds(pl.multiple_of(m * 256 + (2 * s + parity) * 16, 16), 16)
                here = pl.ds(pl.multiple_of((m * HALF + s) * 16, 16), 16)
                old = alpha[at, :]
                moved = momentum_rate * mom[at, :] + (old + out[t : t + 16, :])
                stage1[here, :] = moved
                stage0[here, :] = old - step_rate * moved
        if finish is not None:
            finish(m)


def third_body(
    early_low, early_high, low, high, middle, coefs, alpha, mom, after, stage0, stage1, buf0, buf1, out,
):
    for row in range(SPAN):
        at = row * 16
        if STEPS <= row < STEPS + ROWS:
            buf0[at : at + 16, :] = middle[pl.ds(row - STEPS, 16, stride=ROWS), :]
        else:
            near, far, k = (early_low, low, row) if row < STEPS else (early_high, high, row - STEPS - ROWS)
            buf0[at : at + 4, :] = near[k * 4 : k * 4 + 4, :]
            buf0[at + 4 : at + 16, :] = far[k * 12 : k * 12 + 12, :]

    def emit(row, value):
        out[pl.ds(row, 16, stride=ROWS), :] = value

    diffuse(lambda row: buf0[row * 16 : row * 16 + 16, :], 16, 16, coefs, (buf0, buf1), emit)
    update_alpha(lax.axis_index("mem") % 2, out, alpha, mom, stage0, stage1)


def static_last_body(low, high, grad, coefs, field, static_mom, after, new_static, new_static_mom, buf0, buf1, out):
    x, _, _ = place()
    load = halo_loader(low, high, lambda row: grad[pl.ds(x * 96 + row, VARS, stride=ROWS), :], VARS, 144)
    for row in range(SPAN):
        buf0[row * 8 : row * 8 + VARS, :] = load(row)

    def emit(row, value):
        out[pl.ds(row, 8, stride=ROWS), :] = value

    diffuse(lambda row: buf0[row * 8 : row * 8 + 8, :], 8, 8, coefs, (buf0, buf1), emit)
    old = field[pl.ds(pl.multiple_of(x * 128, 128), 96), :]
    moved = momentum_rate * static_mom[...] + (old + out[0:96, :])
    new_static_mom[...] = moved
    new_static[...] = old - step_rate * moved


def fourth_body(
    low, high, middle, coefs, alpha, mom, done0, done1, done2, done3,
    new_alpha, new_mom, new_static, new_static_mom,
    buf0, buf1, out, stage0, stage1, sem,
):
    c = lax.axis_index("mem") % 2

    def leave(source, target, parity, k):
        return pltpu.make_async_copy(source.reshape(2, HALF, ROWS, LANES), target.at[:, :, parity], sem.at[k])

    copies = [
        leave(done0, new_alpha, c, 0),
        leave(done1, new_mom, c, 1),
        pltpu.make_async_copy(done2, new_static, sem.at[2]),
        pltpu.make_async_copy(done3, new_static_mom, sem.at[3]),
    ]
    for copy in copies:
        copy.start()

    def emit(row, value):
        out[pl.ds(row, 16, stride=ROWS), :] = value

    load = halo_loader(low, high, lambda row: middle[pl.ds(row, 16, stride=ROWS), :], 16)
    diffuse(load, 16, 16, coefs, (buf0, buf1), emit)
    def finish(m):
        for k, (stage, target) in enumerate(((stage0, new_alpha), (stage1, new_mom))):
            part = stage.at[m * 128 : m * 128 + 128].reshape(HALF, ROWS, LANES)
            copy = pltpu.make_async_copy(part, target.at[m, :, 1 - c], sem.at[4 + 2 * m + k])
            copy.start()
            copies.append(copy)

    update_alpha(1 - c, out, alpha, mom, stage0, stage1, finish)
    for copy in copies:
        copy.wait()


def local(
    perturb,
    alpha,
    alpha_mom,
    static_ctl,
    static_mom,
    loc_coef,
    static_coef,
    obs_cell,
    obs_mask,
    obs_value,
    obs_weight,
):
    tiles = lax.axis_size("tile")
    up = [(i, (i + 1) % tiles) for i in range(tiles)]
    down = [(target, source) for source, target in up]
    members = lax.axis_size("mem")

    def swap(value, bits):
        return lax.ppermute(value, "mem", [(i, i ^ bits) for i in range(members)])

    def halo(forward, backward):
        return lax.ppermute(forward, "tile", up), lax.ppermute(backward, "tile", down)

    mom2 = alpha_mom.reshape(512, LANES)
    bufs16 = [f32(SPAN * 16, LANES), f32(SPAN * 16, LANES)]
    raw = f32(88, LANES)

    alpha2 = alpha.reshape(512, LANES)
    loc2 = loc_coef.reshape(32, LANES)
    quarter = shape(192, LANES)
    half = shape(256, LANES)
    a_f, a_b = call(
        pack_body,
        "pack",
        [HBM] * 2,
        [shape(216, LANES)] * 2,
        [f32(512, LANES), f32(32, LANES), pltpu.SemaphoreType.DMA((2,))],
        grant=GRANT,
    )(alpha2, loc2)
    a_low, a_high = halo(a_f, a_b)
    b_f, b_b, c_f, c_b, field, held = call(
        fetch_body,
        "fetch",
        [HBM] * 5,
        [quarter] * 4 + [half, quarter],
        [f32(512, LANES), pltpu.SemaphoreType.DMA((8,))],
        flops=BUSY,
        grant=GRANT2,
    )(
        alpha2,
        obs_value.reshape(VARS, 16, 8, LANES),
        obs_weight.reshape(VARS, 16, 8, LANES),
        static_ctl,
        static_coef.reshape(32, LANES),
    )
    b_low, b_high = halo(b_f, b_b)
    (sums,) = call(prepare_body, "prepare", [VM] * 3, [shape(384, LANES)], flops=BUSY)(
        obs_cell.reshape(8, LANES), obs_mask.reshape(8, LANES), held
    )

    part_a, loc_k = call(
        first_body,
        "first",
        [VM] * 6,
        [shape(HALF, VARS, ROWS, LANES), shape(200, LANES)],
        [raw] + bufs16 + [f32(256, LANES)],
        flops=BUSY,
    )(alpha2, a_low, a_high, loc2, perturb, sums)
    got = swap(part_a, 1)
    (second,) = call(second_body, "second", [VM] * 4, [half], bufs16, flops=BUSY)(alpha2, b_low, b_high, loc_k)
    o0, o1, o2, o3 = call(sum_body, "sum", [VM] * 3, [quarter] * 4)(second, perturb, got)
    r2, r1, r3 = swap(o2, 4), swap(o1, 2), swap(o3, 6)
    mine = o0 + r2 + r1 + r3
    other = swap(mine, 8)
    c_low, c_high = halo(*lax.optimization_barrier((c_f, c_b, o0))[:2])
    static, static_k = call(
        static_first_body,
        "static_first",
        [VM] * 3,
        [quarter, shape(200, LANES)],
        [raw] + bufs16 + [f32(256, LANES)],
        flops=BUSY,
    )(c_low, c_high, field)
    early = shape(48, LANES)
    grad, g_f, g_b, start = call(
        gradient_body, "gradient", [VM] * 5, [quarter, early, early, shape(64, LANES)]
    )(mine, other, static, sums, perturb)
    g2, g1, g3 = swap(grad, 4), swap(grad, 2), swap(grad, 6)
    g_low, g_high = halo(g_f, g_b)
    far = shape(216, LANES)
    (rest,) = call(join_body, "join", [VM] * 4, [shape(768, LANES)], flops=0)(g2, g1, g3, grad)
    rest = swap(rest, 1)
    p_f, p_b, p_m, g_low, g_high = call(
        project_own_body,
        "project_own",
        [VM] * 8,
        [far, far, half, early, early],
        flops=BUSY,
    )(g2, g1, g3, grad, perturb, start, g_low, g_high)
    p_low, p_high = halo(p_f, p_b)
    q_f, q_b, q_m = call(project_other_body, "project_other", [VM] * 2, [quarter, quarter, half])(rest, perturb)
    q_low, q_high = halo(q_f, q_b)
    whole = shape(2, HALF, 2, ROWS, LANES)
    work = bufs16 + [f32(256, LANES)]
    static_ready = call(static_last_body, "static_last", [VM] * 7, [shape(96, LANES)] * 2, work, flops=BUSY)(
        p_low, p_high, grad, static_k, field, static_mom.reshape(96, LANES), q_m
    )
    ready = call(third_body, "third", [VM] * 9, [half, half], work, flops=BUSY)(
        g_low, g_high, p_low, p_high, p_m, loc_k, alpha2, mom2, q_m
    )
    new_alpha, new_alpha_mom, new_static, new_static_mom = call(
        fourth_body,
        "fourth",
        [VM] * 10,
        [whole, whole, shape(96, LANES), shape(96, LANES)],
        bufs16 + [f32(256, LANES)] * 3 + [pltpu.SemaphoreType.DMA((8,))],
        out_specs=[HBM] * 4,
    )(q_low, q_high, q_m, loc_k, alpha2, mom2, *ready, *static_ready)
    return (
        new_alpha.reshape(alpha.shape),
        new_alpha_mom.reshape(alpha.shape),
        new_static.reshape(static_mom.shape),
        new_static_mom.reshape(static_mom.shape),
    )


def solution(mesh):
    return jax.shard_map(
        local,
        mesh=mesh,
        in_specs=(
            P("mem", None, None, "tile", None),
            P("mem", None, "tile", None),
            P("mem", None, "tile", None),
            P(None, None, "tile", None),
            P(None, "mem", "tile", None),
            P(None, "tile", None),
            P(None, "tile", None),
            P("tile", None),
            P("tile", None),
            P(None, None, "tile", None),
            P(None, None, "tile", None),
        ),
        out_specs=(
            P("mem", None, "tile", None),
            P("mem", None, "tile", None),
            P(None, "mem", "tile", None),
            P(None, "mem", "tile", None),
        ),
        check_vma=False,
    )
```
